32 devices in a mesh: seq: 4 (over y, x), dp: 8 (over z, core).
Axes of the slice: x: 2, y: 2, z: 4, core: 2. Of those that a mesh axis runs over, the one named last changes fastest.
Arguments:
- latents: bfloat16 [16, 2048, 64], P('dp', 'seq'), may hold values from -6 to 6
- noise_draw: bfloat16 [16, 2048, 64], P('dp', 'seq'), may hold values from -6 to 6
- audio_len: int32 [16], P('dp'), may hold values from 512 to 2048
- bucket: int32 [16], P('dp'), may hold values from 0 to 999
- timing: int32 [16, 2], P('dp'), may hold values from 0 to 63
- prompt: bfloat16 [16, 128, 768], P('dp'), may hold values from -6 to 6
- prompt_len: int32 [16], P('dp'), may hold values from 4 to 128, as said below
- step_count: int32 [1], replicated, may hold values from 2 to 20
- edge_weight: float32 [896, 1536], P(None, ('seq', 'dp'))
- edge_first: float32 [896, 1536], P(None, ('seq', 'dp')), may hold values from -4.7683716e-07 to 4.7683716e-07
- edge_second: float32 [896, 1536], P(None, ('seq', 'dp')), may hold values from 4.1179106e-17 to 6.588657e-16
- attend_weight: float32 [1536, 4608], P(('seq', 'dp')), may hold values from -0.15625 to 0.15625
- attend_first: float32 [1536, 4608], P(('seq', 'dp')), may hold values from -4.7683716e-07 to 4.7683716e-07
- attend_second: float32 [1536, 4608], P(('seq', 'dp')), may hold values from 4.1179106e-17 to 6.588657e-16
- square_weight: float32 [4, 1536, 1536], P(None, ('seq', 'dp'))
- square_first: float32 [4, 1536, 1536], P(None, ('seq', 'dp')), may hold values from -1.1920929e-07 to 1.1920929e-07
- square_second: float32 [4, 1536, 1536], P(None, ('seq', 'dp')), may hold values from 3.2943285e-18 to 5.2709256e-17
- cross_weight: float32 [768, 3072], P(('seq', 'dp')), may hold values from -0.21875 to 0.21875
- cross_first: float32 [768, 3072], P(('seq', 'dp')), may hold values from -4.7683716e-07 to 4.7683716e-07
- cross_second: float32 [768, 3072], P(('seq', 'dp')), may hold values from 4.1179106e-17 to 6.588657e-16
- upward_weight: float32 [1536, 12288], P(('seq', 'dp')), may hold values from -0.15625 to 0.15625
- upward_first: float32 [1536, 12288], P(('seq', 'dp')), may hold values from -4.4703484e-08 to 4.4703484e-08
- upward_second: float32 [1536, 12288], P(('seq', 'dp')), may hold values from 3.2943285e-19 to 5.2709256e-18
- down_weight: float32 [6144, 1536], P(('seq', 'dp')), may hold values from -0.078125 to 0.078125
- down_first: float32 [6144, 1536], P(('seq', 'dp')), may hold values from -1.0430813e-07 to 1.0430813e-07
- down_second: float32 [6144, 1536], P(('seq', 'dp')), may hold values from 2.0589553e-18 to 3.2943285e-17
- gain_weight: float32 [4, 1536], P(None, ('seq', 'dp')), may hold values from 0.5 to 1.5
- gain_first: float32 [4, 1536], P(None, ('seq', 'dp')), may hold values from -1.9073486e-06 to 1.9073486e-06
- gain_second: float32 [4, 1536], P(None, ('seq', 'dp')), may hold values from 6.588657e-16 to 1.0541851e-14
Outputs:
- loss_value: float32 [], replicated
- grad_norm: float32 [], replicated
- new_edge: float32 [896, 1536], P(None, ('seq', 'dp'))
- first_edge: float32 [896, 1536], P(None, ('seq', 'dp'))
- second_edge: float32 [896, 1536], P(None, ('seq', 'dp'))
- new_attend: float32 [1536, 4608], P(('seq', 'dp'))
- first_attend: float32 [1536, 4608], P(('seq', 'dp'))
- second_attend: float32 [1536, 4608], P(('seq', 'dp'))
- new_square: float32 [4, 1536, 1536], P(None, ('seq', 'dp'))
- first_square: float32 [4, 1536, 1536], P(None, ('seq', 'dp'))
- second_square: float32 [4, 1536, 1536], P(None, ('seq', 'dp'))
- new_cross: float32 [768, 3072], P(('seq', 'dp'))
- first_cross: float32 [768, 3072], P(('seq', 'dp'))
- second_cross: float32 [768, 3072], P(('seq', 'dp'))
- new_upward: float32 [1536, 12288], P(('seq', 'dp'))
- first_upward: float32 [1536, 12288], P(('seq', 'dp'))
- second_upward: float32 [1536, 12288], P(('seq', 'dp'))
- new_down: float32 [6144, 1536], P(('seq', 'dp'))
- first_down: float32 [6144, 1536], P(('seq', 'dp'))
- second_down: float32 [6144, 1536], P(('seq', 'dp'))
- clip_gain: float32 [4, 1536], P(None, ('seq', 'dp'))
- first_gain: float32 [4, 1536], P(None, ('seq', 'dp'))
- second_gain: float32 [4, 1536], P(None, ('seq', 'dp'))
The draws below stay inside these ranges and needn't reach their ends.
Inputs may be any that keep to these rules, and one draw needn't show every extreme that they name: `prompt_len`: valid prompt tokens of each clip, mostly short with a long tail; the first clip's prompt fills all 128 slots.
All inputs are finite; a program needn't handle non-finite values.
Results may differ from the reference program's by a relative error of at most 0.011.
Values may be sent and summed in bfloat16 or wider, within the bound.
A program may use at most 1 GiB of HBM per device.

```python
import math
import jax
import jax.numpy as jnp
from jax import lax

D = 1536
H = 24
HD = 64
FF = 6144
CD = 768
C = 64
TF = 256
L = 2048
PT = 128
NB = 1000
CLIPS = 16
NPARAM = 48568320


def draw_prompt_len(key, part):
    first_key = jax.random.fold_in(key, 11)
    second_key = jax.random.fold_in(key, 12)
    a = jax.random.randint(first_key, (CLIPS,), 0, PT - 3)
    b = jax.random.randint(second_key, (CLIPS,), 0, PT - 3)
    lengths = 4 + a * b // (PT - 4)
    return lengths.at[0].set(PT).astype(jnp.int32)


def draw_edge_weight(key, part):
    base = jax.random.normal(key, (2 * C + 3 * TF, D), jnp.float32)
    index = jnp.arange(2 * C + 3 * TF)
    factor = jnp.where(index < C, C ** (-0.5), jnp.where(index < 2 * C, D ** (-0.5), jnp.where(index < 2 * C + TF, TF ** (-0.5), (2 * TF) ** (-0.5))))
    return base * factor[:, None].astype(jnp.float32)


def draw_square_weight(key, part):
    base = jax.random.normal(key, (4, D, D), jnp.float32)
    factor = jnp.array([(L / (3.0 * D)) ** 0.5, D ** (-0.5), (8.0 / D) ** 0.5, D ** (-0.5)], jnp.float32)
    return base * factor[:, None, None]


def with_ends(drawn, key, smallest, largest):
    longest = drawn.shape.index(max(drawn.shape))
    spots = []
    for shift in (0, 1):
        where = [jax.random.randint(jax.random.fold_in(key, axis), (), 0, length) for axis, length in enumerate(drawn.shape)]
        where[longest] = (where[longest] + shift) % drawn.shape[longest]
        spots.append(tuple(where))
    return drawn.at[spots[0]].set(smallest).at[spots[1]].set(largest)


def levels(key, shape, shards, low, top_value):
    def one(dim, shards_of):
        steps = jax.random.uniform(jax.random.fold_in(jax.random.fold_in(key, 6), dim), (shards_of,), jnp.float32, low / len(shards), top_value / len(shards))
        return jnp.repeat(jnp.exp(steps), shape[dim] // shards_of).reshape((-1,) + (1,) * (len(shape) - dim - 1))

    level = one(*shards[0])
    for cut in shards[1:]:
        level = level * one(*cut)
    return level


def centred(own_key, shape, spread, limit, shards=(), kind=jnp.bfloat16):
    level = levels(own_key, shape, shards, -0.22, 0.18) if shards else 1.0
    drawn = jax.random.normal(own_key, shape, jnp.float32) * spread * level
    return jnp.minimum(jnp.maximum(drawn, -limit), limit).astype(kind)


def setup_inputs(seed: int = 0) -> dict:
    streams_of = jax.random.split(jax.random.key(seed), 30)
    return {
        "latents": centred(streams_of[0], (CLIPS, L, C), 1.0, 6.0, ((0, 8), (1, 4))),
        "noise_draw": centred(streams_of[1], (CLIPS, L, C), 1.0, 6.0, ((0, 8), (1, 4))),
        "audio_len": with_ends(jax.random.randint(streams_of[2], (CLIPS,), L // 4, L + 1), jax.random.fold_in(streams_of[2], 1), L // 4, L).astype(jnp.int32),
        "bucket": with_ends(jax.random.randint(streams_of[3], (CLIPS,), 0, NB), jax.random.fold_in(streams_of[3], 1), 0, NB - 1).astype(jnp.int32),
        "timing": with_ends(jax.random.randint(streams_of[4], (CLIPS, 2), 0, 64), jax.random.fold_in(streams_of[4], 1), 0, 63).astype(jnp.int32),
        "prompt": centred(streams_of[5], (CLIPS, PT, CD), 1.0, 6.0, ((0, 8),)),
        "prompt_len": draw_prompt_len(jax.random.fold_in(streams_of[29], 71), 0),
        "step_count": jax.random.randint(streams_of[7], (1,), 2, 21).astype(jnp.int32),
        "edge_weight": draw_edge_weight(jax.random.fold_in(streams_of[29], 71), 0),
        "edge_first": centred(streams_of[9], (2 * C + 3 * TF, D), (0.00022 * NPARAM ** -0.5), 4.76837158203125e-07, ((1, 32),), jnp.float32),
        "edge_second": jnp.clip(jnp.exp(math.log(6.588656897525008e-16) - 2.7725887 * jax.random.uniform(streams_of[10], (2 * C + 3 * TF, D), jnp.float32) ** levels(streams_of[10], (2 * C + 3 * TF, D), ((1, 32),), -0.2, 0.2)), 4.11791056095313e-17, 6.588656897525008e-16),
        "attend_weight": centred(streams_of[11], (D, 3 * D), D ** -0.5, 0.15625, ((0, 32),), jnp.float32),
        "attend_first": centred(streams_of[12], (D, 3 * D), (0.00022 * NPARAM ** -0.5), 4.76837158203125e-07, ((0, 32),), jnp.float32),
        "attend_second": jnp.clip(jnp.exp(math.log(6.588656897525008e-16) - 2.7725887 * jax.random.uniform(streams_of[13], (D, 3 * D), jnp.float32) ** levels(streams_of[13], (D, 3 * D), ((0, 32),), -0.2, 0.2)), 4.11791056095313e-17, 6.588656897525008e-16),
        "square_weight": draw_square_weight(jax.random.fold_in(streams_of[29], 71), 0),
        "square_first": centred(streams_of[15], (4, D, D), (0.00006 * NPARAM ** -0.5), 1.1920928955078125e-07, ((1, 32),), jnp.float32),
        "square_second": jnp.clip(jnp.exp(math.log(5.270925557724676e-17) - 2.7725887 * jax.random.uniform(streams_of[16], (4, D, D), jnp.float32) ** levels(streams_of[16], (4, D, D), ((1, 32),), -0.2, 0.2)), 3.2943284735779223e-18, 5.270925557724676e-17),
        "cross_weight": centred(streams_of[17], (CD, 2 * D), CD ** -0.5, 0.21875, ((0, 32),), jnp.float32),
        "cross_first": centred(streams_of[18], (CD, 2 * D), (0.00022 * NPARAM ** -0.5), 4.76837158203125e-07, ((0, 32),), jnp.float32),
        "cross_second": jnp.clip(jnp.exp(math.log(6.588656897525008e-16) - 2.7725887 * jax.random.uniform(streams_of[19], (CD, 2 * D), jnp.float32) ** levels(streams_of[19], (CD, 2 * D), ((0, 32),), -0.2, 0.2)), 4.11791056095313e-17, 6.588656897525008e-16),
        "upward_weight": centred(streams_of[20], (D, 2 * FF), D ** -0.5, 0.15625, ((0, 32),), jnp.float32),
        "upward_first": centred(streams_of[21], (D, 2 * FF), (0.00002 * NPARAM ** -0.5), 4.470348358154297e-08, ((0, 32),), jnp.float32),
        "upward_second": jnp.clip(jnp.exp(math.log(5.270925557724676e-18) - 2.7725887 * jax.random.uniform(streams_of[22], (D, 2 * FF), jnp.float32) ** levels(streams_of[22], (D, 2 * FF), ((0, 32),), -0.2, 0.2)), 3.2943284735779223e-19, 5.270925557724676e-18),
        "down_weight": centred(streams_of[23], (FF, D), FF ** -0.5, 0.078125, ((0, 32),), jnp.float32),
        "down_first": centred(streams_of[24], (FF, D), (0.000048 * NPARAM ** -0.5), 1.043081283569336e-07, ((0, 32),), jnp.float32),
        "down_second": jnp.clip(jnp.exp(math.log(3.294328514936953e-17) - 2.7725887 * jax.random.uniform(streams_of[25], (FF, D), jnp.float32) ** levels(streams_of[25], (FF, D), ((0, 32),), -0.2, 0.2)), 2.0589553218355956e-18, 3.294328514936953e-17),
        "gain_weight": jnp.clip(1.0 + 0.1 * jax.random.normal(streams_of[26], (4, D), jnp.float32), 0.5, 1.5),
        "gain_first": centred(streams_of[27], (4, D), (0.00088 * NPARAM ** -0.5), 1.9073486328125e-06, ((1, 32),), jnp.float32),
        "gain_second": jnp.clip(jnp.exp(math.log(1.0541851036040013e-14) - 2.7725887 * jax.random.uniform(streams_of[28], (4, D), jnp.float32) ** levels(streams_of[28], (4, D), ((1, 32),), -0.2, 0.2)), 6.588656897525008e-16, 1.0541851036040013e-14),
    }


highest = lax.Precision.HIGHEST
clip_norm = 0.002
learn_rate = 0.1
weight_decay = 0.1
rot_width = 32

@jax.custom_vjp
def low(v):
    return lax.optimization_barrier(v.astype(jnp.bfloat16)).astype(jnp.float32)

@jax.custom_vjp
def low_back(v):
    return v

def low_keep(v):
    return (low(v), None)

def low_pass(kept, grad):
    return (grad,)

def back_keep(v):
    return (v, None)

def back_low(kept, grad):
    return (low(grad),)
low.defvjp(low_keep, low_pass)
low_back.defvjp(back_keep, back_low)

def matmul(a, b):
    return jnp.dot(a, b, precision=highest, preferred_element_type=jnp.float32)

def both_round(v):
    return low(low_back(v))

def layer_normalize(h, norm_gain):
    centered_input = h - lax.optimization_barrier(jnp.mean(h, -1, keepdims=True))
    inverse_deviation = lax.rsqrt(lax.optimization_barrier(jnp.mean(centered_input * centered_input, -1, keepdims=True)) + 1e-05)
    return centered_input * inverse_deviation * norm_gain

def plan(bucket):
    t = (bucket.astype(jnp.float32) + 0.5) / NB
    keep_rate = jnp.cos(t * (math.pi / 2))
    noise_rate = jnp.sin(t * (math.pi / 2))
    snr_ratio = keep_rate * keep_rate / (noise_rate * noise_rate)
    return (t, keep_rate, noise_rate, jnp.minimum(snr_ratio, 5.0) / (snr_ratio + 1.0))

def time_features(t):
    freqs = jnp.exp(-math.log(10000.0) * jnp.arange(TF // 2, dtype=jnp.float32) / (TF // 2))
    angle = t[:, None] * 1000.0 * freqs[None, :]
    return jnp.concatenate([jnp.cos(angle), jnp.sin(angle)], -1)

def timing_features(timing):
    seconds = timing.astype(jnp.float32) / 64.0
    return jnp.concatenate([time_features(seconds[:, 0]), time_features(seconds[:, 1])], -1)

def rope_tables(positions):
    inverse = 10000.0 ** (-2.0 * jnp.arange(rot_width // 2, dtype=jnp.float32) / rot_width)
    angle = positions[:, None].astype(jnp.float32) * inverse[None, :]
    angle = jnp.concatenate([angle, angle], -1)
    return (jnp.cos(angle), jnp.sin(angle))

def rotate(x):
    half = rot_width // 2
    return jnp.concatenate([-x[..., half:], x[..., :half]], -1)

def apply_rope(x, cosine, sine_part):
    turned = x[..., :rot_width]
    turned = turned * cosine[None, :, None, :] + rotate(turned) * sine_part[None, :, None, :]
    return jnp.concatenate([turned, x[..., rot_width:]], -1)

def self_item(q, k, v):
    s = low_back(matmul(q, k.T)) * HD ** (-0.5)
    return matmul(low(jax.nn.softmax(s, -1)), v)
self_checked = jax.checkpoint(self_item)

def forward(weights, batch, weight_sum):
    clean, noisy_part, alen, buck, tim, prm, plen = batch
    groups = clean.shape[0]
    edge, attend, square, cross, upward, down, norm_gains = [low(w) for w in weights]
    t, keep_rate, noise_rate, clip_weight = plan(buck)
    x_in = low(keep_rate[:, None, None] * clean + noise_rate[:, None, None] * noisy_part).reshape(groups * L, C)
    t_feat = low(time_features(t))
    z_feat = low(timing_features(tim))
    t_hidden = low(jax.nn.silu(matmul(t_feat, edge[2 * C:2 * C + TF])))
    leading_token = matmul(t_hidden, square[3]) + matmul(z_feat, edge[2 * C + TF:])
    prefix_normed = low(layer_normalize(leading_token, norm_gains[0]))
    kv_prefix = low(matmul(prefix_normed, attend[:, D:]))
    k_prefix = kv_prefix[:, :D].reshape(groups * H, 1, HD)
    v_prefix = kv_prefix[:, D:].reshape(groups * H, 1, HD)
    h = low_back(matmul(x_in, edge[:C]))
    first_normed = low(layer_normalize(h, norm_gains[0]))
    projected = low_back(matmul(first_normed, attend)).reshape(groups, L, 3, H, HD)
    cosine, sine_part = rope_tables(jnp.arange(L) + 1)
    q = both_round(apply_rope(projected[:, :, 0], cosine, sine_part))
    k = both_round(apply_rope(projected[:, :, 1], cosine, sine_part))
    v = both_round(projected[:, :, 2])

    def as_items(x):
        return x.transpose(0, 2, 1, 3).reshape(groups * H, L, HD)
    keys = jnp.concatenate([k_prefix, as_items(k)], 1)
    values = jnp.concatenate([v_prefix, as_items(v)], 1)
    o = lax.map(lambda parts: self_checked(parts[0], parts[1], parts[2]), (as_items(q), keys, values))
    o = both_round(o.reshape(groups, H, L, HD).transpose(0, 2, 1, 3).reshape(groups * L, D))
    h = h + low_back(matmul(o, square[0]))
    second_normed = low(layer_normalize(h, norm_gains[1]))
    cross_q = both_round(matmul(second_normed, square[1])).reshape(groups, L, H, HD)
    cross_kv = low(jnp.einsum('gpc,ce->gpe', prm, cross, precision=highest))
    cross_k = cross_kv[..., :D].reshape(groups, PT, H, HD)
    cross_v = cross_kv[..., D:].reshape(groups, PT, H, HD)
    key_mask = jnp.arange(PT)[None, :] < plen[:, None]
    scores = low_back(jnp.einsum('gfhd,gphd->ghfp', cross_q, cross_k, precision=highest)) * HD ** (-0.5)
    scores = jnp.where(key_mask[:, None, None, :], scores, -1000000000.0)
    probs = jax.nn.softmax(scores, -1)
    co = both_round(jnp.einsum('ghfp,gphd->gfhd', low(probs), cross_v, precision=highest).reshape(groups * L, D))
    h = h + low_back(matmul(co, square[2]))
    third_normed = low(layer_normalize(h, norm_gains[2]))
    gate_up = low_back(matmul(third_normed, upward))
    hidden = low(jax.nn.silu(gate_up[:, :FF]) * gate_up[:, FF:])
    h = h + low_back(matmul(hidden, down))
    fourth_normed = low(layer_normalize(h, norm_gains[3]))
    predicted = low_back(matmul(fourth_normed, edge[C:2 * C].T))
    target = (keep_rate[:, None, None] * noisy_part - noise_rate[:, None, None] * clean).reshape(groups * L, C)
    frame_mask = (jnp.arange(L)[None, :] < alen[:, None]).astype(jnp.float32)
    row_weight = (clip_weight[:, None] * frame_mask).reshape(groups * L)
    error = predicted - target
    return jnp.sum(row_weight[:, None] * error * error) / (C * weight_sum)

def adam(w, m, v, g, first_fix, second_fix):
    first = 0.9 * m + 0.1 * g
    second = 0.999 * v + 0.001 * g * g
    new = w - learn_rate * (first / first_fix / (jnp.sqrt(second / second_fix) + 1e-08) + weight_decay * w)
    return (new, first, second)

def reference(latents, noise_draw, audio_len, bucket, timing, prompt, prompt_len, step_count, edge_weight, edge_first, edge_second, attend_weight, attend_first, attend_second, square_weight, square_first, square_second, cross_weight, cross_first, cross_second, upward_weight, upward_first, upward_second, down_weight, down_first, down_second, gain_weight, gain_first, gain_second):
    weights = (edge_weight, attend_weight, square_weight, cross_weight, upward_weight, down_weight, gain_weight)
    firsts = (edge_first, attend_first, square_first, cross_first, upward_first, down_first, gain_first)
    seconds = (edge_second, attend_second, square_second, cross_second, upward_second, down_second, gain_second)
    t, keep_rate, noise_rate, clip_weight = plan(bucket)
    weight_sum = jnp.sum(clip_weight * audio_len.astype(jnp.float32))
    pairs = CLIPS // 2

    def regroup(x):
        return x.reshape((pairs, 2) + x.shape[1:])
    inputs = (regroup(latents.astype(jnp.float32)), regroup(noise_draw.astype(jnp.float32)), regroup(audio_len), regroup(bucket), regroup(timing), regroup(prompt.astype(jnp.float32)), regroup(prompt_len))

    def one_pair(carry, batch):
        grads, total = carry
        value, pull = jax.vjp(lambda w: forward(w, batch, weight_sum), weights)
        step_grads, = pull(jnp.ones_like(value))
        return ((jax.tree.map(jnp.add, grads, step_grads), total + value), None)
    zero_grads = jax.tree.map(jnp.zeros_like, weights)
    (grads, loss_value), unused = lax.scan(one_pair, (zero_grads, jnp.zeros((), jnp.float32)), inputs)
    grad_norm = jnp.sqrt(sum((jnp.sum(g * g) for g in grads)))
    factor = jnp.minimum(1.0, clip_norm / grad_norm)
    count = step_count[0].astype(jnp.float32)
    first_fix = 1.0 - 0.9 ** count
    second_fix = 1.0 - 0.999 ** count
    out = [adam(w, m, v, g * factor, first_fix, second_fix) for w, m, v, g in zip(weights, firsts, seconds, grads)]
    return (loss_value, grad_norm, out[0][0], out[0][1], out[0][2], out[1][0], out[1][1], out[1][2], out[2][0], out[2][1], out[2][2], out[3][0], out[3][1], out[3][2], out[4][0], out[4][1], out[4][2], out[5][0], out[5][1], out[5][2], grads[6] * factor, out[6][1], out[6][2])
```

```python
import functools
import math

import jax
import jax.numpy as jnp
from jax import lax
from jax.experimental import pallas as pl
from jax.experimental.pallas import tpu as pltpu
from jax.sharding import Mesh
from jax.sharding import PartitionSpec as P

D = 1536
H = 24
HD = 64
FF = 6144
C = 64
TF = 256
PT = 128
NB = 1000


highest = lax.Precision.HIGHEST
clip_norm = 0.002
learn_rate = 0.1
weight_decay = 0.1
rot_width = 32


def layer_normalize(h, norm_gain):
    centered_input = h - jnp.mean(h, -1, keepdims=True)
    inverse_deviation = lax.rsqrt(
        jnp.mean(centered_input * centered_input, -1, keepdims=True) + 1e-05
    )
    standardized = centered_input * inverse_deviation
    return (standardized * norm_gain, standardized, inverse_deviation)


def norm_backward(incoming_gradient, standardized, inverse_deviation, norm_gain):
    scaled_gradient = incoming_gradient * norm_gain
    gain_gradient = jnp.sum(incoming_gradient * standardized, 0)
    d_in = inverse_deviation * (
        scaled_gradient
        - jnp.mean(scaled_gradient, -1, keepdims=True)
        - standardized * jnp.mean(scaled_gradient * standardized, -1, keepdims=True)
    )
    return (d_in, gain_gradient)


def plan(bucket):
    t = (bucket.astype(jnp.float32) + 0.5) / NB
    keep_rate = jnp.cos(t * (math.pi / 2))
    noise_rate = jnp.sin(t * (math.pi / 2))
    snr_ratio = keep_rate * keep_rate / (noise_rate * noise_rate)
    return (t, keep_rate, noise_rate, jnp.minimum(snr_ratio, 5.0) / (snr_ratio + 1.0))


def time_features(t):
    freqs = jnp.exp(-math.log(10000.0) * jnp.arange(TF // 2, dtype=jnp.float32) / (TF // 2))
    angle = t[:, None] * 1000.0 * freqs[None, :]
    return jnp.concatenate([jnp.cos(angle), jnp.sin(angle)], -1)


def timing_features(timing):
    seconds = timing.astype(jnp.float32) / 64.0
    return jnp.concatenate([time_features(seconds[:, 0]), time_features(seconds[:, 1])], -1)


def rope_tables(positions):
    inverse = 10000.0 ** (-2.0 * jnp.arange(rot_width // 2, dtype=jnp.float32) / rot_width)
    angle = positions[:, None].astype(jnp.float32) * inverse[None, :]
    angle = jnp.concatenate([angle, angle], -1)
    return (jnp.cos(angle), jnp.sin(angle))


def rotate(x):
    half = rot_width // 2
    return jnp.concatenate([-x[..., half:], x[..., :half]], -1)


def apply_rope(x, cosine, sine_part):
    turned = x[..., :rot_width]
    turned = turned * cosine[None, :, None, :] + rotate(turned) * sine_part[None, :, None, :]
    return jnp.concatenate([turned, x[..., rot_width:]], -1)


def rope_back(incoming_gradient, cosine, sine_part):
    turned = incoming_gradient[..., :rot_width]
    turned = turned * cosine[None, :, None, :] - rotate(turned * sine_part[None, :, None, :])
    return jnp.concatenate([turned, incoming_gradient[..., rot_width:]], -1)


def split_blocks(x, count, block):
    return x.reshape((x.shape[0], count, block) + x.shape[2:]).swapaxes(0, 1)


def join_blocks(x):
    x = x.swapaxes(0, 1)
    return x.reshape((x.shape[0], x.shape[1] * x.shape[2]) + x.shape[3:])


def attend(q, keys, values):
    rows_q = q.shape[1]
    block = min(512, rows_q)
    count = rows_q // block
    score_scale = HD ** (-0.5)

    def one_block(q_block):
        s = (
            jnp.einsum("ibd,ikd->ibk", q_block, keys, preferred_element_type=jnp.float32)
            * score_scale
        )
        top = jnp.max(s, -1, keepdims=True)
        lse = top + jnp.log(jnp.sum(jnp.exp(s - top), -1, keepdims=True))
        p = jnp.exp(s - lse)
        o = jnp.einsum(
            "ibk,ikd->ibd", p.astype(jnp.bfloat16), values, preferred_element_type=jnp.float32
        )
        return (o, lse[..., 0])

    outs, lses = lax.map(one_block, split_blocks(q, count, block))
    return (join_blocks(outs), join_blocks(lses))


def attend_back(q, keys, values, lse, grad_o):
    rows_q = q.shape[1]
    block = min(512, rows_q)
    count = rows_q // block
    score_scale = HD ** (-0.5)

    def one_block(carry, parts):
        d_key, d_value = carry
        q_block, g_block, l_block = parts
        s = (
            jnp.einsum("ibd,ikd->ibk", q_block, keys, preferred_element_type=jnp.float32)
            * score_scale
        )
        p = jnp.exp(s - l_block[..., None])
        d_prob = jnp.einsum("ibd,ikd->ibk", g_block, values, preferred_element_type=jnp.float32)
        d_value = d_value + jnp.einsum(
            "ibk,ibd->ikd", p.astype(jnp.bfloat16), g_block, preferred_element_type=jnp.float32
        )
        d_score = (p * (d_prob - jnp.sum(d_prob * p, -1, keepdims=True)) * score_scale).astype(
            jnp.bfloat16
        )
        d_query = jnp.einsum("ibk,ikd->ibd", d_score, keys, preferred_element_type=jnp.float32)
        d_key = d_key + jnp.einsum(
            "ibk,ibd->ikd", d_score, q_block, preferred_element_type=jnp.float32
        )
        return ((d_key, d_value), d_query)

    zeros = jnp.zeros(keys.shape, jnp.float32)
    parts = (
        split_blocks(q, count, block),
        split_blocks(grad_o, count, block),
        split_blocks(lse, count, block),
    )
    (d_key, d_value), d_queries = lax.scan(one_block, (zeros, zeros), parts)
    return (join_blocks(d_queries), d_key, d_value)


def adam(w, m, v, g, first_fix, second_fix):
    first = 0.9 * m + 0.1 * g
    second = 0.999 * v + 0.001 * g * g
    new = w - learn_rate * (
        first / first_fix / (jnp.sqrt(second / second_fix) + 1e-08) + weight_decay * w
    )
    return (new, first, second)


def exact(form, a, b):
    return jnp.einsum(form, a, b, precision=highest, preferred_element_type=jnp.float32)


def general_body(
    latents,
    noise_draw,
    audio_len,
    bucket,
    timing,
    prompt,
    prompt_len,
    step_count,
    edge_weight,
    edge_first,
    edge_second,
    attend_weight,
    attend_first,
    attend_second,
    square_weight,
    square_first,
    square_second,
    cross_weight,
    cross_first,
    cross_second,
    upward_weight,
    upward_first,
    upward_second,
    down_weight,
    down_first,
    down_second,
    gain_weight,
    gain_first,
    gain_second,
):
    low_type = jnp.bfloat16
    wide = jnp.float32
    groups, frames = (latents.shape[0], latents.shape[1])
    total_rows = groups * frames
    items = groups * H
    edge16, attend16, square16, cross16, upward16, down16, gain16 = (
        lax.all_gather(edge_weight.astype(low_type), ("seq", "dp"), axis=1, tiled=True),
        lax.all_gather(attend_weight.astype(low_type), ("seq", "dp"), axis=0, tiled=True),
        lax.all_gather(square_weight.astype(low_type), ("seq", "dp"), axis=1, tiled=True),
        lax.all_gather(cross_weight.astype(low_type), ("seq", "dp"), axis=0, tiled=True),
        lax.all_gather(upward_weight.astype(low_type), ("seq", "dp"), axis=0, tiled=True),
        lax.all_gather(down_weight.astype(low_type), ("seq", "dp"), axis=0, tiled=True),
        lax.all_gather(gain_weight.astype(low_type), ("seq", "dp"), axis=1, tiled=True),
    )
    norm_gains = gain16.astype(wide)
    positions = lax.axis_index("seq") * frames + jnp.arange(frames, dtype=jnp.int32)
    t, keep_rate, noise_rate, clip_weight = plan(bucket)
    frame_mask = (positions[None, :] < audio_len[:, None]).astype(wide)
    row_weight = (clip_weight[:, None] * frame_mask).reshape(total_rows)
    weight_sum = lax.psum(jnp.sum(row_weight), ("seq", "dp"))
    clean = latents.astype(wide)
    noisy_part = noise_draw.astype(wide)
    x_in = (
        (keep_rate[:, None, None] * clean + noise_rate[:, None, None] * noisy_part)
        .astype(low_type)
        .reshape(total_rows, C)
    )
    t_feat = time_features(t).astype(low_type)
    z_feat = timing_features(timing).astype(low_type)
    t_pre = jnp.dot(t_feat, edge16[2 * C : 2 * C + TF], preferred_element_type=wide)
    t_hidden = jax.nn.silu(t_pre).astype(low_type)
    leading_token = jnp.dot(t_hidden, square16[3], preferred_element_type=wide) + jnp.dot(
        z_feat, edge16[2 * C + TF :], preferred_element_type=wide
    )
    prefix_normed, prefix_standardized, prefix_inverse_deviation = layer_normalize(
        leading_token, norm_gains[0]
    )
    n_prefix_low = prefix_normed.astype(low_type)
    kv_prefix = jnp.dot(n_prefix_low, attend16[:, D:], preferred_element_type=wide).astype(low_type)
    k_prefix = kv_prefix[:, :D].reshape(items, 1, HD)
    v_prefix = kv_prefix[:, D:].reshape(items, 1, HD)
    hidden_start = jnp.dot(x_in, edge16[:C], preferred_element_type=wide)
    first_normed, first_standardized, first_inverse_deviation = layer_normalize(
        hidden_start, norm_gains[0]
    )
    n1_low = first_normed.astype(low_type)
    projected = jnp.dot(n1_low, attend16, preferred_element_type=wide).reshape(
        groups, frames, 3, H, HD
    )
    cosine, sine_part = rope_tables(positions + 1)
    rotated = jnp.stack(
        [
            apply_rope(projected[:, :, 0], cosine, sine_part),
            apply_rope(projected[:, :, 1], cosine, sine_part),
            projected[:, :, 2],
        ]
    ).astype(low_type)
    as_items = rotated.transpose(0, 1, 3, 2, 4).reshape(3, items, frames, HD)
    q_use = as_items[0]
    key_value = lax.all_gather(as_items[1:], "seq", axis=2, tiled=True)
    keys = jnp.concatenate([k_prefix, key_value[0]], 1)
    values = jnp.concatenate([v_prefix, key_value[1]], 1)
    o_items, lse = attend(q_use, keys, values)
    o_local = o_items.astype(low_type)
    o_low = o_local.reshape(groups, H, frames, HD).transpose(0, 2, 1, 3).reshape(total_rows, D)
    hidden_after_self = hidden_start + jnp.dot(o_low, square16[0], preferred_element_type=wide)
    second_normed, second_standardized, second_inverse_deviation = layer_normalize(
        hidden_after_self, norm_gains[1]
    )
    n2_low = second_normed.astype(low_type)
    cross_q = (
        jnp.dot(n2_low, square16[1], preferred_element_type=wide)
        .astype(low_type)
        .reshape(groups, frames, H, HD)
    )
    cross_kv = jnp.einsum("gpc,ce->gpe", prompt, cross16, preferred_element_type=wide).astype(
        low_type
    )
    cross_k = cross_kv[..., :D].reshape(groups, PT, H, HD)
    cross_v = cross_kv[..., D:].reshape(groups, PT, H, HD)
    key_mask = jnp.arange(PT)[None, :] < prompt_len[:, None]
    score_scale = HD ** (-0.5)
    scores = (
        jnp.einsum("gfhd,gphd->ghfp", cross_q, cross_k, preferred_element_type=wide) * score_scale
    )
    scores = jnp.where(key_mask[:, None, None, :], scores, -1000000000.0)
    probs = jax.nn.softmax(scores, -1)
    probs_low = probs.astype(low_type)
    co_low = (
        jnp.einsum("ghfp,gphd->gfhd", probs_low, cross_v, preferred_element_type=wide)
        .astype(low_type)
        .reshape(total_rows, D)
    )
    hidden_after_cross = hidden_after_self + jnp.dot(
        co_low, square16[2], preferred_element_type=wide
    )
    third_normed, third_standardized, third_inverse_deviation = layer_normalize(
        hidden_after_cross, norm_gains[2]
    )
    n3_low = third_normed.astype(low_type)
    gate_up = jnp.dot(n3_low, upward16, preferred_element_type=wide)
    gate, upper = (gate_up[:, :FF], gate_up[:, FF:])
    hidden = (jax.nn.silu(gate) * upper).astype(low_type)
    hidden_after_feed = hidden_after_cross + jnp.dot(hidden, down16, preferred_element_type=wide)
    fourth_normed, fourth_standardized, fourth_inverse_deviation = layer_normalize(
        hidden_after_feed, norm_gains[3]
    )
    n4_low = fourth_normed.astype(low_type)
    predicted = jnp.einsum("rd,cd->rc", n4_low, edge16[C : 2 * C], preferred_element_type=wide)
    target = (keep_rate[:, None, None] * noisy_part - noise_rate[:, None, None] * clean).reshape(
        total_rows, C
    )
    error = predicted - target
    loss_local = jnp.sum(row_weight[:, None] * error * error)
    d_pred = (2.0 / (C * weight_sum) * row_weight[:, None] * error).astype(low_type)
    g_out = jnp.einsum("rc,rd->cd", d_pred, n4_low, preferred_element_type=wide)
    fourth_norm_gradient = jnp.dot(d_pred, edge16[C : 2 * C], preferred_element_type=wide)
    hidden_gradient, fourth_gain_gradient = norm_backward(
        fourth_norm_gradient, fourth_standardized, fourth_inverse_deviation, norm_gains[3]
    )
    d_f = hidden_gradient.astype(low_type)
    g_down = jnp.einsum("rf,rd->fd", hidden, d_f, preferred_element_type=wide)
    d_hidden = jnp.einsum("rd,fd->rf", d_f, down16, preferred_element_type=wide)
    sig = jax.nn.sigmoid(gate)
    d_gate_up = jnp.concatenate(
        [d_hidden * upper * sig * (1.0 + gate * (1.0 - sig)), d_hidden * gate * sig], -1
    ).astype(low_type)
    g_up = jnp.einsum("rd,re->de", n3_low, d_gate_up, preferred_element_type=wide)
    third_norm_gradient = jnp.einsum("re,de->rd", d_gate_up, upward16, preferred_element_type=wide)
    partial_gradient, third_gain_gradient = norm_backward(
        third_norm_gradient, third_standardized, third_inverse_deviation, norm_gains[2]
    )
    hidden_gradient = hidden_gradient + partial_gradient
    d_c = hidden_gradient.astype(low_type)
    g_co = jnp.einsum("rd,re->de", co_low, d_c, preferred_element_type=wide)
    d_co = (
        jnp.einsum("re,de->rd", d_c, square16[2], preferred_element_type=wide)
        .astype(low_type)
        .reshape(groups, frames, H, HD)
    )
    d_prob = jnp.einsum("gfhd,gphd->ghfp", d_co, cross_v, preferred_element_type=wide)
    d_cv = jnp.einsum("ghfp,gfhd->gphd", probs_low, d_co, preferred_element_type=wide)
    d_score = (probs * (d_prob - jnp.sum(d_prob * probs, -1, keepdims=True)) * score_scale).astype(
        low_type
    )
    d_cq = (
        jnp.einsum("ghfp,gphd->gfhd", d_score, cross_k, preferred_element_type=wide)
        .astype(low_type)
        .reshape(total_rows, D)
    )
    d_ck = jnp.einsum("ghfp,gfhd->gphd", d_score, cross_q, preferred_element_type=wide)
    d_cross_kv = jnp.concatenate([d_ck.reshape(groups, PT, D), d_cv.reshape(groups, PT, D)], -1)
    g_cross = exact("gpc,gpe->ce", prompt.astype(wide), d_cross_kv)
    g_cq = jnp.einsum("rd,re->de", n2_low, d_cq, preferred_element_type=wide)
    second_norm_gradient = jnp.einsum("re,de->rd", d_cq, square16[1], preferred_element_type=wide)
    partial_gradient, second_gain_gradient = norm_backward(
        second_norm_gradient, second_standardized, second_inverse_deviation, norm_gains[1]
    )
    hidden_gradient = hidden_gradient + partial_gradient
    d_a = hidden_gradient.astype(low_type)
    g_o = jnp.einsum("rd,re->de", o_low, d_a, preferred_element_type=wide)
    d_o = jnp.einsum("re,de->rd", d_a, square16[0], preferred_element_type=wide).astype(low_type)
    d_o_items = d_o.reshape(groups, frames, H, HD).transpose(0, 2, 1, 3).reshape(items, frames, HD)
    d_query, d_key, d_value = attend_back(q_use, keys, values, lse, d_o_items)
    summed_key, summed_value = (
        lax.psum_scatter(
            d_key[:, 1:].astype(jnp.bfloat16), "seq", scatter_dimension=1, tiled=True
        ).astype(jnp.float32),
        lax.psum_scatter(
            d_value[:, 1:].astype(jnp.bfloat16), "seq", scatter_dimension=1, tiled=True
        ).astype(jnp.float32),
    )
    d_items = jnp.stack(
        [d_query.astype(low_type), summed_key.astype(low_type), summed_value.astype(low_type)]
    )
    d_key_prefix = d_key[:, :1]
    d_value_prefix = d_value[:, :1]
    d_rot = d_items.astype(wide).reshape(3, groups, H, frames, HD).transpose(1, 3, 0, 2, 4)
    d_projected = (
        jnp.stack(
            [
                rope_back(d_rot[:, :, 0], cosine, sine_part),
                rope_back(d_rot[:, :, 1], cosine, sine_part),
                d_rot[:, :, 2],
            ],
            2,
        )
        .reshape(total_rows, 3 * D)
        .astype(low_type)
    )
    g_attend = jnp.einsum("rd,re->de", n1_low, d_projected, preferred_element_type=wide)
    first_norm_gradient = jnp.einsum(
        "re,de->rd", d_projected, attend16, preferred_element_type=wide
    )
    partial_gradient, first_gain_gradient = norm_backward(
        first_norm_gradient, first_standardized, first_inverse_deviation, norm_gains[0]
    )
    hidden_gradient = hidden_gradient + partial_gradient
    g_in = jnp.einsum(
        "rc,rd->cd", x_in, hidden_gradient.astype(low_type), preferred_element_type=wide
    )
    d_kv_prefix = jnp.concatenate(
        [d_key_prefix.reshape(groups, D), d_value_prefix.reshape(groups, D)], -1
    )
    attend_kv = attend16[:, D:].astype(wide)
    g_attend = g_attend.at[:, D:].add(exact("gd,ge->de", n_prefix_low.astype(wide), d_kv_prefix))
    prefix_norm_gradient = exact("ge,de->gd", d_kv_prefix, attend_kv)
    leading_token_gradient, prefix_gain_gradient = norm_backward(
        prefix_norm_gradient, prefix_standardized, prefix_inverse_deviation, norm_gains[0]
    )
    g_timing = exact("gz,gd->zd", z_feat.astype(wide), leading_token_gradient)
    g_t2 = exact("ge,gd->ed", t_hidden.astype(wide), leading_token_gradient)
    d_t_hidden = exact("gd,ed->ge", leading_token_gradient, square16[3].astype(wide))
    t_sig = jax.nn.sigmoid(t_pre)
    d_t_pre = d_t_hidden * t_sig * (1.0 + t_pre * (1.0 - t_sig))
    g_t1 = exact("gz,gd->zd", t_feat.astype(wide), d_t_pre)
    g_edge = jnp.concatenate([g_in, g_out, g_t1, g_timing], 0)
    g_square = jnp.stack([g_o, g_cq, g_co, g_t2])
    g_gain = jnp.stack(
        [
            first_gain_gradient + prefix_gain_gradient,
            second_gain_gradient,
            third_gain_gradient,
            fourth_gain_gradient,
        ]
    )
    sharded = (
        lax.psum_scatter(g_edge, ("seq", "dp"), scatter_dimension=1, tiled=True),
        lax.psum_scatter(g_attend, ("seq", "dp"), scatter_dimension=0, tiled=True),
        lax.psum_scatter(g_square, ("seq", "dp"), scatter_dimension=1, tiled=True),
        lax.psum_scatter(g_cross, ("seq", "dp"), scatter_dimension=0, tiled=True),
        lax.psum_scatter(g_up, ("seq", "dp"), scatter_dimension=0, tiled=True),
        lax.psum_scatter(g_down, ("seq", "dp"), scatter_dimension=0, tiled=True),
        lax.psum_scatter(g_gain, ("seq", "dp"), scatter_dimension=1, tiled=True),
    )
    square_local = sum((jnp.sum(g * g) for g in sharded))
    square_total, loss_total = lax.psum((square_local, loss_local), ("seq", "dp"))
    grad_norm = jnp.sqrt(square_total)
    loss_value = loss_total / (C * weight_sum)
    factor = jnp.minimum(1.0, clip_norm / grad_norm)
    count = step_count[0].astype(wide)
    first_fix = 1.0 - 0.9**count
    second_fix = 1.0 - 0.999**count
    weights = (
        edge_weight,
        attend_weight,
        square_weight,
        cross_weight,
        upward_weight,
        down_weight,
        gain_weight,
    )
    firsts = (
        edge_first,
        attend_first,
        square_first,
        cross_first,
        upward_first,
        down_first,
        gain_first,
    )
    seconds = (
        edge_second,
        attend_second,
        square_second,
        cross_second,
        upward_second,
        down_second,
        gain_second,
    )
    out = [
        adam(w, m, v, g * factor, first_fix, second_fix)
        for w, m, v, g in zip(weights, firsts, seconds, sharded)
    ]
    return (
        loss_value,
        grad_norm,
        out[0][0],
        out[0][1],
        out[0][2],
        out[1][0],
        out[1][1],
        out[1][2],
        out[2][0],
        out[2][1],
        out[2][2],
        out[3][0],
        out[3][1],
        out[3][2],
        out[4][0],
        out[4][1],
        out[4][2],
        out[5][0],
        out[5][1],
        out[5][2],
        sharded[6] * factor,
        out[6][1],
        out[6][2],
    )


f32 = jnp.float32
bf16 = jnp.bfloat16
HALF = D // 2
PAIRS = HALF // 128
HIDE = FF // 2


def dot_nt(a, b):
    return lax.dot_general(a, b, (((1,), (1,)), ((), ())), preferred_element_type=f32)


def dot_nn(a, b):
    return lax.dot_general(a, b, (((1,), (0,)), ((), ())), preferred_element_type=f32)


def dot_tn(a, b):
    return lax.dot_general(a, b, (((0,), (0,)), ((), ())), preferred_element_type=f32)


def call(kernel, grid, in_specs, out_specs, out_shape, scratch, cost, *operands):
    return pl.pallas_call(
        kernel,
        grid=grid,
        in_specs=in_specs,
        out_specs=out_specs,
        out_shape=out_shape,
        scratch_shapes=scratch,
        cost_estimate=pl.CostEstimate(flops=cost[0], bytes_accessed=cost[1], transcendentals=0),
        compiler_params=pltpu.CompilerParams(vmem_limit_bytes=60 << 20),
    )(*operands)


def shape_of(shape, kind):
    return jax.ShapeDtypeStruct(shape, kind)


def turn(y, cosine, sine_up, sine_down):
    return y * cosine + pltpu.roll(y, 16, 1) * sine_up + pltpu.roll(y, 112, 1) * sine_down


def turn_tables(positions):
    lane = jnp.arange(128) % HD
    inverse = 10000.0 ** (-2.0 * jnp.arange(rot_width // 2, dtype=f32) / rot_width)
    angle = positions[:, None].astype(f32) * inverse[None, :]
    wide_angle = jnp.tile(angle, (1, 128 // (rot_width // 2)))
    cosine = jnp.where(lane[None, :] < rot_width, jnp.cos(wide_angle), 1.0)
    sine = jnp.sin(wide_angle)
    second = (lane[None, :] >= rot_width // 2) & (lane[None, :] < rot_width)
    sine_up = jnp.where(second, sine, 0.0)
    sine_down = jnp.where(lane[None, :] < rot_width // 2, -sine, 0.0)
    return (cosine, sine_up, sine_down)


def qkv_kernel(n_ref, w_ref, cos_ref, up_ref, down_ref, out_ref):
    part = pl.program_id(0)
    y = dot_nn(n_ref[...], w_ref[...])

    @pl.when(part < 2)
    def _():
        scale = jnp.where(part == 0, HD ** (-0.5), 1.0)
        for j in range(PAIRS):
            block = y[:, j * 128 : (j + 1) * 128]
            turned = turn(block, cos_ref[...], up_ref[...], down_ref[...])
            out_ref[:, j * 128 : (j + 1) * 128] = (turned * scale).astype(bf16)

    @pl.when(part == 2)
    def _():
        out_ref[...] = y.astype(bf16)


def qkv_project(n, w, tables, block=512):
    rows = n.shape[0]
    table = pl.BlockSpec((block, 128), lambda p, i: (i, 0))
    return call(
        qkv_kernel,
        (3, rows // block),
        [
            pl.BlockSpec((block, D), lambda p, i: (i, 0)),
            pl.BlockSpec((D, HALF), lambda p, i: (0, p)),
            table,
            table,
            table,
        ],
        pl.BlockSpec((block, HALF), lambda p, i: (i, p)),
        shape_of((rows, 3 * HALF), bf16),
        [],
        (2 * rows * D * 3 * HALF, 4 * rows * D * 2),
        n,
        w,
        *tables,
    )


def attend_kernel(q_ref, k_ref, v_ref, k0_ref, v0_ref, o_ref, lse_ref, *, chunk, count):
    q = q_ref[...]
    rows = q.shape[0]
    lane = lax.broadcasted_iota(jnp.int32, q.shape, 1)
    k0 = k0_ref[0:1].astype(f32)
    v0 = v0_ref[0:1].astype(f32)
    outs = []
    for head in range(2):
        mine = jnp.where((lane // HD) == head, q, jnp.zeros_like(q))
        top = jnp.sum(mine.astype(f32) * k0, 1, keepdims=True)
        total = jnp.ones_like(top)
        acc = jnp.broadcast_to(v0, (rows, 128))
        for c in range(count):
            s = dot_nt(mine, k_ref[c * chunk : (c + 1) * chunk])
            new_top = jnp.maximum(top, jnp.max(s, 1, keepdims=True))
            fade = jnp.exp(top - new_top)
            p = jnp.exp(s - new_top)
            total = total * fade + jnp.sum(p, 1, keepdims=True)
            acc = acc * fade + dot_nn(p.astype(bf16), v_ref[c * chunk : (c + 1) * chunk])
            top = new_top
        outs.append(acc / total)
        lse_ref[0, head : head + 1, :] = (top + jnp.log(total)).T
    o_ref[...] = jnp.where(lane < HD, outs[0], outs[1]).astype(bf16)


def attend_forward(qkv, k0, v0, block=1024, chunk=512):
    rows = qkv.shape[0]
    lead = pl.BlockSpec((16, 128), lambda j, i: (0, j))
    return call(
        functools.partial(attend_kernel, chunk=chunk, count=rows // chunk),
        (PAIRS, rows // block),
        [
            pl.BlockSpec((block, 128), lambda j, i: (i, j)),
            pl.BlockSpec((rows, 128), lambda j, i: (0, PAIRS + j)),
            pl.BlockSpec((rows, 128), lambda j, i: (0, 2 * PAIRS + j)),
            lead,
            lead,
        ],
        [
            pl.BlockSpec((block, 128), lambda j, i: (i, j)),
            pl.BlockSpec((1, 2, block), lambda j, i: (j, 0, i)),
        ],
        [shape_of((rows, HALF), bf16), shape_of((PAIRS, 2, rows), f32)],
        [],
        (16 * rows * rows * HALF, 5 * rows * D * 2),
        qkv,
        qkv,
        qkv,
        k0,
        v0,
    )


def attend_back_kernel(
    q_ref, g_ref, o_ref, lse_ref, cos_ref, up_ref, down_ref,
    k_ref, v_ref, k0_ref, v0_ref, kcos_ref, kup_ref, kdown_ref,
    dq_ref, dk_ref, dv_ref, dk0_ref, dv0_ref,
    kt, dka, dva, dk0a, dv0a, *, chunk, count, steps,
):
    i = pl.program_id(1)

    @pl.when(i == 0)
    def _():
        kt[...] = k_ref[...].T
        dka[...] = jnp.zeros_like(dka)
        dva[...] = jnp.zeros_like(dva)
        dk0a[...] = jnp.zeros_like(dk0a)
        dv0a[...] = jnp.zeros_like(dv0a)

    q = q_ref[...]
    g = g_ref[...]
    rows = q.shape[0]
    lane = lax.broadcasted_iota(jnp.int32, q.shape, 1)
    row = lax.broadcasted_iota(jnp.int32, (16, rows), 0)
    go = (g.astype(f32) * o_ref[...].astype(f32)).T
    k0t = k0_ref[...].T
    dqs = []
    for head in range(2):
        sel = (lane // HD) == head
        low_row, high_row = head * HD, (head + 1) * HD
        qm = jnp.where(sel, q, jnp.zeros_like(q))
        gm = jnp.where(sel, g, jnp.zeros_like(g))
        lse = lse_ref[0, head : head + 1, :]
        delta = jnp.sum(go[low_row:high_row], 0, keepdims=True)
        s = dot_nt(k0_ref[...], qm)
        p = jnp.where(row == 0, jnp.exp(s - lse), 0.0)
        ds = (p * (dot_nt(v0_ref[...], gm) - delta)).astype(bf16)
        dk0a[...] += dot_nn(ds, qm)
        dv0a[...] += dot_nn(p.astype(bf16), gm)
        dq = dot_nn(k0t[low_row:high_row], ds)
        for c in range(count):
            part = pl.ds(c * chunk, chunk)
            p = jnp.exp(dot_nt(k_ref[part], qm) - lse)
            ds = (p * (dot_nt(v_ref[part], gm) - delta)).astype(bf16)
            dva[part] += dot_nn(p.astype(bf16), gm)
            dka[part] += dot_nn(ds, qm)
            dq = dq + dot_nn(kt[low_row:high_row, c * chunk : (c + 1) * chunk], ds)
        dqs.append(dq)
    dq = (jnp.concatenate(dqs, 0).T * HD ** (-0.5)).astype(bf16).astype(f32)
    dq_ref[...] = turn(dq, cos_ref[...], -up_ref[...], -down_ref[...]).astype(bf16)

    @pl.when(i == steps - 1)
    def _():
        dk = dka[...].astype(bf16).astype(f32)
        dk_ref[...] = turn(dk, kcos_ref[...], -kup_ref[...], -kdown_ref[...]).astype(bf16)
        dv_ref[...] = dva[...].astype(bf16)
        dk0_ref[...] = dk0a[...]
        dv0_ref[...] = dv0a[...]


def attend_backward(qkv, g, o, lse, k0, v0, tables, block=512, chunk=512):
    rows = qkv.shape[0]
    q_spec = pl.BlockSpec((block, 128), lambda j, i: (i, j))
    table = pl.BlockSpec((block, 128), lambda j, i: (i, 0))
    whole_table = pl.BlockSpec((rows, 128), lambda j, i: (0, 0))
    lead = pl.BlockSpec((16, 128), lambda j, i: (0, j))

    def whole(n):
        return pl.BlockSpec((rows, 128), lambda j, i: (0, n * PAIRS + j))

    return call(
        functools.partial(
            attend_back_kernel, chunk=chunk, count=rows // chunk, steps=rows // block
        ),
        (PAIRS, rows // block),
        [
            q_spec, q_spec, q_spec,
            pl.BlockSpec((1, 2, block), lambda j, i: (j, 0, i)),
            table, table, table,
            whole(1), whole(2), lead, lead,
            whole_table, whole_table, whole_table,
        ],
        [q_spec, whole(0), whole(0), lead, lead],
        [shape_of((rows, HALF), bf16)] * 3 + [shape_of((16, HALF), f32)] * 2,
        [
            pltpu.VMEM((128, rows), bf16),
            pltpu.VMEM((rows, 128), f32),
            pltpu.VMEM((rows, 128), f32),
            pltpu.VMEM((16, 128), f32),
            pltpu.VMEM((16, 128), f32),
        ],
        (32 * rows * rows * HALF, 10 * rows * D * 2),
        qkv, g, o, lse, *tables, qkv, qkv, k0, v0, *tables,
    )


def prompt_probs(k, qm, mask):
    s = dot_nt(k, qm) * HD ** (-0.5) + mask
    e = jnp.exp(s - jnp.max(s, 0, keepdims=True))
    return e / jnp.sum(e, 0, keepdims=True)


def cross_kernel(q_ref, k_ref, v_ref, mask_ref, o_ref):
    q = q_ref[...]
    lane = lax.broadcasted_iota(jnp.int32, q.shape, 1)
    vt = v_ref[...].T
    outs = []
    for head in range(2):
        qm = jnp.where((lane // HD) == head, q, jnp.zeros_like(q))
        p = prompt_probs(k_ref[...], qm, mask_ref[...])
        outs.append(dot_nn(vt[head * HD : (head + 1) * HD], p.astype(bf16)))
    o_ref[...] = jnp.concatenate(outs, 0).T.astype(bf16)


def cross_back_kernel(
    q_ref, g_ref, k_ref, v_ref, mask_ref, dq_ref, dk_ref, dv_ref, dka, dva, *, steps
):
    i = pl.program_id(1)

    @pl.when(i == 0)
    def _():
        dka[...] = jnp.zeros_like(dka)
        dva[...] = jnp.zeros_like(dva)

    q = q_ref[...]
    g = g_ref[...]
    lane = lax.broadcasted_iota(jnp.int32, q.shape, 1)
    kt = k_ref[...].T
    dqs = []
    for head in range(2):
        sel = (lane // HD) == head
        qm = jnp.where(sel, q, jnp.zeros_like(q))
        gm = jnp.where(sel, g, jnp.zeros_like(g))
        p = prompt_probs(k_ref[...], qm, mask_ref[...])
        dp = dot_nt(v_ref[...], gm)
        ds = (p * (dp - jnp.sum(dp * p, 0, keepdims=True)) * HD ** (-0.5)).astype(bf16)
        dva[...] += dot_nn(p.astype(bf16), gm)
        dka[...] += dot_nn(ds, qm)
        dqs.append(dot_nn(kt[head * HD : (head + 1) * HD], ds))
    dq_ref[...] = jnp.concatenate(dqs, 0).T.astype(bf16)

    @pl.when(i == steps - 1)
    def _():
        dk_ref[...] = dka[...]
        dv_ref[...] = dva[...]


def cross_specs(rows, tokens, block):
    q_spec = pl.BlockSpec((block, 128), lambda j, i: (i, j))
    key_spec = pl.BlockSpec((tokens, 128), lambda j, i: (0, j))
    value_spec = pl.BlockSpec((tokens, 128), lambda j, i: (0, PAIRS + j))
    mask_spec = pl.BlockSpec((tokens, 1), lambda j, i: (0, 0))
    return (q_spec, key_spec, value_spec, mask_spec)


def cross_forward(q, kv, mask, block=1024):
    rows, tokens = (q.shape[0], kv.shape[0])
    q_spec, key_spec, value_spec, mask_spec = cross_specs(rows, tokens, block)
    return call(
        cross_kernel,
        (PAIRS, rows // block),
        [q_spec, key_spec, value_spec, mask_spec],
        q_spec,
        shape_of((rows, HALF), bf16),
        [],
        (16 * rows * tokens * HALF, 4 * rows * D),
        q, kv, kv, mask,
    )


def cross_backward(q, g, kv, mask, block=1024):
    rows, tokens = (q.shape[0], kv.shape[0])
    q_spec, key_spec, value_spec, mask_spec = cross_specs(rows, tokens, block)
    return call(
        functools.partial(cross_back_kernel, steps=rows // block),
        (PAIRS, rows // block),
        [q_spec, q_spec, key_spec, value_spec, mask_spec],
        [q_spec, key_spec, key_spec],
        [
            shape_of((rows, HALF), bf16),
            shape_of((tokens, HALF), f32),
            shape_of((tokens, HALF), f32),
        ],
        [pltpu.VMEM((tokens, 128), f32), pltpu.VMEM((tokens, 128), f32)],
        (32 * rows * tokens * HALF, 8 * rows * D),
        q, g, kv, kv, mask,
    )


def gate_up_kernel(n_ref, wg_ref, wu_ref, hidden_ref, gate_ref, up_ref):
    n = n_ref[...]
    gate = dot_nn(n, wg_ref[...])
    up = dot_nn(n, wu_ref[...])
    hidden_ref[...] = (gate / (1.0 + jnp.exp(-gate)) * up).astype(bf16)
    gate_ref[...] = gate.astype(bf16)
    up_ref[...] = up.astype(bf16)


def gate_up(n, w, block=512, columns=512):
    rows = n.shape[0]
    count = HIDE // columns
    out = pl.BlockSpec((block, columns), lambda j, i: (i, j))
    return call(
        gate_up_kernel,
        (count, rows // block),
        [
            pl.BlockSpec((block, D), lambda j, i: (i, 0)),
            pl.BlockSpec((D, columns), lambda j, i: (0, j)),
            pl.BlockSpec((D, columns), lambda j, i: (0, count + j)),
        ],
        [out, out, out],
        [shape_of((rows, HIDE), bf16)] * 3,
        [],
        (4 * rows * D * HIDE, 8 * rows * HIDE + 4 * D * HIDE),
        n, w, w,
    )


def down_back_kernel(d_ref, w_ref, gate_ref, up_ref, dgate_ref, dup_ref):
    d = dot_nt(d_ref[...], w_ref[...])
    gate = gate_ref[...].astype(f32)
    up = up_ref[...].astype(f32)
    sig = 1.0 / (1.0 + jnp.exp(-gate))
    dgate_ref[...] = (d * up * sig * (1.0 + gate * (1.0 - sig))).astype(bf16)
    dup_ref[...] = (d * gate * sig).astype(bf16)


def down_back(d, w, gate, up, block=512, columns=512):
    rows = d.shape[0]
    out = pl.BlockSpec((block, columns), lambda j, i: (i, j))
    return call(
        down_back_kernel,
        (HIDE // columns, rows // block),
        [
            pl.BlockSpec((block, D), lambda j, i: (i, 0)),
            pl.BlockSpec((columns, D), lambda j, i: (j, 0)),
            out,
            out,
        ],
        [out, out],
        [shape_of((rows, HIDE), bf16)] * 2,
        [],
        (2 * rows * D * HIDE, 10 * rows * HIDE + 2 * D * HIDE),
        d, w, gate, up,
    )


def chip_body(
    latents, noise_draw, audio_len, bucket, timing, prompt, prompt_len, step_count,
    edge_weight, edge_first, edge_second,
    attend_weight, attend_first, attend_second,
    square_weight, square_first, square_second,
    cross_weight, cross_first, cross_second,
    upward_weight, upward_first, upward_second,
    down_weight, down_first, down_second,
    gain_weight, gain_first, gain_second,
    *, planes, chips,
):
    peers = ("seq", "z")
    many = planes * chips
    groups = latents.shape[0]
    clips = groups * 2 * planes
    frames = latents.shape[1] * chips
    own = frames // 2
    s_at, z_at, k_at = (lax.axis_index("seq"), lax.axis_index("z"), lax.axis_index("core"))
    device = (s_at * planes + z_at) * 2 + k_at
    first_core = k_at == 0

    def swap(x):
        return lax.ppermute(x, "core", [(0, 1), (1, 0)])

    def across(x, axis, size, bit):
        return lax.ppermute(x, axis, [(i, i ^ bit) for i in range(size)])

    def bits(size):
        found = []
        bit = size // 2
        while bit:
            found.append(bit)
            bit //= 2
        return found

    hops = [("z", planes, b) for b in bits(planes)] + [("seq", chips, b) for b in bits(chips)]

    def in_order(mine, other, axis=0):
        return jnp.where(
            first_core,
            jnp.concatenate([mine, other], axis),
            jnp.concatenate([other, mine], axis),
        )

    def pick(x, index, axis):
        return lax.dynamic_index_in_dim(x, index, axis, keepdims=False)

    def halves_of(x, view, axis):
        x = x.reshape(view)
        rows = view[0]
        return (
            pick(x, k_at, axis).reshape(rows, -1),
            pick(x, 1 - k_at, axis).reshape(rows, -1),
        )

    rows = attend_weight.shape[0]
    attend_view = (rows, 3, 2, HALF)
    square_view = (rows, 3, 2, HALF)
    cross_view = (cross_weight.shape[0], 2, 2, HALF)
    up_view = (rows, 2, many, 2, FF // (2 * many))
    attend16 = attend_weight.astype(bf16)
    edge16 = jnp.concatenate(
        [edge_weight[: 2 * C].astype(bf16), gain_weight.astype(bf16)], 0
    ).T
    edge16 = jnp.pad(edge16, ((0, 0), (0, 256 - edge16.shape[1])))
    mine, other = halves_of(attend16, attend_view, 2)
    mine, other = (jnp.concatenate([mine, edge16], 1), jnp.concatenate([other, edge16], 1))
    first_group = lax.all_gather(in_order(mine, swap(other)), peers, axis=0, tiled=True)
    mine, other = halves_of(
        square_weight[:3].astype(bf16).transpose(1, 0, 2), square_view, 2
    )
    square_cols = lax.all_gather(in_order(mine, swap(other)), peers, axis=0, tiled=True)
    mine, other = halves_of(cross_weight.astype(bf16), cross_view, 2)
    cross_w = lax.all_gather(in_order(mine, swap(other)), peers, axis=0, tiled=True)
    mine, other = halves_of(upward_weight.astype(bf16), up_view, 3)
    up_w = lax.all_gather(in_order(mine, swap(other)), peers, axis=0, tiled=True)
    down_w = lax.all_gather(down_weight.astype(bf16), peers, axis=0, tiled=True)

    attend_w = first_group[:, : 3 * HALF]
    w_in_t = first_group[:, 3 * HALF : 3 * HALF + C]
    w_out_t = first_group[:, 3 * HALF + C : 3 * HALF + 2 * C]
    norm_gains = first_group[:, 3 * HALF + 2 * C : 3 * HALF + 2 * C + 4].astype(f32).T

    def rows_half(columns):
        mine_rows = lax.dynamic_slice_in_dim(columns, k_at * HALF, HALF, 0)
        other_rows = lax.dynamic_slice_in_dim(columns, (1 - k_at) * HALF, HALF, 0)
        return in_order(mine_rows, swap(other_rows), 1)

    w_o = rows_half(square_cols[:, :HALF])
    w_cq = square_cols[:, HALF : 2 * HALF]
    w_co = rows_half(square_cols[:, 2 * HALF :])

    local = jnp.stack(
        [audio_len, bucket, timing[:, 0], timing[:, 1], prompt_len], 1
    ).astype(f32)
    clip_index = jnp.arange(clips)
    place = (clip_index // groups) == (z_at * 2 + k_at)
    scalars = jnp.where(place[:, None], jnp.tile(local, (clips // groups, 1)), 0.0)
    scalars = scalars + swap(scalars)
    for b in bits(planes):
        scalars = scalars + across(scalars, "z", planes, b)
    order = (z_at ^ (clip_index // chips)) * chips + (s_at ^ (clip_index % chips))
    chosen = order[:, None] == clip_index[None, :]
    scalars = jnp.sum(jnp.where(chosen[:, :, None], scalars[None], 0.0), 1)
    lengths = scalars[:, 0]
    t, keep_rates, noise_rates, clip_weights = plan(scalars[:, 1])
    weight_sum = jnp.sum(clip_weights * lengths)
    keep_rate, noise_rate, clip_weight = (keep_rates[0], noise_rates[0], clip_weights[0])

    t_feat = time_features(t).astype(bf16)
    z_feat = timing_features(scalars[:, 2:4]).astype(bf16)
    w_t1 = edge_weight[2 * C : 2 * C + TF].astype(bf16)
    w_t2 = square_weight[3].astype(bf16)
    w_timing = edge_weight[2 * C + TF :].astype(bf16)
    t_pre = dot_nn(t_feat, w_t1)
    t_hidden = jax.nn.silu(t_pre).astype(bf16)
    lead = lax.dynamic_update_slice(
        jnp.zeros((clips, D), f32), dot_nn(z_feat, w_timing), (0, device * rows)
    ) + dot_nn(t_hidden, w_t2)
    for axis, size, bit in hops:
        count = lead.shape[0] // 2
        lead = lead[:count] + across(lead[count:], axis, size, bit)
    lead = lead + swap(lead)
    prefix_normed, prefix_std, prefix_dev = layer_normalize(lead, norm_gains[0])
    n_prefix = jnp.pad(prefix_normed.astype(bf16), ((0, 15), (0, 0)))
    kv_prefix = dot_nn(n_prefix, attend_w[:, HALF:]).astype(bf16)
    k0, v0 = (kv_prefix[:, :HALF], kv_prefix[:, HALF:])

    part = s_at // groups
    member = s_at % groups
    both = jnp.stack([latents, noise_draw])
    plane = lax.all_gather(both, ("seq", "core"), axis=0, tiled=False)
    plane = plane.reshape((chips, 2) + both.shape)
    plane = pick(pick(plane, part, 1), member, 2)
    clip = plane.transpose(1, 0, 2, 3).reshape(2, frames, C)

    def mine_first(x, axis):
        return jnp.concatenate(
            [
                lax.dynamic_slice_in_dim(x, k_at * own, own, axis),
                lax.dynamic_slice_in_dim(x, (1 - k_at) * own, own, axis),
            ],
            axis,
        )

    clip = mine_first(clip, 1).astype(f32)
    clean, noisy_part = (clip[0], clip[1])
    frame = jnp.arange(frames)
    positions = jnp.where(first_core, frame, (frame + own) % frames)
    row_weight = clip_weight * (positions[:own].astype(f32) < lengths[0]).astype(f32)
    local_prompt = pick(prompt, member, 0)
    other_prompt = swap(local_prompt)
    prompt_low = jnp.where(part == k_at, local_prompt, other_prompt)
    tokens = prompt_low.shape[0]
    mask = jnp.where(
        jnp.arange(tokens)[:, None].astype(f32) < scalars[0, 4], 0.0, -1000000000.0
    ).astype(f32)

    def shared_sum(product):
        given = product(1).astype(bf16)
        return product(0) + swap(given).astype(f32)

    def cut(x, which):
        return x[which * own : (which + 1) * own]

    def both_halves(x):
        return jnp.concatenate([x, swap(x)], 0)

    x_in = (keep_rate * clean + noise_rate * noisy_part).astype(bf16)
    h0 = dot_nt(x_in, w_in_t)
    n1 = layer_normalize(h0, norm_gains[0])[0].astype(bf16)
    h0 = h0[:own]
    tables = turn_tables(positions + 1)
    qkv = qkv_project(n1, first_group, tables)
    o, lse = attend_forward(qkv, k0, v0)
    h1 = h0 + shared_sum(lambda i: dot_nn(cut(o, i), w_o))
    n2 = both_halves(layer_normalize(h1, norm_gains[1])[0].astype(bf16))
    cross_q = dot_nn(n2, w_cq).astype(bf16)
    cross_kv = dot_nn(prompt_low, cross_w).astype(bf16)
    co = cross_forward(cross_q, cross_kv, mask)
    h2 = h1 + shared_sum(lambda i: dot_nn(cut(co, i), w_co))
    n3 = both_halves(layer_normalize(h2, norm_gains[2])[0].astype(bf16))
    hidden, gate, upper = gate_up(n3, up_w)
    h3 = h2 + shared_sum(lambda i: dot_nn(cut(hidden, i), down_w))
    n4, std4, dev4 = layer_normalize(h3, norm_gains[3])
    n4 = n4.astype(bf16)
    predicted = dot_nn(n4, w_out_t)
    target = keep_rate * noisy_part[:own] - noise_rate * clean[:own]
    error = predicted - target
    loss_local = jnp.sum(row_weight[:, None] * error * error)

    d_pred = (2.0 / (C * weight_sum) * row_weight[:, None] * error).astype(bf16)
    g_out_t = dot_tn(n4, d_pred)
    d_h, gain4 = norm_backward(dot_nt(d_pred, w_out_t), std4, dev4, norm_gains[3])
    d_f = both_halves(d_h.astype(bf16))

    def scattered(g):
        return lax.psum_scatter(g.astype(bf16), peers, scatter_dimension=0, tiled=True)

    s_down = scattered(dot_tn(hidden, d_f))
    d_gate, d_up = down_back(d_f, down_w, gate, upper)
    s_gate = scattered(dot_tn(n3, d_gate))
    s_upper = scattered(dot_tn(n3, d_up))
    d_n3 = shared_sum(
        lambda i: dot_nt(cut(d_gate, i), up_w[:, :HIDE]) + dot_nt(cut(d_up, i), up_w[:, HIDE:])
    )

    def norm_again(d_n, h, gain):
        _, std, dev = layer_normalize(h, gain)
        return norm_backward(d_n, std, dev, gain)

    d_part, gain3 = norm_again(d_n3, h2, norm_gains[2])
    d_h = d_h + d_part
    d_c = both_halves(d_h.astype(bf16))
    g_co = dot_tn(co, d_c).astype(bf16)
    d_co = dot_nt(d_c, w_co).astype(bf16)
    d_cq, d_ck, d_cv = cross_backward(cross_q, d_co, cross_kv, mask)
    g_cross = dot_tn(prompt_low, jnp.concatenate([d_ck, d_cv], 1).astype(bf16))
    s_cross = scattered(g_cross)
    g_cq = dot_tn(n2, d_cq).astype(bf16)
    d_n2 = shared_sum(lambda i: dot_nt(cut(d_cq, i), w_cq))
    d_part, gain2 = norm_again(d_n2, h1, norm_gains[1])
    d_h = d_h + d_part
    d_a = both_halves(d_h.astype(bf16))
    g_o = dot_tn(o, d_a).astype(bf16)

    def columns_half(g):
        kept = lax.dynamic_slice_in_dim(g, k_at * HALF, HALF, 1)
        given = lax.dynamic_slice_in_dim(g, (1 - k_at) * HALF, HALF, 1)
        return in_order(kept, swap(given), 0)

    s_square = scattered(jnp.concatenate([columns_half(g_o), g_cq, columns_half(g_co)], 1))
    d_o = dot_nt(d_a, w_o).astype(bf16)
    d_q, d_k, d_v, d_k0, d_v0 = attend_backward(qkv, d_o, o, lse, k0, v0, tables)
    d_projected = jnp.concatenate([d_q, d_k, d_v], 1)
    d_kv0 = jnp.concatenate([d_k0, d_v0], 1)
    extra = n_prefix[0].astype(f32)[:, None] * jnp.pad(d_kv0[0], (HALF, 0))[None, :]
    s_attend = scattered(dot_tn(n1, d_projected) + extra)
    d_n1 = shared_sum(lambda i: dot_nt(cut(d_projected, i), attend_w))
    d_part, gain1 = norm_again(d_n1, h0, norm_gains[0])
    d_h = d_h + d_part
    g_in_t = dot_tn(d_h.astype(bf16), x_in[:own])

    high = d_kv0.astype(bf16)
    rest = (d_kv0 - high.astype(f32)).astype(bf16)
    d_np = dot_nt(jnp.concatenate([high, rest], 0), attend_w[:, HALF:])
    d_np = d_np[:1] + d_np[16:17]
    d_np = d_np + swap(d_np)
    d_lead, prefix_gain = norm_backward(d_np, prefix_std, prefix_dev, norm_gains[0])
    for axis, size, bit in reversed(hops):
        d_lead = jnp.concatenate([d_lead, across(d_lead, axis, size, bit)], 0)
    g_t2 = exact("ge,gd->ed", t_hidden.astype(f32), d_lead)
    d_lead_here = lax.dynamic_slice(d_lead, (0, device * rows), (clips, rows))
    g_timing = exact("gz,gd->zd", z_feat.astype(f32), d_lead_here)
    d_t_hidden = exact("gd,ed->ge", d_lead, w_t2.astype(f32))
    t_sig = jax.nn.sigmoid(t_pre)
    d_t_pre = d_t_hidden * t_sig * (1.0 + t_pre * (1.0 - t_sig))
    g_t1 = exact("gz,gd->zd", t_feat.astype(f32), d_t_pre)

    gains = jnp.stack([gain1 + 0.5 * prefix_gain, gain2, gain3, gain4], 1)
    s_edge = lax.psum_scatter(
        jnp.concatenate([g_in_t, g_out_t, gains], 1),
        ("seq", "z", "core"),
        scatter_dimension=0,
        tiled=True,
    )

    def to_owner(x, view, axis):
        count = x.shape[0] // 2
        kept = lax.dynamic_slice_in_dim(x, k_at * count, count, 0)
        given = lax.dynamic_slice_in_dim(x, (1 - k_at) * count, count, 0)
        taken = swap(given)
        shape = view[:axis] + view[axis + 1 :]
        joined = jnp.where(
            first_core,
            jnp.stack([kept.reshape(shape), taken.reshape(shape)], axis),
            jnp.stack([taken.reshape(shape), kept.reshape(shape)], axis),
        )
        return joined.astype(f32)

    g_attend = to_owner(s_attend, attend_view, 2).reshape(rows, 3 * D)
    g_square = to_owner(s_square, square_view, 2).reshape(rows, 3, D).transpose(1, 0, 2)
    g_square = jnp.concatenate([g_square, g_t2[None]], 0)
    g_cross = to_owner(s_cross, cross_view, 2).reshape(cross_view[0], 2 * D)
    g_up = to_owner(jnp.concatenate([s_gate, s_upper], 1), up_view, 3).reshape(rows, 2 * FF)
    g_down = s_down.astype(f32)
    g_edge = jnp.concatenate([s_edge[:, : 2 * C].T, g_t1, g_timing], 0)
    g_gain = s_edge[:, 2 * C :].T
    sharded = (g_edge, g_attend, g_square, g_cross, g_up, g_down, g_gain)
    totals = jnp.stack([sum(jnp.sum(g * g) for g in sharded), loss_local])
    totals = totals + swap(totals)
    for axis, size, bit in hops:
        totals = totals + across(totals, axis, size, bit)
    grad_norm = jnp.sqrt(totals[0])
    loss_value = totals[1] / (C * weight_sum)
    factor = jnp.minimum(1.0, clip_norm / grad_norm)
    count = step_count[0].astype(f32)
    first_fix = 1.0 - 0.9**count
    second_fix = 1.0 - 0.999**count
    states = (
        (edge_weight, edge_first, edge_second),
        (attend_weight, attend_first, attend_second),
        (square_weight, square_first, square_second),
        (cross_weight, cross_first, cross_second),
        (upward_weight, upward_first, upward_second),
        (down_weight, down_first, down_second),
        (gain_weight, gain_first, gain_second),
    )
    out = [
        adam(w, m, v, g * factor, first_fix, second_fix)
        for (w, m, v), g in zip(states, sharded)
    ]
    flat = [x for triple in out[:6] for x in triple]
    return (loss_value, grad_norm, *flat, g_gain * factor, out[6][1], out[6][2])


def solution(mesh):
    chips, spread = (mesh.shape["seq"], mesh.shape["dp"])
    split_mesh = Mesh(mesh.devices.reshape(chips, spread // 2, 2), ("seq", "z", "core"))

    def whole(*args):
        groups = args[0].shape[0] // spread
        one_clip_per_chip = groups * 2 == chips and chips & (chips - 1) == 0
        if one_clip_per_chip:
            inner = functools.partial(chip_body, planes=spread // 2, chips=chips)
            dp, used = ("z", "core"), split_mesh
        else:
            inner, dp, used = (general_body, "dp", mesh)
        every = ("seq",) + (dp if isinstance(dp, tuple) else (dp,))
        by_row, by_column, by_middle = (P(every, None), P(None, every), P(None, every, None))
        frames = P(dp, "seq", None)
        clip = P(dp)
        kinds = (by_column, by_row, by_middle, by_row, by_row, by_row, by_column)
        weights = tuple(kind for kind in kinds for _ in range(3))
        return jax.shard_map(
            inner,
            mesh=used,
            in_specs=(frames, frames, clip, clip, P(dp, None), P(dp, None, None), clip, P())
            + weights,
            out_specs=(P(), P()) + weights,
            check_vma=False,
        )(*args)

    return whole
```

```python
import functools
import math

import jax
import jax.numpy as jnp
from jax import lax
from jax.experimental import pallas as pl
from jax.experimental.pallas import tpu as pltpu
from jax.sharding import Mesh
from jax.sharding import PartitionSpec as P

D = 1536
H = 24
HD = 64
FF = 6144
C = 64
TF = 256
PT = 128
NB = 1000


highest = lax.Precision.HIGHEST
clip_norm = 0.002
learn_rate = 0.1
weight_decay = 0.1
rot_width = 32


def layer_normalize(h, norm_gain):
    centered_input = h - jnp.mean(h, -1, keepdims=True)
    inverse_deviation = lax.rsqrt(
        jnp.mean(centered_input * centered_input, -1, keepdims=True) + 1e-05
    )
    standardized = centered_input * inverse_deviation
    return (standardized * norm_gain, standardized, inverse_deviation)


def norm_backward(incoming_gradient, standardized, inverse_deviation, norm_gain):
    scaled_gradient = incoming_gradient * norm_gain
    gain_gradient = jnp.sum(incoming_gradient * standardized, 0)
    d_in = inverse_deviation * (
        scaled_gradient
        - jnp.mean(scaled_gradient, -1, keepdims=True)
        - standardized * jnp.mean(scaled_gradient * standardized, -1, keepdims=True)
    )
    return (d_in, gain_gradient)


def plan(bucket):
    t = (bucket.astype(jnp.float32) + 0.5) / NB
    keep_rate = jnp.cos(t * (math.pi / 2))
    noise_rate = jnp.sin(t * (math.pi / 2))
    snr_ratio = keep_rate * keep_rate / (noise_rate * noise_rate)
    return (t, keep_rate, noise_rate, jnp.minimum(snr_ratio, 5.0) / (snr_ratio + 1.0))


def time_features(t):
    freqs = jnp.exp(-math.log(10000.0) * jnp.arange(TF // 2, dtype=jnp.float32) / (TF // 2))
    angle = t[:, None] * 1000.0 * freqs[None, :]
    return jnp.concatenate([jnp.cos(angle), jnp.sin(angle)], -1)


def timing_features(timing):
    seconds = timing.astype(jnp.float32) / 64.0
    return jnp.concatenate([time_features(seconds[:, 0]), time_features(seconds[:, 1])], -1)


def rope_tables(positions):
    inverse = 10000.0 ** (-2.0 * jnp.arange(rot_width // 2, dtype=jnp.float32) / rot_width)
    angle = positions[:, None].astype(jnp.float32) * inverse[None, :]
    angle = jnp.concatenate([angle, angle], -1)
    return (jnp.cos(angle), jnp.sin(angle))


def rotate(x):
    half = rot_width // 2
    return jnp.concatenate([-x[..., half:], x[..., :half]], -1)


def apply_rope(x, cosine, sine_part):
    turned = x[..., :rot_width]
    turned = turned * cosine[None, :, None, :] + rotate(turned) * sine_part[None, :, None, :]
    return jnp.concatenate([turned, x[..., rot_width:]], -1)


def rope_back(incoming_gradient, cosine, sine_part):
    turned = incoming_gradient[..., :rot_width]
    turned = turned * cosine[None, :, None, :] - rotate(turned * sine_part[None, :, None, :])
    return jnp.concatenate([turned, incoming_gradient[..., rot_width:]], -1)


def split_blocks(x, count, block):
    return x.reshape((x.shape[0], count, block) + x.shape[2:]).swapaxes(0, 1)


def join_blocks(x):
    x = x.swapaxes(0, 1)
    return x.reshape((x.shape[0], x.shape[1] * x.shape[2]) + x.shape[3:])


def attend(q, keys, values):
    rows_q = q.shape[1]
    block = min(512, rows_q)
    count = rows_q // block
    score_scale = HD ** (-0.5)

    def one_block(q_block):
        s = (
            jnp.einsum("ibd,ikd->ibk", q_block, keys, preferred_element_type=jnp.float32)
            * score_scale
        )
        top = jnp.max(s, -1, keepdims=True)
        lse = top + jnp.log(jnp.sum(jnp.exp(s - top), -1, keepdims=True))
        p = jnp.exp(s - lse)
        o = jnp.einsum(
            "ibk,ikd->ibd", p.astype(jnp.bfloat16), values, preferred_element_type=jnp.float32
        )
        return (o, lse[..., 0])

    outs, lses = lax.map(one_block, split_blocks(q, count, block))
    return (join_blocks(outs), join_blocks(lses))


def attend_back(q, keys, values, lse, grad_o):
    rows_q = q.shape[1]
    block = min(512, rows_q)
    count = rows_q // block
    score_scale = HD ** (-0.5)

    def one_block(carry, parts):
        d_key, d_value = carry
        q_block, g_block, l_block = parts
        s = (
            jnp.einsum("ibd,ikd->ibk", q_block, keys, preferred_element_type=jnp.float32)
            * score_scale
        )
        p = jnp.exp(s - l_block[..., None])
        d_prob = jnp.einsum("ibd,ikd->ibk", g_block, values, preferred_element_type=jnp.float32)
        d_value = d_value + jnp.einsum(
            "ibk,ibd->ikd", p.astype(jnp.bfloat16), g_block, preferred_element_type=jnp.float32
        )
        d_score = (p * (d_prob - jnp.sum(d_prob * p, -1, keepdims=True)) * score_scale).astype(
            jnp.bfloat16
        )
        d_query = jnp.einsum("ibk,ikd->ibd", d_score, keys, preferred_element_type=jnp.float32)
        d_key = d_key + jnp.einsum(
            "ibk,ibd->ikd", d_score, q_block, preferred_element_type=jnp.float32
        )
        return ((d_key, d_value), d_query)

    zeros = jnp.zeros(keys.shape, jnp.float32)
    parts = (
        split_blocks(q, count, block),
        split_blocks(grad_o, count, block),
        split_blocks(lse, count, block),
    )
    (d_key, d_value), d_queries = lax.scan(one_block, (zeros, zeros), parts)
    return (join_blocks(d_queries), d_key, d_value)


def adam(w, m, v, g, first_fix, second_fix):
    first = 0.9 * m + 0.1 * g
    second = 0.999 * v + 0.001 * g * g
    new = w - learn_rate * (
        first / first_fix / (jnp.sqrt(second / second_fix) + 1e-08) + weight_decay * w
    )
    return (new, first, second)


def exact(form, a, b):
    return jnp.einsum(form, a, b, precision=highest, preferred_element_type=jnp.float32)


def general_body(
    latents,
    noise_draw,
    audio_len,
    bucket,
    timing,
    prompt,
    prompt_len,
    step_count,
    edge_weight,
    edge_first,
    edge_second,
    attend_weight,
    attend_first,
    attend_second,
    square_weight,
    square_first,
    square_second,
    cross_weight,
    cross_first,
    cross_second,
    upward_weight,
    upward_first,
    upward_second,
    down_weight,
    down_first,
    down_second,
    gain_weight,
    gain_first,
    gain_second,
):
    low_type = jnp.bfloat16
    wide = jnp.float32
    groups, frames = (latents.shape[0], latents.shape[1])
    total_rows = groups * frames
    items = groups * H
    edge16, attend16, square16, cross16, upward16, down16, gain16 = (
        lax.all_gather(edge_weight.astype(low_type), ("seq", "dp"), axis=1, tiled=True),
        lax.all_gather(attend_weight.astype(low_type), ("seq", "dp"), axis=0, tiled=True),
        lax.all_gather(square_weight.astype(low_type), ("seq", "dp"), axis=1, tiled=True),
        lax.all_gather(cross_weight.astype(low_type), ("seq", "dp"), axis=0, tiled=True),
        lax.all_gather(upward_weight.astype(low_type), ("seq", "dp"), axis=0, tiled=True),
        lax.all_gather(down_weight.astype(low_type), ("seq", "dp"), axis=0, tiled=True),
        lax.all_gather(gain_weight.astype(low_type), ("seq", "dp"), axis=1, tiled=True),
    )
    norm_gains = gain16.astype(wide)
    positions = lax.axis_index("seq") * frames + jnp.arange(frames, dtype=jnp.int32)
    t, keep_rate, noise_rate, clip_weight = plan(bucket)
    frame_mask = (positions[None, :] < audio_len[:, None]).astype(wide)
    row_weight = (clip_weight[:, None] * frame_mask).reshape(total_rows)
    weight_sum = lax.psum(jnp.sum(row_weight), ("seq", "dp"))
    clean = latents.astype(wide)
    noisy_part = noise_draw.astype(wide)
    x_in = (
        (keep_rate[:, None, None] * clean + noise_rate[:, None, None] * noisy_part)
        .astype(low_type)
        .reshape(total_rows, C)
    )
    t_feat = time_features(t).astype(low_type)
    z_feat = timing_features(timing).astype(low_type)
    t_pre = jnp.dot(t_feat, edge16[2 * C : 2 * C + TF], preferred_element_type=wide)
    t_hidden = jax.nn.silu(t_pre).astype(low_type)
    leading_token = jnp.dot(t_hidden, square16[3], preferred_element_type=wide) + jnp.dot(
        z_feat, edge16[2 * C + TF :], preferred_element_type=wide
    )
    prefix_normed, prefix_standardized, prefix_inverse_deviation = layer_normalize(
        leading_token, norm_gains[0]
    )
    n_prefix_low = prefix_normed.astype(low_type)
    kv_prefix = jnp.dot(n_prefix_low, attend16[:, D:], preferred_element_type=wide).astype(low_type)
    k_prefix = kv_prefix[:, :D].reshape(items, 1, HD)
    v_prefix = kv_prefix[:, D:].reshape(items, 1, HD)
    hidden_start = jnp.dot(x_in, edge16[:C], preferred_element_type=wide)
    first_normed, first_standardized, first_inverse_deviation = layer_normalize(
        hidden_start, norm_gains[0]
    )
    n1_low = first_normed.astype(low_type)
    projected = jnp.dot(n1_low, attend16, preferred_element_type=wide).reshape(
        groups, frames, 3, H, HD
    )
    cosine, sine_part = rope_tables(positions + 1)
    rotated = jnp.stack(
        [
            apply_rope(projected[:, :, 0], cosine, sine_part),
            apply_rope(projected[:, :, 1], cosine, sine_part),
            projected[:, :, 2],
        ]
    ).astype(low_type)
    as_items = rotated.transpose(0, 1, 3, 2, 4).reshape(3, items, frames, HD)
    q_use = as_items[0]
    key_value = lax.all_gather(as_items[1:], "seq", axis=2, tiled=True)
    keys = jnp.concatenate([k_prefix, key_value[0]], 1)
    values = jnp.concatenate([v_prefix, key_value[1]], 1)
    o_items, lse = attend(q_use, keys, values)
    o_local = o_items.astype(low_type)
    o_low = o_local.reshape(groups, H, frames, HD).transpose(0, 2, 1, 3).reshape(total_rows, D)
    hidden_after_self = hidden_start + jnp.dot(o_low, square16[0], preferred_element_type=wide)
    second_normed, second_standardized, second_inverse_deviation = layer_normalize(
        hidden_after_self, norm_gains[1]
    )
    n2_low = second_normed.astype(low_type)
    cross_q = (
        jnp.dot(n2_low, square16[1], preferred_element_type=wide)
        .astype(low_type)
        .reshape(groups, frames, H, HD)
    )
    cross_kv = jnp.einsum("gpc,ce->gpe", prompt, cross16, preferred_element_type=wide).astype(
        low_type
    )
    cross_k = cross_kv[..., :D].reshape(groups, PT, H, HD)
    cross_v = cross_kv[..., D:].reshape(groups, PT, H, HD)
    key_mask = jnp.arange(PT)[None, :] < prompt_len[:, None]
    score_scale = HD ** (-0.5)
    scores = (
        jnp.einsum("gfhd,gphd->ghfp", cross_q, cross_k, preferred_element_type=wide) * score_scale
    )
    scores = jnp.where(key_mask[:, None, None, :], scores, -1000000000.0)
    probs = jax.nn.softmax(scores, -1)
    probs_low = probs.astype(low_type)
    co_low = (
        jnp.einsum("ghfp,gphd->gfhd", probs_low, cross_v, preferred_element_type=wide)
        .astype(low_type)
        .reshape(total_rows, D)
    )
    hidden_after_cross = hidden_after_self + jnp.dot(
        co_low, square16[2], preferred_element_type=wide
    )
    third_normed, third_standardized, third_inverse_deviation = layer_normalize(
        hidden_after_cross, norm_gains[2]
    )
    n3_low = third_normed.astype(low_type)
    gate_up = jnp.dot(n3_low, upward16, preferred_element_type=wide)
    gate, upper = (gate_up[:, :FF], gate_up[:, FF:])
    hidden = (jax.nn.silu(gate) * upper).astype(low_type)
    hidden_after_feed = hidden_after_cross + jnp.dot(hidden, down16, preferred_element_type=wide)
    fourth_normed, fourth_standardized, fourth_inverse_deviation = layer_normalize(
        hidden_after_feed, norm_gains[3]
    )
    n4_low = fourth_normed.astype(low_type)
    predicted = jnp.einsum("rd,cd->rc", n4_low, edge16[C : 2 * C], preferred_element_type=wide)
    target = (keep_rate[:, None, None] * noisy_part - noise_rate[:, None, None] * clean).reshape(
        total_rows, C
    )
    error = predicted - target
    loss_local = jnp.sum(row_weight[:, None] * error * error)
    d_pred = (2.0 / (C * weight_sum) * row_weight[:, None] * error).astype(low_type)
    g_out = jnp.einsum("rc,rd->cd", d_pred, n4_low, preferred_element_type=wide)
    fourth_norm_gradient = jnp.dot(d_pred, edge16[C : 2 * C], preferred_element_type=wide)
    hidden_gradient, fourth_gain_gradient = norm_backward(
        fourth_norm_gradient, fourth_standardized, fourth_inverse_deviation, norm_gains[3]
    )
    d_f = hidden_gradient.astype(low_type)
    g_down = jnp.einsum("rf,rd->fd", hidden, d_f, preferred_element_type=wide)
    d_hidden = jnp.einsum("rd,fd->rf", d_f, down16, preferred_element_type=wide)
    sig = jax.nn.sigmoid(gate)
    d_gate_up = jnp.concatenate(
        [d_hidden * upper * sig * (1.0 + gate * (1.0 - sig)), d_hidden * gate * sig], -1
    ).astype(low_type)
    g_up = jnp.einsum("rd,re->de", n3_low, d_gate_up, preferred_element_type=wide)
    third_norm_gradient = jnp.einsum("re,de->rd", d_gate_up, upward16, preferred_element_type=wide)
    partial_gradient, third_gain_gradient = norm_backward(
        third_norm_gradient, third_standardized, third_inverse_deviation, norm_gains[2]
    )
    hidden_gradient = hidden_gradient + partial_gradient
    d_c = hidden_gradient.astype(low_type)
    g_co = jnp.einsum("rd,re->de", co_low, d_c, preferred_element_type=wide)
    d_co = (
        jnp.einsum("re,de->rd", d_c, square16[2], preferred_element_type=wide)
        .astype(low_type)
        .reshape(groups, frames, H, HD)
    )
    d_prob = jnp.einsum("gfhd,gphd->ghfp", d_co, cross_v, preferred_element_type=wide)
    d_cv = jnp.einsum("ghfp,gfhd->gphd", probs_low, d_co, preferred_element_type=wide)
    d_score = (probs * (d_prob - jnp.sum(d_prob * probs, -1, keepdims=True)) * score_scale).astype(
        low_type
    )
    d_cq = (
        jnp.einsum("ghfp,gphd->gfhd", d_score, cross_k, preferred_element_type=wide)
        .astype(low_type)
        .reshape(total_rows, D)
    )
    d_ck = jnp.einsum("ghfp,gfhd->gphd", d_score, cross_q, preferred_element_type=wide)
    d_cross_kv = jnp.concatenate([d_ck.reshape(groups, PT, D), d_cv.reshape(groups, PT, D)], -1)
    g_cross = exact("gpc,gpe->ce", prompt.astype(wide), d_cross_kv)
    g_cq = jnp.einsum("rd,re->de", n2_low, d_cq, preferred_element_type=wide)
    second_norm_gradient = jnp.einsum("re,de->rd", d_cq, square16[1], preferred_element_type=wide)
    partial_gradient, second_gain_gradient = norm_backward(
        second_norm_gradient, second_standardized, second_inverse_deviation, norm_gains[1]
    )
    hidden_gradient = hidden_gradient + partial_gradient
    d_a = hidden_gradient.astype(low_type)
    g_o = jnp.einsum("rd,re->de", o_low, d_a, preferred_element_type=wide)
    d_o = jnp.einsum("re,de->rd", d_a, square16[0], preferred_element_type=wide).astype(low_type)
    d_o_items = d_o.reshape(groups, frames, H, HD).transpose(0, 2, 1, 3).reshape(items, frames, HD)
    d_query, d_key, d_value = attend_back(q_use, keys, values, lse, d_o_items)
    summed_key, summed_value = (
        lax.psum_scatter(
            d_key[:, 1:].astype(jnp.bfloat16), "seq", scatter_dimension=1, tiled=True
        ).astype(jnp.float32),
        lax.psum_scatter(
            d_value[:, 1:].astype(jnp.bfloat16), "seq", scatter_dimension=1, tiled=True
        ).astype(jnp.float32),
    )
    d_items = jnp.stack(
        [d_query.astype(low_type), summed_key.astype(low_type), summed_value.astype(low_type)]
    )
    d_key_prefix = d_key[:, :1]
    d_value_prefix = d_value[:, :1]
    d_rot = d_items.astype(wide).reshape(3, groups, H, frames, HD).transpose(1, 3, 0, 2, 4)
    d_projected = (
        jnp.stack(
            [
                rope_back(d_rot[:, :, 0], cosine, sine_part),
                rope_back(d_rot[:, :, 1], cosine, sine_part),
                d_rot[:, :, 2],
            ],
            2,
        )
        .reshape(total_rows, 3 * D)
        .astype(low_type)
    )
    g_attend = jnp.einsum("rd,re->de", n1_low, d_projected, preferred_element_type=wide)
    first_norm_gradient = jnp.einsum(
        "re,de->rd", d_projected, attend16, preferred_element_type=wide
    )
    partial_gradient, first_gain_gradient = norm_backward(
        first_norm_gradient, first_standardized, first_inverse_deviation, norm_gains[0]
    )
    hidden_gradient = hidden_gradient + partial_gradient
    g_in = jnp.einsum(
        "rc,rd->cd", x_in, hidden_gradient.astype(low_type), preferred_element_type=wide
    )
    d_kv_prefix = jnp.concatenate(
        [d_key_prefix.reshape(groups, D), d_value_prefix.reshape(groups, D)], -1
    )
    attend_kv = attend16[:, D:].astype(wide)
    g_attend = g_attend.at[:, D:].add(exact("gd,ge->de", n_prefix_low.astype(wide), d_kv_prefix))
    prefix_norm_gradient = exact("ge,de->gd", d_kv_prefix, attend_kv)
    leading_token_gradient, prefix_gain_gradient = norm_backward(
        prefix_norm_gradient, prefix_standardized, prefix_inverse_deviation, norm_gains[0]
    )
    g_timing = exact("gz,gd->zd", z_feat.astype(wide), leading_token_gradient)
    g_t2 = exact("ge,gd->ed", t_hidden.astype(wide), leading_token_gradient)
    d_t_hidden = exact("gd,ed->ge", leading_token_gradient, square16[3].astype(wide))
    t_sig = jax.nn.sigmoid(t_pre)
    d_t_pre = d_t_hidden * t_sig * (1.0 + t_pre * (1.0 - t_sig))
    g_t1 = exact("gz,gd->zd", t_feat.astype(wide), d_t_pre)
    g_edge = jnp.concatenate([g_in, g_out, g_t1, g_timing], 0)
    g_square = jnp.stack([g_o, g_cq, g_co, g_t2])
    g_gain = jnp.stack(
        [
            first_gain_gradient + prefix_gain_gradient,
            second_gain_gradient,
            third_gain_gradient,
            fourth_gain_gradient,
        ]
    )
    sharded = (
        lax.psum_scatter(g_edge, ("seq", "dp"), scatter_dimension=1, tiled=True),
        lax.psum_scatter(g_attend, ("seq", "dp"), scatter_dimension=0, tiled=True),
        lax.psum_scatter(g_square, ("seq", "dp"), scatter_dimension=1, tiled=True),
        lax.psum_scatter(g_cross, ("seq", "dp"), scatter_dimension=0, tiled=True),
        lax.psum_scatter(g_up, ("seq", "dp"), scatter_dimension=0, tiled=True),
        lax.psum_scatter(g_down, ("seq", "dp"), scatter_dimension=0, tiled=True),
        lax.psum_scatter(g_gain, ("seq", "dp"), scatter_dimension=1, tiled=True),
    )
    square_local = sum((jnp.sum(g * g) for g in sharded))
    square_total, loss_total = lax.psum((square_local, loss_local), ("seq", "dp"))
    grad_norm = jnp.sqrt(square_total)
    loss_value = loss_total / (C * weight_sum)
    factor = jnp.minimum(1.0, clip_norm / grad_norm)
    count = step_count[0].astype(wide)
    first_fix = 1.0 - 0.9**count
    second_fix = 1.0 - 0.999**count
    weights = (
        edge_weight,
        attend_weight,
        square_weight,
        cross_weight,
        upward_weight,
        down_weight,
        gain_weight,
    )
    firsts = (
        edge_first,
        attend_first,
        square_first,
        cross_first,
        upward_first,
        down_first,
        gain_first,
    )
    seconds = (
        edge_second,
        attend_second,
        square_second,
        cross_second,
        upward_second,
        down_second,
        gain_second,
    )
    out = [
        adam(w, m, v, g * factor, first_fix, second_fix)
        for w, m, v, g in zip(weights, firsts, seconds, sharded)
    ]
    return (
        loss_value,
        grad_norm,
        out[0][0],
        out[0][1],
        out[0][2],
        out[1][0],
        out[1][1],
        out[1][2],
        out[2][0],
        out[2][1],
        out[2][2],
        out[3][0],
        out[3][1],
        out[3][2],
        out[4][0],
        out[4][1],
        out[4][2],
        out[5][0],
        out[5][1],
        out[5][2],
        sharded[6] * factor,
        out[6][1],
        out[6][2],
    )


f32 = jnp.float32
bf16 = jnp.bfloat16
HALF = D // 2
PAIRS = HALF // 128
TRIO = PAIRS // 2
THIRD = HALF // 2
HIDE = FF // 2
CROSS = 768


def dot_nt(a, b):
    return lax.dot_general(a, b, (((1,), (1,)), ((), ())), preferred_element_type=f32)


def dot_nn(a, b):
    return lax.dot_general(a, b, (((1,), (0,)), ((), ())), preferred_element_type=f32)


def dot_tn(a, b):
    return lax.dot_general(a, b, (((0,), (0,)), ((), ())), preferred_element_type=f32)


def call(kernel, grid, in_specs, out_specs, out_shape, scratch, cost, *operands):
    return pl.pallas_call(
        kernel,
        grid=grid,
        in_specs=in_specs,
        out_specs=out_specs,
        out_shape=out_shape,
        scratch_shapes=scratch,
        cost_estimate=pl.CostEstimate(flops=cost[0], bytes_accessed=cost[1], transcendentals=0),
        compiler_params=pltpu.CompilerParams(vmem_limit_bytes=60 << 20),
    )(*operands)


def shape_of(shape, kind):
    return jax.ShapeDtypeStruct(shape, kind)


def turn(y, cosine, sine_up, sine_down):
    return y * cosine + pltpu.roll(y, 16, 1) * sine_up + pltpu.roll(y, 112, 1) * sine_down


def turn_tables(positions):
    lane = jnp.arange(128) % HD
    inverse = 10000.0 ** (-2.0 * jnp.arange(rot_width // 2, dtype=f32) / rot_width)
    angle = positions[:, None].astype(f32) * inverse[None, :]
    wide_angle = jnp.tile(angle, (1, 128 // (rot_width // 2)))
    cosine = jnp.where(lane[None, :] < rot_width, jnp.cos(wide_angle), 1.0)
    sine = jnp.sin(wide_angle)
    second = (lane[None, :] >= rot_width // 2) & (lane[None, :] < rot_width)
    sine_up = jnp.where(second, sine, 0.0)
    sine_down = jnp.where(lane[None, :] < rot_width // 2, -sine, 0.0)
    return (cosine, sine_up, sine_down)


def start_kernel(x_ref, w_ref, gain_ref, h_ref, n_ref, *, own):
    h = dot_nt(x_ref[...], w_ref[...])
    n_ref[...] = layer_normalize(h, gain_ref[...])[0].astype(bf16)

    @pl.when(pl.program_id(0) < own)
    def _():
        h_ref[...] = h


def start_forward(x, w, gain, block=256):
    rows = x.shape[0]
    own = rows // 2 // block
    return call(
        functools.partial(start_kernel, own=own),
        (rows // block,),
        [
            pl.BlockSpec((block, 128), lambda i: (i, 0)),
            pl.BlockSpec((D, 128), lambda i: (0, 3 * PAIRS)),
            pl.BlockSpec((1, D), lambda i: (0, 0)),
        ],
        [
            pl.BlockSpec((block, D), lambda i: (jnp.minimum(i, own - 1), 0)),
            pl.BlockSpec((block, D), lambda i: (i, 0)),
        ],
        [shape_of((rows // 2, D), f32), shape_of((rows, D), bf16)],
        [],
        (2 * rows * D * 128, 4 * rows * D),
        x, w, gain,
    )


def qkv_kernel(n_ref, w_ref, cos_ref, up_ref, down_ref, out_ref):
    part = pl.program_id(0) % 3
    y = dot_nn(n_ref[...], w_ref[...])

    @pl.when(part < 2)
    def _():
        scale = jnp.where(part == 0, HD ** (-0.5), 1.0)
        for j in range(TRIO):
            block = y[:, j * 128 : (j + 1) * 128]
            turned = turn(block, cos_ref[...], up_ref[...], down_ref[...])
            out_ref[:, j * 128 : (j + 1) * 128] = (turned * scale).astype(bf16)

    @pl.when(part == 2)
    def _():
        out_ref[...] = y.astype(bf16)


def qkv_project(n, w, tables, block=1024):
    rows = n.shape[0]
    table = pl.BlockSpec((block, 128), lambda p, i: (i, 0))
    return call(
        qkv_kernel,
        (6, rows // block),
        [
            pl.BlockSpec((block, D), lambda p, i: (i, 0)),
            pl.BlockSpec((D, THIRD), lambda p, i: (0, p)),
            table,
            table,
            table,
        ],
        pl.BlockSpec((block, THIRD), lambda p, i: (i, p)),
        shape_of((rows, 3 * HALF), bf16),
        [],
        (2 * rows * D * 3 * HALF, 4 * rows * D * 2),
        n,
        w,
        *tables,
    )


def attend_kernel(q_ref, k_ref, v_ref, k0_ref, v0_ref, o_ref, lse_ref, *, chunk, count):
    q = q_ref[...]
    rows = q.shape[0]
    lane = lax.broadcasted_iota(jnp.int32, q.shape, 1)
    k0 = k0_ref[0:1].astype(f32)
    v0 = v0_ref[0:1].astype(f32)
    outs = []
    for head in range(2):
        mine = jnp.where((lane // HD) == head, q, jnp.zeros_like(q))
        top = jnp.sum(mine.astype(f32) * k0, 1, keepdims=True)
        total = jnp.ones_like(top)
        acc = jnp.broadcast_to(v0, (rows, 128))
        for c in range(count):
            s = dot_nt(mine, k_ref[c * chunk : (c + 1) * chunk])
            new_top = jnp.maximum(top, jnp.max(s, 1, keepdims=True))
            fade = jnp.exp(top - new_top)
            p = jnp.exp(s - new_top)
            total = total * fade + jnp.sum(p, 1, keepdims=True)
            acc = acc * fade + dot_nn(p.astype(bf16), v_ref[c * chunk : (c + 1) * chunk])
            top = new_top
        outs.append(acc / total)
        lse_ref[0, head : head + 1, :] = (top + jnp.log(total)).T
    o_ref[...] = jnp.where(lane < HD, outs[0], outs[1]).astype(bf16)


def column_of(j, which):
    return (j // TRIO) * (3 * TRIO) + which * TRIO + j % TRIO


def attend_forward(qkv, kv0, block=1024, chunk=1024):
    rows = qkv.shape[0]
    return call(
        functools.partial(attend_kernel, chunk=chunk, count=rows // chunk),
        (PAIRS, rows // block),
        [
            pl.BlockSpec((block, 128), lambda j, i: (i, column_of(j, 0))),
            pl.BlockSpec((rows, 128), lambda j, i: (0, column_of(j, 1))),
            pl.BlockSpec((rows, 128), lambda j, i: (0, column_of(j, 2))),
            pl.BlockSpec((16, 128), lambda j, i: (0, column_of(j, 1))),
            pl.BlockSpec((16, 128), lambda j, i: (0, column_of(j, 2))),
        ],
        [
            pl.BlockSpec((block, 128), lambda j, i: (i, j)),
            pl.BlockSpec((1, 2, block), lambda j, i: (j, 0, i)),
        ],
        [shape_of((rows, HALF), bf16), shape_of((PAIRS, 2, rows), f32)],
        [],
        (16 * rows * rows * HALF, 5 * rows * D * 2),
        qkv,
        qkv,
        qkv,
        kv0,
        kv0,
    )


def attend_back_kernel(*refs, chunk, count, steps, waits):
    (
        q_ref, g_ref, o_ref, lse_ref, cos_ref, up_ref, down_ref,
        k_ref, v_ref, k0_ref, v0_ref, kcos_ref, kup_ref, kdown_ref,
    ) = refs[:14]
    (
        dq_ref, dk_ref, dv_ref, dk0_ref, dv0_ref, kt, dka, dva, dk0a, dv0a,
    ) = refs[14 + waits :]
    i = pl.program_id(1)

    @pl.when(i == 0)
    def _():
        kt[...] = k_ref[...].T
        dka[...] = jnp.zeros_like(dka)
        dva[...] = jnp.zeros_like(dva)
        dk0a[...] = jnp.zeros_like(dk0a)
        dv0a[...] = jnp.zeros_like(dv0a)

    q = q_ref[...]
    g = g_ref[...]
    rows = q.shape[0]
    lane = lax.broadcasted_iota(jnp.int32, q.shape, 1)
    row = lax.broadcasted_iota(jnp.int32, (16, rows), 0)
    go = (g.astype(f32) * o_ref[...].astype(f32)).T
    k0t = k0_ref[...].T
    dqs = []
    for head in range(2):
        sel = (lane // HD) == head
        low_row, high_row = head * HD, (head + 1) * HD
        qm = jnp.where(sel, q, jnp.zeros_like(q))
        gm = jnp.where(sel, g, jnp.zeros_like(g))
        lse = lse_ref[0, head : head + 1, :]
        delta = jnp.sum(go[low_row:high_row], 0, keepdims=True)
        s = dot_nt(k0_ref[...], qm)
        p = jnp.where(row == 0, jnp.exp(s - lse), 0.0)
        ds = (p * (dot_nt(v0_ref[...], gm) - delta)).astype(bf16)
        dk0a[...] += dot_nn(ds, qm)
        dv0a[...] += dot_nn(p.astype(bf16), gm)
        dq = dot_nn(k0t[low_row:high_row], ds)
        for c in range(count):
            part = pl.ds(c * chunk, chunk)
            p = jnp.exp(dot_nt(k_ref[part], qm) - lse)
            ds = (p * (dot_nt(v_ref[part], gm) - delta)).astype(bf16)
            dva[part] += dot_nn(p.astype(bf16), gm)
            dka[part] += dot_nn(ds, qm)
            dq = dq + dot_nn(kt[low_row:high_row, c * chunk : (c + 1) * chunk], ds)
        dqs.append(dq)
    dq = (jnp.concatenate(dqs, 0).T * HD ** (-0.5)).astype(bf16).astype(f32)
    dq_ref[...] = turn(dq, cos_ref[...], -up_ref[...], -down_ref[...]).astype(bf16)

    @pl.when(i == steps - 1)
    def _():
        dk = dka[...].astype(bf16).astype(f32)
        dk_ref[...] = turn(dk, kcos_ref[...], -kup_ref[...], -kdown_ref[...]).astype(bf16)
        dv_ref[...] = dva[...].astype(bf16)
        dk0_ref[...] = dk0a[...]
        dv0_ref[...] = dv0a[...]


def attend_backward(qkv, g, o, lse, kv0, tables, half, after, block=1024, chunk=512):
    rows = qkv.shape[0]
    first = half * TRIO
    out = pl.BlockSpec((block, 128), lambda j, i: (i, j))
    head = pl.BlockSpec((block, 128), lambda j, i: (i, first + j))
    table = pl.BlockSpec((block, 128), lambda j, i: (i, 0))
    whole_table = pl.BlockSpec((rows, 128), lambda j, i: (0, 0))
    whole = pl.BlockSpec((rows, 128), lambda j, i: (0, j))
    lead = pl.BlockSpec((16, 128), lambda j, i: (0, j))

    def part(size, which):
        return pl.BlockSpec((size, 128), lambda j, i: (0, column_of(first + j, which)))

    return call(
        functools.partial(
            attend_back_kernel,
            chunk=chunk, count=rows // chunk, steps=rows // block, waits=len(after),
        ),
        (TRIO, rows // block),
        [
            pl.BlockSpec((block, 128), lambda j, i: (i, column_of(first + j, 0))),
            head, head,
            pl.BlockSpec((1, 2, block), lambda j, i: (first + j, 0, i)),
            table, table, table,
            part(rows, 1), part(rows, 2), part(16, 1), part(16, 2),
            whole_table, whole_table, whole_table,
        ]
        + [pl.BlockSpec(memory_space=pl.ANY)] * len(after),
        [out, whole, whole, lead, lead],
        [shape_of((rows, THIRD), bf16)] * 3 + [shape_of((16, THIRD), f32)] * 2,
        [
            pltpu.VMEM((128, rows), bf16),
            pltpu.VMEM((rows, 128), f32),
            pltpu.VMEM((rows, 128), f32),
            pltpu.VMEM((16, 128), f32),
            pltpu.VMEM((16, 128), f32),
        ],
        (16 * rows * rows * HALF, 5 * rows * D * 2),
        qkv, g, o, lse, *tables, qkv, qkv, kv0, kv0, *tables, *after,
    )


def prompt_probs(k, qm, mask):
    s = dot_nt(k, qm) * HD ** (-0.5) + mask
    e = jnp.exp(s - jnp.max(s, 0, keepdims=True))
    return e / jnp.sum(e, 0, keepdims=True)


def cross_kernel(q_ref, k_ref, v_ref, mask_ref, o_ref):
    q = q_ref[...]
    lane = lax.broadcasted_iota(jnp.int32, q.shape, 1)
    vt = v_ref[...].T
    outs = []
    for head in range(2):
        qm = jnp.where((lane // HD) == head, q, jnp.zeros_like(q))
        p = prompt_probs(k_ref[...], qm, mask_ref[...])
        outs.append(dot_nn(vt[head * HD : (head + 1) * HD], p.astype(bf16)))
    o_ref[...] = jnp.concatenate(outs, 0).T.astype(bf16)


def cross_back_kernel(
    q_ref, g_ref, k_ref, v_ref, mask_ref, dq_ref, dk_ref, dv_ref, dka, dva, *, steps
):
    i = pl.program_id(1)

    @pl.when(i == 0)
    def _():
        dka[...] = jnp.zeros_like(dka)
        dva[...] = jnp.zeros_like(dva)

    q = q_ref[...]
    g = g_ref[...]
    lane = lax.broadcasted_iota(jnp.int32, q.shape, 1)
    kt = k_ref[...].T
    dqs = []
    for head in range(2):
        sel = (lane // HD) == head
        qm = jnp.where(sel, q, jnp.zeros_like(q))
        gm = jnp.where(sel, g, jnp.zeros_like(g))
        p = prompt_probs(k_ref[...], qm, mask_ref[...])
        dp = dot_nt(v_ref[...], gm)
        ds = (p * (dp - jnp.sum(dp * p, 0, keepdims=True)) * HD ** (-0.5)).astype(bf16)
        dva[...] += dot_nn(p.astype(bf16), gm)
        dka[...] += dot_nn(ds, qm)
        dqs.append(dot_nn(kt[head * HD : (head + 1) * HD], ds))
    dq_ref[...] = jnp.concatenate(dqs, 0).T.astype(bf16)

    @pl.when(i == steps - 1)
    def _():
        dk_ref[...] = dka[...]
        dv_ref[...] = dva[...]


def cross_specs(rows, tokens, block):
    q_spec = pl.BlockSpec((block, 128), lambda j, i: (i, j))
    key_spec = pl.BlockSpec((tokens, 128), lambda j, i: (0, j))
    value_spec = pl.BlockSpec((tokens, 128), lambda j, i: (0, PAIRS + j))
    mask_spec = pl.BlockSpec((tokens, 1), lambda j, i: (0, 0))
    return (q_spec, key_spec, value_spec, mask_spec)


def cross_forward(q, kv, mask, block=1024):
    rows, tokens = (q.shape[0], kv.shape[0])
    q_spec, key_spec, value_spec, mask_spec = cross_specs(rows, tokens, block)
    return call(
        cross_kernel,
        (PAIRS, rows // block),
        [q_spec, key_spec, value_spec, mask_spec],
        q_spec,
        shape_of((rows, HALF), bf16),
        [],
        (16 * rows * tokens * HALF, 4 * rows * D),
        q, kv, kv, mask,
    )


def cross_backward(q, g, kv, mask, block=1024):
    rows, tokens = (q.shape[0], kv.shape[0])
    q_spec, key_spec, value_spec, mask_spec = cross_specs(rows, tokens, block)
    return call(
        functools.partial(cross_back_kernel, steps=rows // block),
        (PAIRS, rows // block),
        [q_spec, q_spec, key_spec, value_spec, mask_spec],
        [q_spec, key_spec, key_spec],
        [
            shape_of((rows, HALF), bf16),
            shape_of((tokens, HALF), f32),
            shape_of((tokens, HALF), f32),
        ],
        [pltpu.VMEM((tokens, 128), f32), pltpu.VMEM((tokens, 128), f32)],
        (32 * rows * tokens * HALF, 8 * rows * D),
        q, g, kv, kv, mask,
    )


def gate_up_kernel(n_ref, wg_ref, wu_ref, hidden_ref, gate_ref, up_ref):
    n = n_ref[...]
    gate = dot_nn(n, wg_ref[...])
    up = dot_nn(n, wu_ref[...])
    hidden_ref[...] = (gate / (1.0 + jnp.exp(-gate)) * up).astype(bf16)
    gate_ref[...] = gate.astype(bf16)
    up_ref[...] = up.astype(bf16)


def gate_up(n, w, block=512, columns=512):
    rows = n.shape[0]
    count = HIDE // columns
    out = pl.BlockSpec((block, columns), lambda j, i: (i, j))
    return call(
        gate_up_kernel,
        (count, rows // block),
        [
            pl.BlockSpec((block, D), lambda j, i: (i, 0)),
            pl.BlockSpec((D, columns), lambda j, i: (0, j)),
            pl.BlockSpec((D, columns), lambda j, i: (0, count + j)),
        ],
        [out, out, out],
        [shape_of((rows, HIDE), bf16)] * 3,
        [],
        (4 * rows * D * HIDE, 8 * rows * HIDE + 4 * D * HIDE),
        n, w, w,
    )


def down_back_kernel(d_ref, w_ref, gate_ref, up_ref, after_ref, dgate_ref, dup_ref):
    for part in range(0, w_ref.shape[0], 256):
        cols = slice(part, part + 256)
        d = dot_nt(d_ref[...], w_ref[cols])
        gate = gate_ref[:, cols].astype(f32)
        sig = 1.0 / (1.0 + jnp.exp(-gate))
        d_sig = d * sig
        dgate_ref[:, cols] = (d_sig * up_ref[:, cols] * (1.0 + gate * (1.0 - sig))).astype(bf16)
        dup_ref[:, cols] = (d_sig * gate).astype(bf16)


def down_back(d, w, gate, up, after, block=512, columns=1024):
    rows = d.shape[0]
    out = pl.BlockSpec((block, columns), lambda j, i: (i, j))
    return call(
        down_back_kernel,
        (HIDE // columns, rows // block),
        [
            pl.BlockSpec((block, D), lambda j, i: (i, 0)),
            pl.BlockSpec((columns, D), lambda j, i: (j, 0)),
            out,
            out,
            pl.BlockSpec(memory_space=pl.ANY),
        ],
        [out, out],
        [shape_of((rows, HIDE), bf16)] * 2,
        [],
        (2 * rows * D * HIDE, 10 * rows * HIDE + 2 * D * HIDE),
        d, w, gate, up, after,
    )


def chip_body(
    latents, noise_draw, audio_len, bucket, timing, prompt, prompt_len, step_count,
    edge_weight, edge_first, edge_second,
    attend_weight, attend_first, attend_second,
    square_weight, square_first, square_second,
    cross_weight, cross_first, cross_second,
    upward_weight, upward_first, upward_second,
    down_weight, down_first, down_second,
    gain_weight, gain_first, gain_second,
    *, planes, chips,
):
    peers = ("seq", "z")
    many = planes * chips
    groups = latents.shape[0]
    clips = groups * 2 * planes
    frames = latents.shape[1] * chips
    own = frames // 2
    s_at, z_at, k_at = (lax.axis_index("seq"), lax.axis_index("z"), lax.axis_index("core"))
    device = (s_at * planes + z_at) * 2 + k_at
    first_core = k_at == 0

    def swap(x):
        return lax.ppermute(x, "core", [(0, 1), (1, 0)])

    def across(x, axis, size, bit):
        return lax.ppermute(x, axis, [(i, i ^ bit) for i in range(size)])

    def bits(size):
        found = []
        bit = size // 2
        while bit:
            found.append(bit)
            bit //= 2
        return found

    hops = [("z", planes, b) for b in bits(planes)] + [("seq", chips, b) for b in bits(chips)]

    def in_order(mine, other, axis=0):
        return jnp.where(
            first_core,
            jnp.concatenate([mine, other], axis),
            jnp.concatenate([other, mine], axis),
        )

    def pick(x, index, axis):
        return lax.dynamic_index_in_dim(x, index, axis, keepdims=False)

    def halves_of(x, view, axis):
        x = x.reshape(view)
        rows = view[0]
        return (
            pick(x, k_at, axis).reshape(rows, -1),
            pick(x, 1 - k_at, axis).reshape(rows, -1),
        )

    rows = attend_weight.shape[0]
    attend_view = (rows, 2, 3, 2, THIRD)
    square_view = (rows, 3, 2, HALF)
    cross_view = (cross_weight.shape[0], 2, 2, HALF)
    up_view = (rows, 2, many, 2, FF // (2 * many))
    attend16 = attend_weight.astype(bf16).reshape(rows, 3, 2, 2, THIRD).transpose(0, 3, 1, 2, 4)
    edge16 = jnp.concatenate(
        [edge_weight[: 2 * C].astype(bf16), gain_weight.astype(bf16)], 0
    ).T
    edge16 = jnp.pad(edge16, ((0, 0), (0, 256 - edge16.shape[1])))
    mine, other = halves_of(attend16, attend_view, 3)
    mine, other = (jnp.concatenate([mine, edge16], 1), jnp.concatenate([other, edge16], 1))
    first_group = lax.all_gather(in_order(mine, swap(other)), peers, axis=0, tiled=True)
    mine, other = halves_of(
        square_weight[:3].astype(bf16).transpose(1, 0, 2), square_view, 2
    )
    square_mine = in_order(mine, swap(other))
    mine, other = halves_of(cross_weight.astype(bf16), cross_view, 2)
    cross_mine = in_order(mine, swap(other))
    cross_mine = jnp.concatenate([cross_mine[:, :HALF], cross_mine[:, HALF:]], 0)
    square_cols = lax.all_gather(
        jnp.concatenate([square_mine, cross_mine], 1), peers, axis=0, tiled=True
    )
    mine, other = halves_of(upward_weight.astype(bf16), up_view, 3)
    up_w = lax.all_gather(in_order(mine, swap(other)), peers, axis=0, tiled=True)
    down_w = lax.all_gather(down_weight.astype(bf16), peers, axis=0, tiled=True)

    attend_w = first_group[:, : 3 * HALF]
    w_in_t = first_group[:, 3 * HALF : 3 * HALF + C]
    w_out_t = first_group[:, 3 * HALF + C : 3 * HALF + 2 * C]
    norm_gains = first_group[:, 3 * HALF + 2 * C : 3 * HALF + 2 * C + 4].astype(f32).T

    def rows_half(columns):
        mine_rows = lax.dynamic_slice_in_dim(columns, k_at * HALF, HALF, 0)
        other_rows = lax.dynamic_slice_in_dim(columns, (1 - k_at) * HALF, HALF, 0)
        return in_order(mine_rows, swap(other_rows), 1)

    local = jnp.stack(
        [audio_len, bucket, timing[:, 0], timing[:, 1], prompt_len], 1
    ).astype(f32)
    clip_index = jnp.arange(clips)
    place = (clip_index // groups) == (z_at * 2 + k_at)
    scalars = jnp.where(place[:, None], jnp.tile(local, (clips // groups, 1)), 0.0)
    scalars = scalars + swap(scalars)
    for b in bits(planes):
        scalars = scalars + across(scalars, "z", planes, b)
    order = (z_at ^ (clip_index // chips)) * chips + (s_at ^ (clip_index % chips))
    chosen = order[:, None] == clip_index[None, :]
    scalars = jnp.sum(jnp.where(chosen[:, :, None], scalars[None], 0.0), 1)
    lengths = scalars[:, 0]
    t, keep_rates, noise_rates, clip_weights = plan(scalars[:, 1])
    weight_sum = jnp.sum(clip_weights * lengths)
    keep_rate, noise_rate, clip_weight = (keep_rates[0], noise_rates[0], clip_weights[0])

    t_feat = time_features(t).astype(bf16)
    z_feat = timing_features(scalars[:, 2:4]).astype(bf16)
    w_t1 = edge_weight[2 * C : 2 * C + TF].astype(bf16)
    w_t2 = square_weight[3].astype(bf16)
    w_timing = edge_weight[2 * C + TF :].astype(bf16)
    t_pre = dot_nn(t_feat, w_t1)
    t_hidden = jax.nn.silu(t_pre).astype(bf16)
    lead = lax.dynamic_update_slice(
        jnp.zeros((clips, D), f32), dot_nn(z_feat, w_timing), (0, device * rows)
    ) + dot_nn(t_hidden, w_t2)
    for axis, size, bit in hops:
        count = lead.shape[0] // 2
        lead = lead[:count] + across(lead[count:], axis, size, bit)
    lead = lead + swap(lead)
    prefix_normed, prefix_std, prefix_dev = layer_normalize(lead, norm_gains[0])
    n_prefix = jnp.pad(prefix_normed.astype(bf16), ((0, 15), (0, 0)))
    kv_prefix = dot_nn(n_prefix, attend_w).astype(bf16)

    part = s_at // groups
    member = s_at % groups
    both = jnp.stack([latents, noise_draw])
    blocks = [pick(both, member, 1)]
    for offset in range(1, chips):
        given = pick(both, (s_at ^ offset) % groups, 1)
        blocks.append(across(given, "seq", chips, offset))
    blocks = jnp.stack(blocks, 1)
    blocks = jnp.where(part == k_at, blocks, swap(blocks))
    seen = s_at ^ jnp.arange(chips)

    def mine_first(x, axis):
        low_half, high_half = jnp.split(x, 2, axis)
        return in_order(low_half, high_half, axis)

    clip = mine_first(blocks, 1).reshape(2, frames, C).astype(f32)
    clean, noisy_part = (clip[0], clip[1])
    positions = (
        mine_first(seen, 0)[:, None] * latents.shape[1] + jnp.arange(latents.shape[1])
    ).reshape(frames)
    row_weight = clip_weight * (positions[:own].astype(f32) < lengths[0]).astype(f32)
    local_prompt = pick(prompt, member, 0)
    other_prompt = swap(local_prompt)
    prompt_low = jnp.where(part == k_at, local_prompt, other_prompt)
    tokens = prompt_low.shape[0]
    mask = jnp.where(
        jnp.arange(tokens)[:, None].astype(f32) < scalars[0, 4], 0.0, -1000000000.0
    ).astype(f32)

    def shared_sum(product):
        given = product(1).astype(bf16)
        return product(0) + swap(given).astype(f32)

    def cut(x, which):
        return x[which * own : (which + 1) * own]

    def both_halves(x):
        return jnp.concatenate([x, swap(x)], 0)

    x_in = (keep_rate * clean + noise_rate * noisy_part).astype(bf16)
    x_wide = jnp.pad(x_in, ((0, 0), (0, C)))
    h0, n1 = start_forward(x_wide, first_group, norm_gains[:1])
    tables = turn_tables(positions + 1)
    qkv = qkv_project(n1, first_group, tables)
    o, lse = attend_forward(qkv, kv_prefix)

    def tie(x):
        return x[0, 0].astype(f32) * 0.0

    square_cols = square_cols[:] + tie(o).astype(bf16)
    cross_w = square_cols[:, 3 * HALF :].reshape(many, 2, CROSS // many, HALF)
    cross_w = jnp.concatenate(
        [cross_w[:, 0].reshape(CROSS, HALF), cross_w[:, 1].reshape(CROSS, HALF)], 1
    )
    w_o = rows_half(square_cols[:, :HALF])
    w_cq = square_cols[:, HALF : 2 * HALF]
    w_co = rows_half(square_cols[:, 2 * HALF : 3 * HALF])

    h1 = h0 + shared_sum(lambda i: dot_nn(cut(o, i), w_o))
    n2 = both_halves(layer_normalize(h1, norm_gains[1])[0].astype(bf16))
    cross_q = dot_nn(n2, w_cq).astype(bf16)
    cross_kv = dot_nn(prompt_low, cross_w).astype(bf16)
    co = cross_forward(cross_q, cross_kv, mask)
    h2 = h1 + shared_sum(lambda i: dot_nn(cut(co, i), w_co))
    n3 = both_halves(layer_normalize(h2, norm_gains[2])[0].astype(bf16))
    hidden, gate, upper = gate_up(n3, up_w)
    h3 = h2 + shared_sum(lambda i: dot_nn(cut(hidden, i), down_w))
    n4, std4, dev4 = layer_normalize(h3, norm_gains[3])
    n4 = n4.astype(bf16)
    predicted = dot_nn(n4, w_out_t)
    target = keep_rate * noisy_part[:own] - noise_rate * clean[:own]
    error = predicted - target
    loss_local = jnp.sum(row_weight[:, None] * error * error)

    d_pred = (2.0 / (C * weight_sum) * row_weight[:, None] * error).astype(bf16)
    g_out_t = dot_tn(n4, d_pred)
    d_h, gain4 = norm_backward(dot_nt(d_pred, w_out_t), std4, dev4, norm_gains[3])
    d_f = both_halves(d_h.astype(bf16))

    y_at, x_at = (s_at // 2, s_at % 2)

    def half_at(x, at, size):
        return lax.dynamic_slice_in_dim(x, at * size, size, 0)

    class Scatter:
        def __init__(self, product, depth, y_first):
            self.product, self.quarter, self.y_first = (product, depth // chips, y_first)
            self.bit, self.later, self.at = (2, 1, x_at) if y_first else (1, 2, y_at)
            given = product(lambda x, axis: self.rows_at(x, axis, True)).astype(bf16)
            self.sent = [given]
            self.taken = across(given, "seq", chips, self.bit)

        def rows_at(self, x, axis, flip):
            quarter = self.quarter

            def block(at):
                return lax.dynamic_slice_in_dim(x, at * quarter, quarter, axis)

            if self.y_first:
                row = (1 - y_at if flip else y_at) * 2
                return lax.dynamic_slice_in_dim(x, row * quarter, 2 * quarter, axis)
            column = 1 - x_at if flip else x_at
            return jnp.concatenate([block(column), block(2 + column)], axis)

        def second(self, behind=0.0):
            own_part = self.product(lambda x, axis: self.rows_at(x, axis, False))
            kept = (own_part + self.taken.astype(f32) + behind).astype(bf16)
            given = half_at(kept, 1 - self.at, self.quarter)
            self.kept = half_at(kept, self.at, self.quarter)
            self.sent = [given]
            self.taken = across(given, "seq", chips, self.later)
            return self

        def third(self, behind=0.0):
            kept = (self.kept.astype(f32) + self.taken.astype(f32) + behind).astype(bf16)
            size = self.quarter // planes
            self.kept = half_at(kept, z_at, size)
            self.sent = [half_at(kept, z_at ^ offset, size) for offset in range(1, planes)]
            self.taken = [
                across(given, "z", planes, offset)
                for offset, given in enumerate(self.sent, 1)
            ]
            return self

        def total(self, behind=0.0):
            return self.kept.astype(f32) + sum(x.astype(f32) for x in self.taken) + behind

    def scattered(product, depth, y_first):
        return Scatter(product, depth, y_first).second().third().total()

    def gradient(left, right, y_first):
        return Scatter(lambda cut_of: dot_tn(cut_of(left, 1), right), left.shape[1], y_first)

    def gathered_sum(g):
        return lax.psum_scatter(g, peers, scatter_dimension=0, tiled=True)

    g_down = dot_tn(hidden, d_f).astype(bf16)
    s_down = gathered_sum(g_down)
    d_gate, d_up = down_back(d_f, down_w, gate, upper, g_down)
    s_gate = gathered_sum(dot_tn(n3, d_gate).astype(bf16))
    s_upper = gathered_sum(dot_tn(n3, d_up).astype(bf16))
    d_n3 = shared_sum(
        lambda i: dot_nt(cut(d_gate, i), up_w[:, :HIDE]) + dot_nt(cut(d_up, i), up_w[:, HIDE:])
    )

    def norm_again(d_n, h, gain):
        _, std, dev = layer_normalize(h, gain)
        return norm_backward(d_n, std, dev, gain)

    d_part, gain3 = norm_again(d_n3, h2, norm_gains[2])
    d_h = d_h + d_part
    d_c = both_halves(d_h.astype(bf16))
    g_co = dot_tn(co, d_c).astype(bf16)
    d_co = dot_nt(d_c, w_co).astype(bf16)
    d_cq, d_ck, d_cv = cross_backward(cross_q, d_co, cross_kv, mask)
    r_cross = gradient(prompt_low, jnp.concatenate([d_ck, d_cv], 1).astype(bf16), False)
    r_cq = gradient(n2, d_cq, False)
    d_n2 = shared_sum(lambda i: dot_nt(cut(d_cq, i), w_cq))
    d_part, gain2 = norm_again(d_n2, h1, norm_gains[1])
    d_h = d_h + d_part
    d_a = both_halves(d_h.astype(bf16))
    g_o = dot_tn(o, d_a).astype(bf16)

    def columns_half(g):
        kept = lax.dynamic_slice_in_dim(g, k_at * HALF, HALF, 1)
        given = lax.dynamic_slice_in_dim(g, (1 - k_at) * HALF, HALF, 1)
        return in_order(kept, swap(given), 0)

    side = jnp.concatenate([columns_half(g_o), columns_half(g_co)], 1)
    r_side = Scatter(lambda cut_of: cut_of(side, 0).astype(f32), D, True)
    d_o = dot_nt(d_a, w_o).astype(bf16)
    lead_column = n_prefix[:1].astype(f32)

    def attend_half(half, after):
        d_q, d_k, d_v, d_k0, d_v0 = attend_backward(qkv, d_o, o, lse, kv_prefix, tables, half, after)
        lead_row = jnp.concatenate([jnp.zeros_like(d_k0), d_k0, d_v0], 1)
        return (jnp.concatenate([d_q, d_k, d_v], 1), lead_row, tie(d_q))

    def attend_gradient(right, lead_row, y_first):
        def product(cut_of):
            return dot_tn(cut_of(n1, 1), right) + cut_of(lead_column, 1).T * lead_row[:1]

        return Scatter(product, D, y_first)

    after = [x for r in (r_cross, r_cq, r_side) for x in r.sent]
    d_first, lead_first, behind_first = attend_half(0, after)
    r_first = attend_gradient(d_first, lead_first, True)
    for r in (r_cross, r_cq, r_side):
        r.second(behind_first)
    after = [x for r in (r_cross, r_cq, r_side, r_first) for x in r.sent]
    d_second, lead_second, behind_second = attend_half(1, after)
    edge_at = 5 * 128
    r_second = attend_gradient(d_second[:, :edge_at], lead_second[:, :edge_at], True)
    r_last = attend_gradient(d_second[:, edge_at:], lead_second[:, edge_at:], False)
    for r in (r_first, r_second, r_last):
        r.second(behind_second)
    d_n1 = shared_sum(
        lambda i: dot_nt(cut(d_first, i), attend_w[:, : 3 * THIRD])
        + dot_nt(cut(d_second, i), attend_w[:, 3 * THIRD :])
    )
    d_part, gain1 = norm_again(d_n1, h0, norm_gains[0])
    d_h = d_h + d_part
    g_in_t = dot_tn(d_h.astype(bf16), x_in[:own])
    s_cross, s_cq, s_side = (r.third(behind_second).total() for r in (r_cross, r_cq, r_side))
    s_square = jnp.concatenate([s_side[:, :HALF], s_cq, s_side[:, HALF:]], 1)
    s_attend = jnp.concatenate([r.third().total() for r in (r_first, r_second, r_last)], 1)
    d_kv0 = jnp.concatenate([lead_first, lead_second], 1)

    high = d_kv0.astype(bf16)
    rest = (d_kv0 - high.astype(f32)).astype(bf16)
    d_np = dot_nt(jnp.concatenate([high, rest], 0), attend_w)
    d_np = d_np[:1] + d_np[16:17]
    d_np = d_np + swap(d_np)
    d_lead, prefix_gain = norm_backward(d_np, prefix_std, prefix_dev, norm_gains[0])
    for axis, size, bit in reversed(hops):
        d_lead = jnp.concatenate([d_lead, across(d_lead, axis, size, bit)], 0)
    g_t2 = exact("ge,gd->ed", t_hidden.astype(f32), d_lead)
    d_lead_here = lax.dynamic_slice(d_lead, (0, device * rows), (clips, rows))
    g_timing = exact("gz,gd->zd", z_feat.astype(f32), d_lead_here)
    d_t_hidden = exact("gd,ed->ge", d_lead, w_t2.astype(f32))
    t_sig = jax.nn.sigmoid(t_pre)
    d_t_pre = d_t_hidden * t_sig * (1.0 + t_pre * (1.0 - t_sig))
    g_t1 = exact("gz,gd->zd", t_feat.astype(f32), d_t_pre)

    def to_owner(x, view, axis):
        count = x.shape[0] // 2
        kept = lax.dynamic_slice_in_dim(x, k_at * count, count, 0)
        given = lax.dynamic_slice_in_dim(x, (1 - k_at) * count, count, 0)
        taken = swap(given.astype(bf16)).astype(f32)
        shape = view[:axis] + view[axis + 1 :]
        joined = jnp.where(
            first_core,
            jnp.stack([kept.reshape(shape), taken.reshape(shape)], axis),
            jnp.stack([taken.reshape(shape), kept.reshape(shape)], axis),
        )
        return joined

    gains = jnp.stack([gain1 + 0.5 * prefix_gain, gain2, gain3, gain4], 1)
    edges = jnp.concatenate([g_in_t, g_out_t], 1)
    gains = jnp.pad(gains, ((0, 0), (0, 128 - gains.shape[1])))
    edges = jnp.where(first_core, edges, gains) + swap(jnp.where(first_core, gains, edges))
    s_edge = scattered(lambda cut_of: cut_of(edges, 0), D, True)
    s_edge = to_owner(s_edge, (rows, 2, 128), 1).reshape(rows, 256)

    g_attend = to_owner(s_attend, attend_view, 3).transpose(0, 2, 3, 1, 4).reshape(rows, 3 * D)
    g_square = to_owner(s_square, square_view, 2).reshape(rows, 3, D).transpose(1, 0, 2)
    g_square = jnp.concatenate([g_square, g_t2[None]], 0)
    g_cross = to_owner(s_cross, cross_view, 2).reshape(cross_view[0], 2 * D)
    g_up = to_owner(jnp.concatenate([s_gate, s_upper], 1).astype(f32), up_view, 3).reshape(rows, 2 * FF)
    g_down = s_down.astype(f32)
    g_edge = jnp.concatenate([s_edge[:, : 2 * C].T, g_t1, g_timing], 0)
    g_gain = s_edge[:, 2 * C : 2 * C + 4].T
    sharded = (g_edge, g_attend, g_square, g_cross, g_up, g_down, g_gain)
    totals = jnp.stack([sum(jnp.sum(g * g) for g in sharded), loss_local])
    totals = totals + swap(totals)
    for axis, size, bit in hops:
        totals = totals + across(totals, axis, size, bit)
    grad_norm = jnp.sqrt(totals[0])
    loss_value = totals[1] / (C * weight_sum)
    factor = jnp.minimum(1.0, clip_norm / grad_norm)
    count = step_count[0].astype(f32)
    first_fix = 1.0 - 0.9**count
    second_fix = 1.0 - 0.999**count
    states = (
        (edge_weight, edge_first, edge_second),
        (attend_weight, attend_first, attend_second),
        (square_weight, square_first, square_second),
        (cross_weight, cross_first, cross_second),
        (upward_weight, upward_first, upward_second),
        (down_weight, down_first, down_second),
        (gain_weight, gain_first, gain_second),
    )
    out = [
        adam(w, m, v, g * factor, first_fix, second_fix)
        for (w, m, v), g in zip(states, sharded)
    ]
    flat = [x for triple in out[:6] for x in triple]
    return (loss_value, grad_norm, *flat, g_gain * factor, out[6][1], out[6][2])


def solution(mesh):
    chips, spread = (mesh.shape["seq"], mesh.shape["dp"])
    split_mesh = Mesh(mesh.devices.reshape(chips, spread // 2, 2), ("seq", "z", "core"))

    def whole(*args):
        groups = args[0].shape[0] // spread
        one_clip_per_chip = groups * 2 == chips == 4 and spread & (spread - 1) == 0
        if one_clip_per_chip:
            inner = functools.partial(chip_body, planes=spread // 2, chips=chips)
            dp, used = ("z", "core"), split_mesh
        else:
            inner, dp, used = (general_body, "dp", mesh)
        every = ("seq",) + (dp if isinstance(dp, tuple) else (dp,))
        by_row, by_column, by_middle = (P(every, None), P(None, every), P(None, every, None))
        frames = P(dp, "seq", None)
        clip = P(dp)
        kinds = (by_column, by_row, by_middle, by_row, by_row, by_row, by_column)
        weights = tuple(kind for kind in kinds for _ in range(3))
        return jax.shard_map(
            inner,
            mesh=used,
            in_specs=(frames, frames, clip, clip, P(dp, None), P(dp, None, None), clip, P())
            + weights,
            out_specs=(P(), P()) + weights,
            check_vma=False,
        )(*args)

    return whole
```

```python
import functools
import math

import jax
import jax.numpy as jnp
from jax import lax
from jax.experimental import pallas as pl
from jax.experimental.pallas import tpu as pltpu
from jax.sharding import Mesh
from jax.sharding import PartitionSpec as P

D = 1536
H = 24
HD = 64
FF = 6144
C = 64
TF = 256
PT = 128
NB = 1000


highest = lax.Precision.HIGHEST
clip_norm = 0.002
learn_rate = 0.1
weight_decay = 0.1
rot_width = 32


def layer_normalize(h, norm_gain):
    centered_input = h - jnp.mean(h, -1, keepdims=True)
    inverse_deviation = lax.rsqrt(
        jnp.mean(centered_input * centered_input, -1, keepdims=True) + 1e-05
    )
    standardized = centered_input * inverse_deviation
    return (standardized * norm_gain, standardized, inverse_deviation)


def norm_backward(incoming_gradient, standardized, inverse_deviation, norm_gain):
    scaled_gradient = incoming_gradient * norm_gain
    gain_gradient = jnp.sum(incoming_gradient * standardized, 0)
    d_in = inverse_deviation * (
        scaled_gradient
        - jnp.mean(scaled_gradient, -1, keepdims=True)
        - standardized * jnp.mean(scaled_gradient * standardized, -1, keepdims=True)
    )
    return (d_in, gain_gradient)


def plan(bucket):
    t = (bucket.astype(jnp.float32) + 0.5) / NB
    keep_rate = jnp.cos(t * (math.pi / 2))
    noise_rate = jnp.sin(t * (math.pi / 2))
    snr_ratio = keep_rate * keep_rate / (noise_rate * noise_rate)
    return (t, keep_rate, noise_rate, jnp.minimum(snr_ratio, 5.0) / (snr_ratio + 1.0))


def time_features(t):
    freqs = jnp.exp(-math.log(10000.0) * jnp.arange(TF // 2, dtype=jnp.float32) / (TF // 2))
    angle = t[:, None] * 1000.0 * freqs[None, :]
    return jnp.concatenate([jnp.cos(angle), jnp.sin(angle)], -1)


def timing_features(timing):
    seconds = timing.astype(jnp.float32) / 64.0
    return jnp.concatenate([time_features(seconds[:, 0]), time_features(seconds[:, 1])], -1)


def rope_tables(positions):
    inverse = 10000.0 ** (-2.0 * jnp.arange(rot_width // 2, dtype=jnp.float32) / rot_width)
    angle = positions[:, None].astype(jnp.float32) * inverse[None, :]
    angle = jnp.concatenate([angle, angle], -1)
    return (jnp.cos(angle), jnp.sin(angle))


def rotate(x):
    half = rot_width // 2
    return jnp.concatenate([-x[..., half:], x[..., :half]], -1)


def apply_rope(x, cosine, sine_part):
    turned = x[..., :rot_width]
    turned = turned * cosine[None, :, None, :] + rotate(turned) * sine_part[None, :, None, :]
    return jnp.concatenate([turned, x[..., rot_width:]], -1)


def rope_back(incoming_gradient, cosine, sine_part):
    turned = incoming_gradient[..., :rot_width]
    turned = turned * cosine[None, :, None, :] - rotate(turned * sine_part[None, :, None, :])
    return jnp.concatenate([turned, incoming_gradient[..., rot_width:]], -1)


def split_blocks(x, count, block):
    return x.reshape((x.shape[0], count, block) + x.shape[2:]).swapaxes(0, 1)


def join_blocks(x):
    x = x.swapaxes(0, 1)
    return x.reshape((x.shape[0], x.shape[1] * x.shape[2]) + x.shape[3:])


def attend(q, keys, values):
    rows_q = q.shape[1]
    block = min(512, rows_q)
    count = rows_q // block
    score_scale = HD ** (-0.5)

    def one_block(q_block):
        s = (
            jnp.einsum("ibd,ikd->ibk", q_block, keys, preferred_element_type=jnp.float32)
            * score_scale
        )
        top = jnp.max(s, -1, keepdims=True)
        lse = top + jnp.log(jnp.sum(jnp.exp(s - top), -1, keepdims=True))
        p = jnp.exp(s - lse)
        o = jnp.einsum(
            "ibk,ikd->ibd", p.astype(jnp.bfloat16), values, preferred_element_type=jnp.float32
        )
        return (o, lse[..., 0])

    outs, lses = lax.map(one_block, split_blocks(q, count, block))
    return (join_blocks(outs), join_blocks(lses))


def attend_back(q, keys, values, lse, grad_o):
    rows_q = q.shape[1]
    block = min(512, rows_q)
    count = rows_q // block
    score_scale = HD ** (-0.5)

    def one_block(carry, parts):
        d_key, d_value = carry
        q_block, g_block, l_block = parts
        s = (
            jnp.einsum("ibd,ikd->ibk", q_block, keys, preferred_element_type=jnp.float32)
            * score_scale
        )
        p = jnp.exp(s - l_block[..., None])
        d_prob = jnp.einsum("ibd,ikd->ibk", g_block, values, preferred_element_type=jnp.float32)
        d_value = d_value + jnp.einsum(
            "ibk,ibd->ikd", p.astype(jnp.bfloat16), g_block, preferred_element_type=jnp.float32
        )
        d_score = (p * (d_prob - jnp.sum(d_prob * p, -1, keepdims=True)) * score_scale).astype(
            jnp.bfloat16
        )
        d_query = jnp.einsum("ibk,ikd->ibd", d_score, keys, preferred_element_type=jnp.float32)
        d_key = d_key + jnp.einsum(
            "ibk,ibd->ikd", d_score, q_block, preferred_element_type=jnp.float32
        )
        return ((d_key, d_value), d_query)

    zeros = jnp.zeros(keys.shape, jnp.float32)
    parts = (
        split_blocks(q, count, block),
        split_blocks(grad_o, count, block),
        split_blocks(lse, count, block),
    )
    (d_key, d_value), d_queries = lax.scan(one_block, (zeros, zeros), parts)
    return (join_blocks(d_queries), d_key, d_value)


def adam(w, m, v, g, first_fix, second_fix):
    first = 0.9 * m + 0.1 * g
    second = 0.999 * v + 0.001 * g * g
    new = w - learn_rate * (
        first / first_fix / (jnp.sqrt(second / second_fix) + 1e-08) + weight_decay * w
    )
    return (new, first, second)


def exact(form, a, b):
    return jnp.einsum(form, a, b, precision=highest, preferred_element_type=jnp.float32)


def general_body(
    latents,
    noise_draw,
    audio_len,
    bucket,
    timing,
    prompt,
    prompt_len,
    step_count,
    edge_weight,
    edge_first,
    edge_second,
    attend_weight,
    attend_first,
    attend_second,
    square_weight,
    square_first,
    square_second,
    cross_weight,
    cross_first,
    cross_second,
    upward_weight,
    upward_first,
    upward_second,
    down_weight,
    down_first,
    down_second,
    gain_weight,
    gain_first,
    gain_second,
):
    low_type = jnp.bfloat16
    wide = jnp.float32
    groups, frames = (latents.shape[0], latents.shape[1])
    total_rows = groups * frames
    items = groups * H
    edge16, attend16, square16, cross16, upward16, down16, gain16 = (
        lax.all_gather(edge_weight.astype(low_type), ("seq", "dp"), axis=1, tiled=True),
        lax.all_gather(attend_weight.astype(low_type), ("seq", "dp"), axis=0, tiled=True),
        lax.all_gather(square_weight.astype(low_type), ("seq", "dp"), axis=1, tiled=True),
        lax.all_gather(cross_weight.astype(low_type), ("seq", "dp"), axis=0, tiled=True),
        lax.all_gather(upward_weight.astype(low_type), ("seq", "dp"), axis=0, tiled=True),
        lax.all_gather(down_weight.astype(low_type), ("seq", "dp"), axis=0, tiled=True),
        lax.all_gather(gain_weight.astype(low_type), ("seq", "dp"), axis=1, tiled=True),
    )
    norm_gains = gain16.astype(wide)
    positions = lax.axis_index("seq") * frames + jnp.arange(frames, dtype=jnp.int32)
    t, keep_rate, noise_rate, clip_weight = plan(bucket)
    frame_mask = (positions[None, :] < audio_len[:, None]).astype(wide)
    row_weight = (clip_weight[:, None] * frame_mask).reshape(total_rows)
    weight_sum = lax.psum(jnp.sum(row_weight), ("seq", "dp"))
    clean = latents.astype(wide)
    noisy_part = noise_draw.astype(wide)
    x_in = (
        (keep_rate[:, None, None] * clean + noise_rate[:, None, None] * noisy_part)
        .astype(low_type)
        .reshape(total_rows, C)
    )
    t_feat = time_features(t).astype(low_type)
    z_feat = timing_features(timing).astype(low_type)
    t_pre = jnp.dot(t_feat, edge16[2 * C : 2 * C + TF], preferred_element_type=wide)
    t_hidden = jax.nn.silu(t_pre).astype(low_type)
    leading_token = jnp.dot(t_hidden, square16[3], preferred_element_type=wide) + jnp.dot(
        z_feat, edge16[2 * C + TF :], preferred_element_type=wide
    )
    prefix_normed, prefix_standardized, prefix_inverse_deviation = layer_normalize(
        leading_token, norm_gains[0]
    )
    n_prefix_low = prefix_normed.astype(low_type)
    kv_prefix = jnp.dot(n_prefix_low, attend16[:, D:], preferred_element_type=wide).astype(low_type)
    k_prefix = kv_prefix[:, :D].reshape(items, 1, HD)
    v_prefix = kv_prefix[:, D:].reshape(items, 1, HD)
    hidden_start = jnp.dot(x_in, edge16[:C], preferred_element_type=wide)
    first_normed, first_standardized, first_inverse_deviation = layer_normalize(
        hidden_start, norm_gains[0]
    )
    n1_low = first_normed.astype(low_type)
    projected = jnp.dot(n1_low, attend16, preferred_element_type=wide).reshape(
        groups, frames, 3, H, HD
    )
    cosine, sine_part = rope_tables(positions + 1)
    rotated = jnp.stack(
        [
            apply_rope(projected[:, :, 0], cosine, sine_part),
            apply_rope(projected[:, :, 1], cosine, sine_part),
            projected[:, :, 2],
        ]
    ).astype(low_type)
    as_items = rotated.transpose(0, 1, 3, 2, 4).reshape(3, items, frames, HD)
    q_use = as_items[0]
    key_value = lax.all_gather(as_items[1:], "seq", axis=2, tiled=True)
    keys = jnp.concatenate([k_prefix, key_value[0]], 1)
    values = jnp.concatenate([v_prefix, key_value[1]], 1)
    o_items, lse = attend(q_use, keys, values)
    o_local = o_items.astype(low_type)
    o_low = o_local.reshape(groups, H, frames, HD).transpose(0, 2, 1, 3).reshape(total_rows, D)
    hidden_after_self = hidden_start + jnp.dot(o_low, square16[0], preferred_element_type=wide)
    second_normed, second_standardized, second_inverse_deviation = layer_normalize(
        hidden_after_self, norm_gains[1]
    )
    n2_low = second_normed.astype(low_type)
    cross_q = (
        jnp.dot(n2_low, square16[1], preferred_element_type=wide)
        .astype(low_type)
        .reshape(groups, frames, H, HD)
    )
    cross_kv = jnp.einsum("gpc,ce->gpe", prompt, cross16, preferred_element_type=wide).astype(
        low_type
    )
    cross_k = cross_kv[..., :D].reshape(groups, PT, H, HD)
    cross_v = cross_kv[..., D:].reshape(groups, PT, H, HD)
    key_mask = jnp.arange(PT)[None, :] < prompt_len[:, None]
    score_scale = HD ** (-0.5)
    scores = (
        jnp.einsum("gfhd,gphd->ghfp", cross_q, cross_k, preferred_element_type=wide) * score_scale
    )
    scores = jnp.where(key_mask[:, None, None, :], scores, -1000000000.0)
    probs = jax.nn.softmax(scores, -1)
    probs_low = probs.astype(low_type)
    co_low = (
        jnp.einsum("ghfp,gphd->gfhd", probs_low, cross_v, preferred_element_type=wide)
        .astype(low_type)
        .reshape(total_rows, D)
    )
    hidden_after_cross = hidden_after_self + jnp.dot(
        co_low, square16[2], preferred_element_type=wide
    )
    third_normed, third_standardized, third_inverse_deviation = layer_normalize(
        hidden_after_cross, norm_gains[2]
    )
    n3_low = third_normed.astype(low_type)
    gate_up = jnp.dot(n3_low, upward16, preferred_element_type=wide)
    gate, upper = (gate_up[:, :FF], gate_up[:, FF:])
    hidden = (jax.nn.silu(gate) * upper).astype(low_type)
    hidden_after_feed = hidden_after_cross + jnp.dot(hidden, down16, preferred_element_type=wide)
    fourth_normed, fourth_standardized, fourth_inverse_deviation = layer_normalize(
        hidden_after_feed, norm_gains[3]
    )
    n4_low = fourth_normed.astype(low_type)
    predicted = jnp.einsum("rd,cd->rc", n4_low, edge16[C : 2 * C], preferred_element_type=wide)
    target = (keep_rate[:, None, None] * noisy_part - noise_rate[:, None, None] * clean).reshape(
        total_rows, C
    )
    error = predicted - target
    loss_local = jnp.sum(row_weight[:, None] * error * error)
    d_pred = (2.0 / (C * weight_sum) * row_weight[:, None] * error).astype(low_type)
    g_out = jnp.einsum("rc,rd->cd", d_pred, n4_low, preferred_element_type=wide)
    fourth_norm_gradient = jnp.dot(d_pred, edge16[C : 2 * C], preferred_element_type=wide)
    hidden_gradient, fourth_gain_gradient = norm_backward(
        fourth_norm_gradient, fourth_standardized, fourth_inverse_deviation, norm_gains[3]
    )
    d_f = hidden_gradient.astype(low_type)
    g_down = jnp.einsum("rf,rd->fd", hidden, d_f, preferred_element_type=wide)
    d_hidden = jnp.einsum("rd,fd->rf", d_f, down16, preferred_element_type=wide)
    sig = jax.nn.sigmoid(gate)
    d_gate_up = jnp.concatenate(
        [d_hidden * upper * sig * (1.0 + gate * (1.0 - sig)), d_hidden * gate * sig], -1
    ).astype(low_type)
    g_up = jnp.einsum("rd,re->de", n3_low, d_gate_up, preferred_element_type=wide)
    third_norm_gradient = jnp.einsum("re,de->rd", d_gate_up, upward16, preferred_element_type=wide)
    partial_gradient, third_gain_gradient = norm_backward(
        third_norm_gradient, third_standardized, third_inverse_deviation, norm_gains[2]
    )
    hidden_gradient = hidden_gradient + partial_gradient
    d_c = hidden_gradient.astype(low_type)
    g_co = jnp.einsum("rd,re->de", co_low, d_c, preferred_element_type=wide)
    d_co = (
        jnp.einsum("re,de->rd", d_c, square16[2], preferred_element_type=wide)
        .astype(low_type)
        .reshape(groups, frames, H, HD)
    )
    d_prob = jnp.einsum("gfhd,gphd->ghfp", d_co, cross_v, preferred_element_type=wide)
    d_cv = jnp.einsum("ghfp,gfhd->gphd", probs_low, d_co, preferred_element_type=wide)
    d_score = (probs * (d_prob - jnp.sum(d_prob * probs, -1, keepdims=True)) * score_scale).astype(
        low_type
    )
    d_cq = (
        jnp.einsum("ghfp,gphd->gfhd", d_score, cross_k, preferred_element_type=wide)
        .astype(low_type)
        .reshape(total_rows, D)
    )
    d_ck = jnp.einsum("ghfp,gfhd->gphd", d_score, cross_q, preferred_element_type=wide)
    d_cross_kv = jnp.concatenate([d_ck.reshape(groups, PT, D), d_cv.reshape(groups, PT, D)], -1)
    g_cross = exact("gpc,gpe->ce", prompt.astype(wide), d_cross_kv)
    g_cq = jnp.einsum("rd,re->de", n2_low, d_cq, preferred_element_type=wide)
    second_norm_gradient = jnp.einsum("re,de->rd", d_cq, square16[1], preferred_element_type=wide)
    partial_gradient, second_gain_gradient = norm_backward(
        second_norm_gradient, second_standardized, second_inverse_deviation, norm_gains[1]
    )
    hidden_gradient = hidden_gradient + partial_gradient
    d_a = hidden_gradient.astype(low_type)
    g_o = jnp.einsum("rd,re->de", o_low, d_a, preferred_element_type=wide)
    d_o = jnp.einsum("re,de->rd", d_a, square16[0], preferred_element_type=wide).astype(low_type)
    d_o_items = d_o.reshape(groups, frames, H, HD).transpose(0, 2, 1, 3).reshape(items, frames, HD)
    d_query, d_key, d_value = attend_back(q_use, keys, values, lse, d_o_items)
    summed_key, summed_value = (
        lax.psum_scatter(
            d_key[:, 1:].astype(jnp.bfloat16), "seq", scatter_dimension=1, tiled=True
        ).astype(jnp.float32),
        lax.psum_scatter(
            d_value[:, 1:].astype(jnp.bfloat16), "seq", scatter_dimension=1, tiled=True
        ).astype(jnp.float32),
    )
    d_items = jnp.stack(
        [d_query.astype(low_type), summed_key.astype(low_type), summed_value.astype(low_type)]
    )
    d_key_prefix = d_key[:, :1]
    d_value_prefix = d_value[:, :1]
    d_rot = d_items.astype(wide).reshape(3, groups, H, frames, HD).transpose(1, 3, 0, 2, 4)
    d_projected = (
        jnp.stack(
            [
                rope_back(d_rot[:, :, 0], cosine, sine_part),
                rope_back(d_rot[:, :, 1], cosine, sine_part),
                d_rot[:, :, 2],
            ],
            2,
        )
        .reshape(total_rows, 3 * D)
        .astype(low_type)
    )
    g_attend = jnp.einsum("rd,re->de", n1_low, d_projected, preferred_element_type=wide)
    first_norm_gradient = jnp.einsum(
        "re,de->rd", d_projected, attend16, preferred_element_type=wide
    )
    partial_gradient, first_gain_gradient = norm_backward(
        first_norm_gradient, first_standardized, first_inverse_deviation, norm_gains[0]
    )
    hidden_gradient = hidden_gradient + partial_gradient
    g_in = jnp.einsum(
        "rc,rd->cd", x_in, hidden_gradient.astype(low_type), preferred_element_type=wide
    )
    d_kv_prefix = jnp.concatenate(
        [d_key_prefix.reshape(groups, D), d_value_prefix.reshape(groups, D)], -1
    )
    attend_kv = attend16[:, D:].astype(wide)
    g_attend = g_attend.at[:, D:].add(exact("gd,ge->de", n_prefix_low.astype(wide), d_kv_prefix))
    prefix_norm_gradient = exact("ge,de->gd", d_kv_prefix, attend_kv)
    leading_token_gradient, prefix_gain_gradient = norm_backward(
        prefix_norm_gradient, prefix_standardized, prefix_inverse_deviation, norm_gains[0]
    )
    g_timing = exact("gz,gd->zd", z_feat.astype(wide), leading_token_gradient)
    g_t2 = exact("ge,gd->ed", t_hidden.astype(wide), leading_token_gradient)
    d_t_hidden = exact("gd,ed->ge", leading_token_gradient, square16[3].astype(wide))
    t_sig = jax.nn.sigmoid(t_pre)
    d_t_pre = d_t_hidden * t_sig * (1.0 + t_pre * (1.0 - t_sig))
    g_t1 = exact("gz,gd->zd", t_feat.astype(wide), d_t_pre)
    g_edge = jnp.concatenate([g_in, g_out, g_t1, g_timing], 0)
    g_square = jnp.stack([g_o, g_cq, g_co, g_t2])
    g_gain = jnp.stack(
        [
            first_gain_gradient + prefix_gain_gradient,
            second_gain_gradient,
            third_gain_gradient,
            fourth_gain_gradient,
        ]
    )
    sharded = (
        lax.psum_scatter(g_edge, ("seq", "dp"), scatter_dimension=1, tiled=True),
        lax.psum_scatter(g_attend, ("seq", "dp"), scatter_dimension=0, tiled=True),
        lax.psum_scatter(g_square, ("seq", "dp"), scatter_dimension=1, tiled=True),
        lax.psum_scatter(g_cross, ("seq", "dp"), scatter_dimension=0, tiled=True),
        lax.psum_scatter(g_up, ("seq", "dp"), scatter_dimension=0, tiled=True),
        lax.psum_scatter(g_down, ("seq", "dp"), scatter_dimension=0, tiled=True),
        lax.psum_scatter(g_gain, ("seq", "dp"), scatter_dimension=1, tiled=True),
    )
    square_local = sum((jnp.sum(g * g) for g in sharded))
    square_total, loss_total = lax.psum((square_local, loss_local), ("seq", "dp"))
    grad_norm = jnp.sqrt(square_total)
    loss_value = loss_total / (C * weight_sum)
    factor = jnp.minimum(1.0, clip_norm / grad_norm)
    count = step_count[0].astype(wide)
    first_fix = 1.0 - 0.9**count
    second_fix = 1.0 - 0.999**count
    weights = (
        edge_weight,
        attend_weight,
        square_weight,
        cross_weight,
        upward_weight,
        down_weight,
        gain_weight,
    )
    firsts = (
        edge_first,
        attend_first,
        square_first,
        cross_first,
        upward_first,
        down_first,
        gain_first,
    )
    seconds = (
        edge_second,
        attend_second,
        square_second,
        cross_second,
        upward_second,
        down_second,
        gain_second,
    )
    out = [
        adam(w, m, v, g * factor, first_fix, second_fix)
        for w, m, v, g in zip(weights, firsts, seconds, sharded)
    ]
    return (
        loss_value,
        grad_norm,
        out[0][0],
        out[0][1],
        out[0][2],
        out[1][0],
        out[1][1],
        out[1][2],
        out[2][0],
        out[2][1],
        out[2][2],
        out[3][0],
        out[3][1],
        out[3][2],
        out[4][0],
        out[4][1],
        out[4][2],
        out[5][0],
        out[5][1],
        out[5][2],
        sharded[6] * factor,
        out[6][1],
        out[6][2],
    )


f32 = jnp.float32
bf16 = jnp.bfloat16
HALF = D // 2
PAIRS = HALF // 128
TRIO = PAIRS // 2
THIRD = HALF // 2
HIDE = FF // 2
CROSS = 768


def dot_nt(a, b):
    return lax.dot_general(a, b, (((1,), (1,)), ((), ())), preferred_element_type=f32)


def dot_nn(a, b):
    return lax.dot_general(a, b, (((1,), (0,)), ((), ())), preferred_element_type=f32)


def dot_tn(a, b):
    return lax.dot_general(a, b, (((0,), (0,)), ((), ())), preferred_element_type=f32)


def call(kernel, grid, in_specs, out_specs, out_shape, scratch, cost, *operands):
    return pl.pallas_call(
        kernel,
        grid=grid,
        in_specs=in_specs,
        out_specs=out_specs,
        out_shape=out_shape,
        scratch_shapes=scratch,
        cost_estimate=pl.CostEstimate(flops=cost[0], bytes_accessed=cost[1], transcendentals=0),
        compiler_params=pltpu.CompilerParams(vmem_limit_bytes=60 << 20),
    )(*operands)


def shape_of(shape, kind):
    return jax.ShapeDtypeStruct(shape, kind)


def turn(y, cosine, sine_up, sine_down):
    return y * cosine + pltpu.roll(y, 16, 1) * sine_up + pltpu.roll(y, 112, 1) * sine_down


def turn_tables(positions):
    lane = jnp.arange(128) % HD
    inverse = 10000.0 ** (-2.0 * jnp.arange(rot_width // 2, dtype=f32) / rot_width)
    angle = positions[:, None].astype(f32) * inverse[None, :]
    wide_angle = jnp.tile(angle, (1, 128 // (rot_width // 2)))
    cosine = jnp.where(lane[None, :] < rot_width, jnp.cos(wide_angle), 1.0)
    sine = jnp.sin(wide_angle)
    second = (lane[None, :] >= rot_width // 2) & (lane[None, :] < rot_width)
    sine_up = jnp.where(second, sine, 0.0)
    sine_down = jnp.where(lane[None, :] < rot_width // 2, -sine, 0.0)
    return (cosine, sine_up, sine_down)


def start_kernel(x_ref, w_ref, gain_ref, h_ref, n_ref, *, own):
    h = dot_nt(x_ref[...], w_ref[...])
    n_ref[...] = layer_normalize(h, gain_ref[...])[0].astype(bf16)

    @pl.when(pl.program_id(0) < own)
    def _():
        h_ref[...] = h


def start_forward(x, w, gain, block=256):
    rows = x.shape[0]
    own = rows // 2 // block
    return call(
        functools.partial(start_kernel, own=own),
        (rows // block,),
        [
            pl.BlockSpec((block, 128), lambda i: (i, 0)),
            pl.BlockSpec((D, 128), lambda i: (0, 3 * PAIRS)),
            pl.BlockSpec((1, D), lambda i: (0, 0)),
        ],
        [
            pl.BlockSpec((block, D), lambda i: (jnp.minimum(i, own - 1), 0)),
            pl.BlockSpec((block, D), lambda i: (i, 0)),
        ],
        [shape_of((rows // 2, D), f32), shape_of((rows, D), bf16)],
        [],
        (2 * rows * D * 128, 4 * rows * D),
        x, w, gain,
    )


def qkv_kernel(n_ref, w_ref, cos_ref, up_ref, down_ref, out_ref):
    part = pl.program_id(0) % 3
    y = dot_nn(n_ref[...], w_ref[...])

    @pl.when(part < 2)
    def _():
        scale = jnp.where(part == 0, HD ** (-0.5), 1.0)
        for j in range(TRIO):
            block = y[:, j * 128 : (j + 1) * 128]
            turned = turn(block, cos_ref[...], up_ref[...], down_ref[...])
            out_ref[:, j * 128 : (j + 1) * 128] = (turned * scale).astype(bf16)

    @pl.when(part == 2)
    def _():
        out_ref[...] = y.astype(bf16)


def qkv_project(n, w, tables, block=1024):
    rows = n.shape[0]
    table = pl.BlockSpec((block, 128), lambda p, i: (i, 0))
    return call(
        qkv_kernel,
        (6, rows // block),
        [
            pl.BlockSpec((block, D), lambda p, i: (i, 0)),
            pl.BlockSpec((D, THIRD), lambda p, i: (0, p)),
            table,
            table,
            table,
        ],
        pl.BlockSpec((block, THIRD), lambda p, i: (i, p)),
        shape_of((rows, 3 * HALF), bf16),
        [],
        (2 * rows * D * 3 * HALF, 4 * rows * D * 2),
        n,
        w,
        *tables,
    )


def attend_kernel(q_ref, k_ref, v_ref, k0_ref, v0_ref, o_ref, lse_ref, *, chunk, count):
    q = q_ref[...]
    rows = q.shape[0]
    lane = lax.broadcasted_iota(jnp.int32, q.shape, 1)
    k0 = k0_ref[0:1].astype(f32)
    v0 = v0_ref[0:1].astype(f32)
    outs = []
    for head in range(2):
        mine = jnp.where((lane // HD) == head, q, jnp.zeros_like(q))
        top = jnp.sum(mine.astype(f32) * k0, 1, keepdims=True)
        total = jnp.ones_like(top)
        acc = jnp.broadcast_to(v0, (rows, 128))
        for c in range(count):
            s = dot_nt(mine, k_ref[c * chunk : (c + 1) * chunk])
            new_top = jnp.maximum(top, jnp.max(s, 1, keepdims=True))
            fade = jnp.exp(top - new_top)
            p = jnp.exp(s - new_top)
            total = total * fade + jnp.sum(p, 1, keepdims=True)
            acc = acc * fade + dot_nn(p.astype(bf16), v_ref[c * chunk : (c + 1) * chunk])
            top = new_top
        outs.append(acc / total)
        lse_ref[0, head : head + 1, :] = (top + jnp.log(total)).T
    o_ref[...] = jnp.where(lane < HD, outs[0], outs[1]).astype(bf16)


def column_of(j, which):
    return (j // TRIO) * (3 * TRIO) + which * TRIO + j % TRIO


def attend_forward(qkv, kv0, block=1024, chunk=1024):
    rows = qkv.shape[0]
    return call(
        functools.partial(attend_kernel, chunk=chunk, count=rows // chunk),
        (PAIRS, rows // block),
        [
            pl.BlockSpec((block, 128), lambda j, i: (i, column_of(j, 0))),
            pl.BlockSpec((rows, 128), lambda j, i: (0, column_of(j, 1))),
            pl.BlockSpec((rows, 128), lambda j, i: (0, column_of(j, 2))),
            pl.BlockSpec((16, 128), lambda j, i: (0, column_of(j, 1))),
            pl.BlockSpec((16, 128), lambda j, i: (0, column_of(j, 2))),
        ],
        [
            pl.BlockSpec((block, 128), lambda j, i: (i, j)),
            pl.BlockSpec((1, 2, block), lambda j, i: (j, 0, i)),
        ],
        [shape_of((rows, HALF), bf16), shape_of((PAIRS, 2, rows), f32)],
        [],
        (16 * rows * rows * HALF, 5 * rows * D * 2),
        qkv,
        qkv,
        qkv,
        kv0,
        kv0,
    )


def attend_back_kernel(*refs, chunk, count, steps, waits):
    (
        q_ref, g_ref, o_ref, lse_ref, cos_ref, up_ref, down_ref,
        k_ref, v_ref, k0_ref, v0_ref, kcos_ref, kup_ref, kdown_ref,
    ) = refs[:14]
    (
        dq_ref, dk_ref, dv_ref, dk0_ref, dv0_ref, kt, dka, dva, dk0a, dv0a,
    ) = refs[14 + waits :]
    i = pl.program_id(1)

    @pl.when(i == 0)
    def _():
        kt[...] = k_ref[...].T
        dka[...] = jnp.zeros_like(dka)
        dva[...] = jnp.zeros_like(dva)
        dk0a[...] = jnp.zeros_like(dk0a)
        dv0a[...] = jnp.zeros_like(dv0a)

    q = q_ref[...]
    g = g_ref[...]
    rows = q.shape[0]
    lane = lax.broadcasted_iota(jnp.int32, q.shape, 1)
    row = lax.broadcasted_iota(jnp.int32, (16, rows), 0)
    go = (g.astype(f32) * o_ref[...].astype(f32)).T
    k0t = k0_ref[...].T
    dqs = []
    for head in range(2):
        sel = (lane // HD) == head
        low_row, high_row = head * HD, (head + 1) * HD
        qm = jnp.where(sel, q, jnp.zeros_like(q))
        gm = jnp.where(sel, g, jnp.zeros_like(g))
        lse = lse_ref[0, head : head + 1, :]
        delta = jnp.sum(go[low_row:high_row], 0, keepdims=True)
        s = dot_nt(k0_ref[...], qm)
        p = jnp.where(row == 0, jnp.exp(s - lse), 0.0)
        ds = (p * (dot_nt(v0_ref[...], gm) - delta)).astype(bf16)
        dk0a[...] += dot_nn(ds, qm)
        dv0a[...] += dot_nn(p.astype(bf16), gm)
        dq = dot_nn(k0t[low_row:high_row], ds)
        for c in range(count):
            part = pl.ds(c * chunk, chunk)
            p = jnp.exp(dot_nt(k_ref[part], qm) - lse)
            ds = (p * (dot_nt(v_ref[part], gm) - delta)).astype(bf16)
            dva[part] += dot_nn(p.astype(bf16), gm)
            dka[part] += dot_nn(ds, qm)
            dq = dq + dot_nn(kt[low_row:high_row, c * chunk : (c + 1) * chunk], ds)
        dqs.append(dq)
    dq = (jnp.concatenate(dqs, 0).T * HD ** (-0.5)).astype(bf16).astype(f32)
    dq_ref[...] = turn(dq, cos_ref[...], -up_ref[...], -down_ref[...]).astype(bf16)

    @pl.when(i == steps - 1)
    def _():
        dk = dka[...].astype(bf16).astype(f32)
        dk_ref[...] = turn(dk, kcos_ref[...], -kup_ref[...], -kdown_ref[...]).astype(bf16)
        dv_ref[...] = dva[...].astype(bf16)
        dk0_ref[...] = dk0a[...]
        dv0_ref[...] = dv0a[...]


def attend_backward(qkv, g, o, lse, kv0, tables, half, after, block=1024, chunk=512):
    rows = qkv.shape[0]
    first = half * TRIO
    out = pl.BlockSpec((block, 128), lambda j, i: (i, j))
    head = pl.BlockSpec((block, 128), lambda j, i: (i, first + j))
    table = pl.BlockSpec((block, 128), lambda j, i: (i, 0))
    whole_table = pl.BlockSpec((rows, 128), lambda j, i: (0, 0))
    whole = pl.BlockSpec((rows, 128), lambda j, i: (0, j))
    lead = pl.BlockSpec((16, 128), lambda j, i: (0, j))

    def part(size, which):
        return pl.BlockSpec((size, 128), lambda j, i: (0, column_of(first + j, which)))

    return call(
        functools.partial(
            attend_back_kernel,
            chunk=chunk, count=rows // chunk, steps=rows // block, waits=len(after),
        ),
        (TRIO, rows // block),
        [
            pl.BlockSpec((block, 128), lambda j, i: (i, column_of(first + j, 0))),
            head, head,
            pl.BlockSpec((1, 2, block), lambda j, i: (first + j, 0, i)),
            table, table, table,
            part(rows, 1), part(rows, 2), part(16, 1), part(16, 2),
            whole_table, whole_table, whole_table,
        ]
        + [pl.BlockSpec(memory_space=pl.ANY)] * len(after),
        [out, whole, whole, lead, lead],
        [shape_of((rows, THIRD), bf16)] * 3 + [shape_of((16, THIRD), f32)] * 2,
        [
            pltpu.VMEM((128, rows), bf16),
            pltpu.VMEM((rows, 128), f32),
            pltpu.VMEM((rows, 128), f32),
            pltpu.VMEM((16, 128), f32),
            pltpu.VMEM((16, 128), f32),
        ],
        (16 * rows * rows * HALF, 5 * rows * D * 2),
        qkv, g, o, lse, *tables, qkv, qkv, kv0, kv0, *tables, *after,
    )


def prompt_probs(k, qm, mask):
    s = dot_nt(k, qm) * HD ** (-0.5) + mask
    e = jnp.exp(s - jnp.max(s, 0, keepdims=True))
    return e / jnp.sum(e, 0, keepdims=True)


def cross_kernel(q_ref, k_ref, v_ref, mask_ref, o_ref):
    q = q_ref[...]
    lane = lax.broadcasted_iota(jnp.int32, q.shape, 1)
    vt = v_ref[...].T
    outs = []
    for head in range(2):
        qm = jnp.where((lane // HD) == head, q, jnp.zeros_like(q))
        p = prompt_probs(k_ref[...], qm, mask_ref[...])
        outs.append(dot_nn(vt[head * HD : (head + 1) * HD], p.astype(bf16)))
    o_ref[...] = jnp.concatenate(outs, 0).T.astype(bf16)


def cross_back_kernel(
    q_ref, g_ref, k_ref, v_ref, mask_ref, dq_ref, dk_ref, dv_ref, dka, dva, *, steps
):
    i = pl.program_id(1)

    @pl.when(i == 0)
    def _():
        dka[...] = jnp.zeros_like(dka)
        dva[...] = jnp.zeros_like(dva)

    q = q_ref[...]
    g = g_ref[...]
    lane = lax.broadcasted_iota(jnp.int32, q.shape, 1)
    kt = k_ref[...].T
    dqs = []
    for head in range(2):
        sel = (lane // HD) == head
        qm = jnp.where(sel, q, jnp.zeros_like(q))
        gm = jnp.where(sel, g, jnp.zeros_like(g))
        p = prompt_probs(k_ref[...], qm, mask_ref[...])
        dp = dot_nt(v_ref[...], gm)
        ds = (p * (dp - jnp.sum(dp * p, 0, keepdims=True)) * HD ** (-0.5)).astype(bf16)
        dva[...] += dot_nn(p.astype(bf16), gm)
        dka[...] += dot_nn(ds, qm)
        dqs.append(dot_nn(kt[head * HD : (head + 1) * HD], ds))
    dq_ref[...] = jnp.concatenate(dqs, 0).T.astype(bf16)

    @pl.when(i == steps - 1)
    def _():
        dk_ref[...] = dka[...]
        dv_ref[...] = dva[...]


def cross_specs(rows, tokens, block):
    q_spec = pl.BlockSpec((block, 128), lambda j, i: (i, j))
    key_spec = pl.BlockSpec((tokens, 128), lambda j, i: (0, j))
    value_spec = pl.BlockSpec((tokens, 128), lambda j, i: (0, PAIRS + j))
    mask_spec = pl.BlockSpec((tokens, 1), lambda j, i: (0, 0))
    return (q_spec, key_spec, value_spec, mask_spec)


def cross_forward(q, kv, mask, block=1024):
    rows, tokens = (q.shape[0], kv.shape[0])
    q_spec, key_spec, value_spec, mask_spec = cross_specs(rows, tokens, block)
    return call(
        cross_kernel,
        (PAIRS, rows // block),
        [q_spec, key_spec, value_spec, mask_spec],
        q_spec,
        shape_of((rows, HALF), bf16),
        [],
        (16 * rows * tokens * HALF, 4 * rows * D),
        q, kv, kv, mask,
    )


def cross_backward(q, g, kv, mask, block=1024):
    rows, tokens = (q.shape[0], kv.shape[0])
    q_spec, key_spec, value_spec, mask_spec = cross_specs(rows, tokens, block)
    return call(
        functools.partial(cross_back_kernel, steps=rows // block),
        (PAIRS, rows // block),
        [q_spec, q_spec, key_spec, value_spec, mask_spec],
        [q_spec, key_spec, key_spec],
        [
            shape_of((rows, HALF), bf16),
            shape_of((tokens, HALF), f32),
            shape_of((tokens, HALF), f32),
        ],
        [pltpu.VMEM((tokens, 128), f32), pltpu.VMEM((tokens, 128), f32)],
        (32 * rows * tokens * HALF, 8 * rows * D),
        q, g, kv, kv, mask,
    )


def gate_up_kernel(n_ref, wg_ref, wu_ref, hidden_ref, gate_ref, up_ref):
    n = n_ref[...]
    gate = dot_nn(n, wg_ref[...])
    up = dot_nn(n, wu_ref[...])
    hidden_ref[...] = (gate / (1.0 + jnp.exp(-gate)) * up).astype(bf16)
    gate_ref[...] = gate.astype(bf16)
    up_ref[...] = up.astype(bf16)


def gate_up(n, w, block=512, columns=512):
    rows = n.shape[0]
    count = HIDE // columns
    out = pl.BlockSpec((block, columns), lambda j, i: (i, j))
    return call(
        gate_up_kernel,
        (count, rows // block),
        [
            pl.BlockSpec((block, D), lambda j, i: (i, 0)),
            pl.BlockSpec((D, columns), lambda j, i: (0, j)),
            pl.BlockSpec((D, columns), lambda j, i: (0, count + j)),
        ],
        [out, out, out],
        [shape_of((rows, HIDE), bf16)] * 3,
        [],
        (4 * rows * D * HIDE, 8 * rows * HIDE + 4 * D * HIDE),
        n, w, w,
    )


def down_back_kernel(d_ref, w_ref, gate_ref, up_ref, after_ref, dgate_ref, dup_ref):
    for part in range(0, w_ref.shape[0], 256):
        cols = slice(part, part + 256)
        d = dot_nt(d_ref[...], w_ref[cols])
        gate = gate_ref[:, cols].astype(f32)
        sig = 1.0 / (1.0 + jnp.exp(-gate))
        d_sig = d * sig
        dgate_ref[:, cols] = (d_sig * up_ref[:, cols] * (1.0 + gate * (1.0 - sig))).astype(bf16)
        dup_ref[:, cols] = (d_sig * gate).astype(bf16)


def down_back(d, w, gate, up, after, block=512, columns=1024):
    rows = d.shape[0]
    out = pl.BlockSpec((block, columns), lambda j, i: (i, j))
    return call(
        down_back_kernel,
        (HIDE // columns, rows // block),
        [
            pl.BlockSpec((block, D), lambda j, i: (i, 0)),
            pl.BlockSpec((columns, D), lambda j, i: (j, 0)),
            out,
            out,
            pl.BlockSpec(memory_space=pl.ANY),
        ],
        [out, out],
        [shape_of((rows, HIDE), bf16)] * 2,
        [],
        (2 * rows * D * HIDE, 10 * rows * HIDE + 2 * D * HIDE),
        d, w, gate, up, after,
    )


def chip_sum_kernel(*refs, inputs, jobs, planes):
    ins, outs = (refs[:inputs], refs[inputs : 2 * inputs])
    scratch = list(refs[2 * inputs : -3])
    send_sem, recv_sem, local_sem = refs[-3:]
    s_at, z_at = (lax.axis_index("seq"), lax.axis_index("z"))
    y_at, x_at = (s_at // 2, s_at % 2)
    y_mate = (1 - y_at) * 2 + x_at
    x_mate = y_at * 2 + (1 - x_at)
    z_mates = [(z_at + offset) % planes for offset in range(1, planes)]
    z_froms = [(z_at + planes - offset) % planes for offset in range(1, planes)]
    barrier = pltpu.get_barrier_semaphore()
    for mate in (y_mate, x_mate):
        pl.semaphore_signal(
            barrier, inc=1, device_id={"seq": mate}, device_id_type=pl.DeviceIdType.MESH
        )
    for mate in z_mates:
        pl.semaphore_signal(
            barrier, inc=1, device_id={"z": mate}, device_id_type=pl.DeviceIdType.MESH
        )
    pl.semaphore_wait(barrier, 1 + planes)

    def remote(job, which, source, target, device):
        copy = pltpu.make_async_remote_copy(
            src_ref=source,
            dst_ref=target,
            send_sem=send_sem.at[job, which],
            recv_sem=recv_sem.at[job, which],
            device_id=device,
            device_id_type=pl.DeviceIdType.MESH,
        )
        copy.start()
        return copy

    def along_z(job, source, received):
        return [
            remote(job, 2 + n, source.at[mate], received.at[n], {"z": mate})
            for n, mate in enumerate(z_mates)
        ]

    state = []
    copies = []
    for n, (full, at, low_col, width, y_first) in enumerate(jobs):
        cols = pl.ds(low_col, width)
        if full:
            own, first, second, third = (scratch.pop(0) for _ in range(4))
            view = ins[at].at[:, :, :, :, cols]
            given = view.at[1 - y_at] if y_first else view.at[:, 1 - x_at]
            kept = view.at[y_at] if y_first else view.at[:, x_at]
            mate = {"seq": y_mate if y_first else x_mate}
            moving = [remote(n, 0, given, first, mate)]
        else:
            own, third = (scratch.pop(0) for _ in range(2))
            first, second = (None, None)
            view = ins[at].at[:, :, cols]
            kept = view.at[z_at]
            moving = along_z(n, view, third)
        local = pltpu.make_async_copy(kept, own, local_sem.at[n])
        local.start()
        copies += moving
        state.append((own, first, second, third, local, moving))

    waiting = []
    for n, (full, at, low_col, width, y_first) in enumerate(jobs):
        own, first, second, third, local, moving = state[n]
        local.wait()
        if not full:
            waiting.append(moving)
            continue
        moving[0].wait_recv()

        def add_first(i, carry):
            half, plane = (i // planes, i % planes)
            own[half, plane] = (
                own[half, plane].astype(f32) + first[half, plane].astype(f32)
            ).astype(bf16)
            return carry

        lax.fori_loop(0, 2 * planes, add_first, 0)
        here = x_at if y_first else y_at
        mate = {"seq": x_mate if y_first else y_mate}
        copy = remote(n, 1, own.at[1 - here], second, mate)
        copies.append(copy)
        waiting.append([copy])
    for n, (full, at, low_col, width, y_first) in enumerate(jobs):
        if not full:
            continue
        own, first, second, third, local, moving = state[n]
        here = x_at if y_first else y_at
        waiting[n][0].wait_recv()

        def add_second(plane, carry):
            second[plane] = (
                own[here, plane].astype(f32) + second[plane].astype(f32)
            ).astype(bf16)
            return carry

        lax.fori_loop(0, planes, add_second, 0)
        waiting[n] = along_z(n, second, third)
        copies += waiting[n]
    for n, (full, at, low_col, width, y_first) in enumerate(jobs):
        own, first, second, third, local, moving = state[n]
        for copy in waiting[n]:
            copy.wait_recv()
        total = (second[z_at] if full else own[...]).astype(f32)
        for m in range(planes - 1):
            total = total + third[m].astype(f32)
        outs[at][:, low_col : low_col + width] = total
    for copy in copies:
        copy.wait_send()


def chip_sums(arrays, jobs, planes):
    scratch = []
    for full, at, _, width, _ in jobs:
        rows = arrays[at].shape[-2]
        if full:
            scratch += [pltpu.VMEM((2, planes, rows, width), bf16)] * 2
            scratch += [pltpu.VMEM((planes, rows, width), bf16)]
        else:
            scratch += [pltpu.VMEM((rows, width), bf16)]
        scratch += [pltpu.VMEM((planes - 1, rows, width), bf16)]
    count = len(jobs)
    scratch += [
        pltpu.SemaphoreType.DMA((count, 1 + planes)),
        pltpu.SemaphoreType.DMA((count, 1 + planes)),
        pltpu.SemaphoreType.DMA((count,)),
    ]
    return pl.pallas_call(
        functools.partial(chip_sum_kernel, inputs=len(arrays), jobs=jobs, planes=planes),
        in_specs=[pl.BlockSpec(memory_space=pl.ANY)] * len(arrays),
        out_specs=[pl.BlockSpec(memory_space=pltpu.VMEM)] * len(arrays),
        out_shape=[shape_of(x.shape[-2:], f32) for x in arrays],
        scratch_shapes=scratch,
        cost_estimate=pl.CostEstimate(flops=10**11, bytes_accessed=10**7, transcendentals=0),
        compiler_params=pltpu.CompilerParams(
            vmem_limit_bytes=56 << 20, collective_id=0, has_side_effects=True
        ),
    )(*arrays)


def chip_body(
    latents, noise_draw, audio_len, bucket, timing, prompt, prompt_len, step_count,
    edge_weight, edge_first, edge_second,
    attend_weight, attend_first, attend_second,
    square_weight, square_first, square_second,
    cross_weight, cross_first, cross_second,
    upward_weight, upward_first, upward_second,
    down_weight, down_first, down_second,
    gain_weight, gain_first, gain_second,
    *, planes, chips,
):
    peers = ("seq", "z")
    many = planes * chips
    groups = latents.shape[0]
    clips = groups * 2 * planes
    frames = latents.shape[1] * chips
    own = frames // 2
    s_at, z_at, k_at = (lax.axis_index("seq"), lax.axis_index("z"), lax.axis_index("core"))
    device = (s_at * planes + z_at) * 2 + k_at
    first_core = k_at == 0

    def swap(x):
        return lax.ppermute(x, "core", [(0, 1), (1, 0)])

    def across(x, axis, size, bit):
        return lax.ppermute(x, axis, [(i, i ^ bit) for i in range(size)])

    def bits(size):
        found = []
        bit = size // 2
        while bit:
            found.append(bit)
            bit //= 2
        return found

    hops = [("z", planes, b) for b in bits(planes)] + [("seq", chips, b) for b in bits(chips)]

    def in_order(mine, other, axis=0):
        return jnp.where(
            first_core,
            jnp.concatenate([mine, other], axis),
            jnp.concatenate([other, mine], axis),
        )

    def pick(x, index, axis):
        return lax.dynamic_index_in_dim(x, index, axis, keepdims=False)

    def halves_of(x, view, axis):
        x = x.reshape(view)
        rows = view[0]
        return (
            pick(x, k_at, axis).reshape(rows, -1),
            pick(x, 1 - k_at, axis).reshape(rows, -1),
        )

    def tie(x):
        return x.reshape(-1, x.shape[-1])[0, 0].astype(f32) * 0.0

    y_at, x_at = (s_at // 2, s_at % 2)

    def gather_chips(x, parts):
        piece = x.shape[0] // parts
        shape = (planes, piece, x.shape[1])
        total = jnp.zeros((2, 2, parts) + shape, x.dtype).swapaxes(2, 3)

        def put(total, block, y, column, z, part):
            return lax.dynamic_update_slice(
                total, block[None, None, :, None], (y, column, z, part, 0, 0)
            )

        for part in range(parts):
            mine = x[part * piece : (part + 1) * piece]
            block = lax.dynamic_update_slice(jnp.zeros(shape, x.dtype), mine[None], (z_at, 0, 0))
            for offset in range(1, planes):
                taken = across(mine, "z", planes, offset)
                block = lax.dynamic_update_slice(block, taken[None], (z_at ^ offset, 0, 0))
            from_x, from_y = (across(block, "seq", chips, 1), across(block, "seq", chips, 2))
            half = planes // 2
            first = across(from_y[:half], "seq", chips, 1)
            second = across(from_x[half:], "seq", chips, 2)
            for taken, y, column, z in (
                (block, y_at, x_at, 0),
                (from_x, y_at, 1 - x_at, 0),
                (from_y, 1 - y_at, x_at, 0),
                (first, 1 - y_at, 1 - x_at, 0),
                (second, 1 - y_at, 1 - x_at, half),
            ):
                total = put(total, taken, y, column, z, part)
        return (total.reshape(-1, x.shape[1]), block, from_x)

    rows = attend_weight.shape[0]
    attend_view = (rows, 2, 3, 2, THIRD)
    square_view = (rows, 3, 2, HALF)
    cross_view = (cross_weight.shape[0], 2, 2, HALF)
    up_view = (rows, 2, many, 2, FF // (2 * many))
    attend16 = attend_weight.astype(bf16).reshape(rows, 3, 2, 2, THIRD).transpose(0, 3, 1, 2, 4)
    edge16 = jnp.concatenate(
        [edge_weight[: 2 * C].astype(bf16), gain_weight.astype(bf16)], 0
    ).T
    edge16 = jnp.pad(edge16, ((0, 0), (0, 256 - edge16.shape[1])))
    mine, other = halves_of(attend16, attend_view, 3)
    mine, other = (jnp.concatenate([mine, edge16], 1), jnp.concatenate([other, edge16], 1))
    first_group = lax.all_gather(in_order(mine, swap(other)), peers, axis=0, tiled=True)
    mine, other = halves_of(
        square_weight[:3].astype(bf16).transpose(1, 0, 2), square_view, 2
    )
    square_mine = in_order(mine, swap(other))
    mine, other = halves_of(cross_weight.astype(bf16), cross_view, 2)
    cross_mine = in_order(mine, swap(other))
    cross_mine = jnp.concatenate([cross_mine[:, :HALF], cross_mine[:, HALF:]], 0)
    square_cols = gather_chips(jnp.concatenate([square_mine, cross_mine], 1), 1)[0]
    mine, other = halves_of(upward_weight.astype(bf16), up_view, 3)
    up_w = lax.all_gather(in_order(mine, swap(other)), peers, axis=0, tiled=True)
    down_w = lax.all_gather(down_weight.astype(bf16), peers, axis=0, tiled=True)

    attend_w = first_group[:, : 3 * HALF]
    w_in_t = first_group[:, 3 * HALF : 3 * HALF + C]
    w_out_t = first_group[:, 3 * HALF + C : 3 * HALF + 2 * C]
    norm_gains = first_group[:, 3 * HALF + 2 * C : 3 * HALF + 2 * C + 4].astype(f32).T

    def rows_half(columns):
        mine_rows = lax.dynamic_slice_in_dim(columns, k_at * HALF, HALF, 0)
        other_rows = lax.dynamic_slice_in_dim(columns, (1 - k_at) * HALF, HALF, 0)
        return in_order(mine_rows, swap(other_rows), 1)

    local = jnp.stack(
        [audio_len, bucket, timing[:, 0], timing[:, 1], prompt_len], 1
    ).astype(f32)
    clip_index = jnp.arange(clips)
    place = (clip_index // groups) == (z_at * 2 + k_at)
    scalars = jnp.where(place[:, None], jnp.tile(local, (clips // groups, 1)), 0.0)
    scalars = scalars + swap(scalars)
    for b in bits(planes):
        scalars = scalars + across(scalars, "z", planes, b)
    order = (z_at ^ (clip_index // chips)) * chips + (s_at ^ (clip_index % chips))
    chosen = order[:, None] == clip_index[None, :]
    scalars = jnp.sum(jnp.where(chosen[:, :, None], scalars[None], 0.0), 1)
    lengths = scalars[:, 0]
    t, keep_rates, noise_rates, clip_weights = plan(scalars[:, 1])
    weight_sum = jnp.sum(clip_weights * lengths)
    keep_rate, noise_rate, clip_weight = (keep_rates[0], noise_rates[0], clip_weights[0])

    t_feat = time_features(t).astype(bf16)
    z_feat = timing_features(scalars[:, 2:4]).astype(bf16)
    w_t1 = edge_weight[2 * C : 2 * C + TF].astype(bf16)
    w_t2 = square_weight[3].astype(bf16)
    w_timing = edge_weight[2 * C + TF :].astype(bf16)
    t_pre = dot_nn(t_feat, w_t1)
    t_hidden = jax.nn.silu(t_pre).astype(bf16)
    lead = lax.dynamic_update_slice(
        jnp.zeros((clips, D), f32), dot_nn(z_feat, w_timing), (0, device * rows)
    ) + dot_nn(t_hidden, w_t2)
    for axis, size, bit in hops:
        count = lead.shape[0] // 2
        lead = lead[:count] + across(lead[count:], axis, size, bit)
    lead = lead + swap(lead)
    prefix_normed, prefix_std, prefix_dev = layer_normalize(lead, norm_gains[0])
    n_prefix = jnp.pad(prefix_normed.astype(bf16), ((0, 15), (0, 0)))
    kv_prefix = dot_nn(n_prefix, attend_w).astype(bf16)

    part = s_at // groups
    member = s_at % groups
    both = jnp.stack([latents, noise_draw])
    blocks = [pick(both, member, 1)]
    for offset in range(1, chips):
        given = pick(both, (s_at ^ offset) % groups, 1)
        blocks.append(across(given, "seq", chips, offset))
    blocks = jnp.stack(blocks, 1)
    blocks = jnp.where(part == k_at, blocks, swap(blocks))
    seen = s_at ^ jnp.arange(chips)

    def mine_first(x, axis):
        low_half, high_half = jnp.split(x, 2, axis)
        return in_order(low_half, high_half, axis)

    clip = mine_first(blocks, 1).reshape(2, frames, C).astype(f32)
    clean, noisy_part = (clip[0], clip[1])
    positions = (
        mine_first(seen, 0)[:, None] * latents.shape[1] + jnp.arange(latents.shape[1])
    ).reshape(frames)
    row_weight = clip_weight * (positions[:own].astype(f32) < lengths[0]).astype(f32)
    local_prompt = pick(prompt, member, 0)
    other_prompt = swap(local_prompt)
    prompt_low = jnp.where(part == k_at, local_prompt, other_prompt)
    tokens = prompt_low.shape[0]
    mask = jnp.where(
        jnp.arange(tokens)[:, None].astype(f32) < scalars[0, 4], 0.0, -1000000000.0
    ).astype(f32)

    def shared_sum(product):
        given = product(1).astype(bf16)
        return product(0) + swap(given).astype(f32)

    def cut(x, which):
        return x[which * own : (which + 1) * own]

    def both_halves(x):
        return jnp.concatenate([x, swap(x)], 0)

    x_in = (keep_rate * clean + noise_rate * noisy_part).astype(bf16)
    x_wide = jnp.pad(x_in, ((0, 0), (0, C)))
    h0, n1 = start_forward(x_wide, first_group, norm_gains[:1])
    tables = turn_tables(positions + 1)
    qkv = qkv_project(n1, first_group, tables)
    o, lse = attend_forward(qkv, kv_prefix)

    square_cols = square_cols + tie(o).astype(bf16)
    cross_w = square_cols[:, 3 * HALF :].reshape(many, 2, CROSS // many, HALF)
    cross_w = jnp.concatenate(
        [cross_w[:, 0].reshape(CROSS, HALF), cross_w[:, 1].reshape(CROSS, HALF)], 1
    )
    w_o = rows_half(square_cols[:, :HALF])
    w_cq = square_cols[:, HALF : 2 * HALF]
    w_co = rows_half(square_cols[:, 2 * HALF : 3 * HALF])

    h1 = h0 + shared_sum(lambda i: dot_nn(cut(o, i), w_o))
    n2 = both_halves(layer_normalize(h1, norm_gains[1])[0].astype(bf16))
    cross_q = dot_nn(n2, w_cq).astype(bf16)
    cross_kv = dot_nn(prompt_low, cross_w).astype(bf16)
    co = cross_forward(cross_q, cross_kv, mask)
    h2 = h1 + shared_sum(lambda i: dot_nn(cut(co, i), w_co))
    n3 = both_halves(layer_normalize(h2, norm_gains[2])[0].astype(bf16))
    hidden, gate, upper = gate_up(n3, up_w)
    h3 = h2 + shared_sum(lambda i: dot_nn(cut(hidden, i), down_w))
    n4, std4, dev4 = layer_normalize(h3, norm_gains[3])
    n4 = n4.astype(bf16)
    predicted = dot_nn(n4, w_out_t)
    target = keep_rate * noisy_part[:own] - noise_rate * clean[:own]
    error = predicted - target
    loss_local = jnp.sum(row_weight[:, None] * error * error)

    d_pred = (2.0 / (C * weight_sum) * row_weight[:, None] * error).astype(bf16)
    g_out_t = dot_tn(n4, d_pred)
    d_h, gain4 = norm_backward(dot_nt(d_pred, w_out_t), std4, dev4, norm_gains[3])
    d_f = both_halves(d_h.astype(bf16))

    def half_at(x, at, size):
        return lax.dynamic_slice_in_dim(x, at * size, size, 0)

    class Scatter:
        def __init__(self, product, depth, y_first):
            self.product, self.quarter, self.y_first = (product, depth // chips, y_first)
            self.bit, self.later, self.at = (2, 1, x_at) if y_first else (1, 2, y_at)
            given = product(lambda x, axis: self.rows_at(x, axis, True)).astype(bf16)
            self.sent = [given]
            self.taken = across(given, "seq", chips, self.bit)

        def rows_at(self, x, axis, flip):
            quarter = self.quarter

            def block(at):
                return lax.dynamic_slice_in_dim(x, at * quarter, quarter, axis)

            if self.y_first:
                row = (1 - y_at if flip else y_at) * 2
                return lax.dynamic_slice_in_dim(x, row * quarter, 2 * quarter, axis)
            column = 1 - x_at if flip else x_at
            return jnp.concatenate([block(column), block(2 + column)], axis)

        def second(self, behind=0.0):
            own_part = self.product(lambda x, axis: self.rows_at(x, axis, False))
            kept = (own_part + self.taken.astype(f32) + behind).astype(bf16)
            given = half_at(kept, 1 - self.at, self.quarter)
            self.kept = half_at(kept, self.at, self.quarter)
            self.sent = [given]
            self.taken = across(given, "seq", chips, self.later)
            return self

        def folded(self, behind):
            kept = (self.kept.astype(f32) + self.taken.astype(f32) + behind).astype(bf16)
            return kept.reshape(planes, -1, kept.shape[1])

    def gradient(left, right, y_first):
        return Scatter(lambda cut_of: dot_tn(cut_of(left, 1), right), left.shape[1], y_first)

    def gathered_sum(g):
        return lax.psum_scatter(g, peers, scatter_dimension=0, tiled=True)

    g_down = dot_tn(hidden, d_f).astype(bf16)
    s_down = gathered_sum(g_down)
    d_gate, d_up = down_back(d_f, down_w, gate, upper, g_down)
    s_gate = gathered_sum(dot_tn(n3, d_gate).astype(bf16))
    s_upper = gathered_sum(dot_tn(n3, d_up).astype(bf16))
    d_n3 = shared_sum(
        lambda i: dot_nt(cut(d_gate, i), up_w[:, :HIDE]) + dot_nt(cut(d_up, i), up_w[:, HIDE:])
    )

    def norm_again(d_n, h, gain):
        _, std, dev = layer_normalize(h, gain)
        return norm_backward(d_n, std, dev, gain)

    d_part, gain3 = norm_again(d_n3, h2, norm_gains[2])
    d_h = d_h + d_part
    d_c = both_halves(d_h.astype(bf16))
    g_co = dot_tn(co, d_c).astype(bf16)
    d_co = dot_nt(d_c, w_co).astype(bf16)
    d_cq, d_ck, d_cv = cross_backward(cross_q, d_co, cross_kv, mask)
    r_cross = gradient(prompt_low, jnp.concatenate([d_ck, d_cv], 1).astype(bf16), False)
    r_cq = gradient(n2, d_cq, False)
    d_n2 = shared_sum(lambda i: dot_nt(cut(d_cq, i), w_cq))
    d_part, gain2 = norm_again(d_n2, h1, norm_gains[1])
    d_h = d_h + d_part
    d_a = both_halves(d_h.astype(bf16))
    g_o = dot_tn(o, d_a).astype(bf16)

    def columns_half(g):
        kept = lax.dynamic_slice_in_dim(g, k_at * HALF, HALF, 1)
        given = lax.dynamic_slice_in_dim(g, (1 - k_at) * HALF, HALF, 1)
        return in_order(kept, swap(given), 0)

    side = jnp.concatenate([columns_half(g_o), columns_half(g_co)], 1)
    r_side = Scatter(lambda cut_of: cut_of(side, 0).astype(f32), D, True)
    d_o = dot_nt(d_a, w_o).astype(bf16)
    lead_column = n_prefix[:1].astype(f32)

    def attend_half(half, after):
        d_q, d_k, d_v, d_k0, d_v0 = attend_backward(qkv, d_o, o, lse, kv_prefix, tables, half, after)
        lead_row = jnp.concatenate([jnp.zeros_like(d_k0), d_k0, d_v0], 1)
        return (jnp.concatenate([d_q, d_k, d_v], 1), lead_row, tie(d_q))

    def attend_gradient(right, lead_row):
        return (dot_tn(n1, right) + lead_column.T * lead_row[:1]).astype(bf16)

    after = [x for r in (r_cross, r_cq, r_side) for x in r.sent]
    d_first, lead_first, behind_first = attend_half(0, after)
    g_first = attend_gradient(d_first, lead_first)
    for r in (r_cross, r_cq, r_side):
        r.second(behind_first)
    after = [x for r in (r_cross, r_cq, r_side) for x in r.sent] + [g_first]
    d_second, lead_second, behind_second = attend_half(1, after)
    g_second = attend_gradient(d_second, lead_second)
    d_n1 = shared_sum(
        lambda i: dot_nt(cut(d_first, i), attend_w[:, : 3 * THIRD])
        + dot_nt(cut(d_second, i), attend_w[:, 3 * THIRD :])
    )
    d_part, gain1 = norm_again(d_n1, h0, norm_gains[0])
    d_h = d_h + d_part
    g_in_t = dot_tn(d_h.astype(bf16), x_in[:own])
    short = [r.folded(behind_second) for r in (r_cross, r_cq, r_side)]
    d_kv0 = jnp.concatenate([lead_first, lead_second], 1)

    high = d_kv0.astype(bf16)
    rest = (d_kv0 - high.astype(f32)).astype(bf16)
    d_np = dot_nt(jnp.concatenate([high, rest], 0), attend_w)
    d_np = d_np[:1] + d_np[16:17]
    d_np = d_np + swap(d_np)
    d_lead, prefix_gain = norm_backward(d_np, prefix_std, prefix_dev, norm_gains[0])

    def to_owner(x, view, axis):
        count = x.shape[0] // 2
        kept = lax.dynamic_slice_in_dim(x, k_at * count, count, 0)
        given = lax.dynamic_slice_in_dim(x, (1 - k_at) * count, count, 0)
        taken = swap(given.astype(bf16)).astype(f32)
        shape = view[:axis] + view[axis + 1 :]
        joined = jnp.where(
            first_core,
            jnp.stack([kept.reshape(shape), taken.reshape(shape)], axis),
            jnp.stack([taken.reshape(shape), kept.reshape(shape)], axis),
        )
        return joined

    gains = jnp.stack([gain1 + 0.5 * prefix_gain, gain2, gain3, gain4], 1)
    edges = jnp.concatenate([g_in_t, g_out_t], 1)
    gains = jnp.pad(gains, ((0, 0), (0, 128 - gains.shape[1])))
    edges = jnp.where(first_core, edges, gains) + swap(jnp.where(first_core, gains, edges))

    def blocks_of(g):
        return g.astype(bf16).reshape(2, 2, planes, -1, g.shape[1])

    wide, narrow = (5 * 128, 4 * 128)
    jobs = (
        (True, 0, 0, wide, True),
        (True, 0, wide, narrow, False),
        (True, 1, 0, wide, False),
        (True, 1, wide, narrow, True),
        (True, 2, 0, 128, True),
        (False, 3, 0, 2 * HALF, True),
        (False, 4, 0, HALF, True),
        (False, 5, 0, 2 * HALF, True),
    )
    s_first, s_second, s_edge, s_cross, s_cq, s_side = chip_sums(
        [blocks_of(g_first), blocks_of(g_second), blocks_of(edges)] + short, jobs, planes
    )
    s_square = jnp.concatenate([s_side[:, :HALF], s_cq, s_side[:, HALF:]], 1)
    s_attend = jnp.concatenate([s_first, s_second], 1)
    s_edge = to_owner(s_edge, (rows, 2, 128), 1).reshape(rows, 256)

    d_lead = d_lead + tie(s_first)
    for axis, size, bit in reversed(hops):
        d_lead = jnp.concatenate([d_lead, across(d_lead, axis, size, bit)], 0)
    g_t2 = exact("ge,gd->ed", t_hidden.astype(f32), d_lead)
    d_lead_here = lax.dynamic_slice(d_lead, (0, device * rows), (clips, rows))
    g_timing = exact("gz,gd->zd", z_feat.astype(f32), d_lead_here)
    d_t_hidden = exact("gd,ed->ge", d_lead, w_t2.astype(f32))
    t_sig = jax.nn.sigmoid(t_pre)
    d_t_pre = d_t_hidden * t_sig * (1.0 + t_pre * (1.0 - t_sig))
    g_t1 = exact("gz,gd->zd", t_feat.astype(f32), d_t_pre)
    g_attend = to_owner(s_attend, attend_view, 3).transpose(0, 2, 3, 1, 4).reshape(rows, 3 * D)
    g_square = to_owner(s_square, square_view, 2).reshape(rows, 3, D).transpose(1, 0, 2)
    g_square = jnp.concatenate([g_square, g_t2[None]], 0)
    g_cross = to_owner(s_cross, cross_view, 2).reshape(cross_view[0], 2 * D)
    g_up = to_owner(jnp.concatenate([s_gate.astype(f32), s_upper.astype(f32) + tie(s_first)], 1), up_view, 3).reshape(rows, 2 * FF)
    g_down = s_down.astype(f32)
    g_edge = jnp.concatenate([s_edge[:, : 2 * C].T, g_t1, g_timing], 0)
    g_gain = s_edge[:, 2 * C : 2 * C + 4].T
    sharded = lax.optimization_barrier(
        (g_edge, g_attend, g_square, g_cross, g_up, g_down, g_gain)
    )
    g_gain = sharded[6]
    totals = jnp.stack([sum(jnp.sum(g * g) for g in sharded), loss_local])
    totals = totals + swap(totals)
    for axis, size, bit in hops:
        totals = totals + across(totals, axis, size, bit)
    grad_norm = jnp.sqrt(totals[0])
    loss_value = totals[1] / (C * weight_sum)
    factor = jnp.minimum(1.0, clip_norm / grad_norm)
    count = step_count[0].astype(f32)
    first_fix = 1.0 - 0.9**count
    second_fix = 1.0 - 0.999**count
    states = (
        (edge_weight, edge_first, edge_second),
        (attend_weight, attend_first, attend_second),
        (square_weight, square_first, square_second),
        (cross_weight, cross_first, cross_second),
        (upward_weight, upward_first, upward_second),
        (down_weight, down_first, down_second),
        (gain_weight, gain_first, gain_second),
    )
    out = [
        adam(w, m, v, g * factor, first_fix, second_fix)
        for (w, m, v), g in zip(states, sharded)
    ]
    flat = [x for triple in out[:6] for x in triple]
    return (loss_value, grad_norm, *flat, g_gain * factor, out[6][1], out[6][2])


def solution(mesh):
    chips, spread = (mesh.shape["seq"], mesh.shape["dp"])
    split_mesh = Mesh(mesh.devices.reshape(chips, spread // 2, 2), ("seq", "z", "core"))

    def whole(*args):
        groups = args[0].shape[0] // spread
        one_clip_per_chip = groups * 2 == chips == 4 and spread & (spread - 1) == 0
        if one_clip_per_chip:
            inner = functools.partial(chip_body, planes=spread // 2, chips=chips)
            dp, used = ("z", "core"), split_mesh
        else:
            inner, dp, used = (general_body, "dp", mesh)
        every = ("seq",) + (dp if isinstance(dp, tuple) else (dp,))
        by_row, by_column, by_middle = (P(every, None), P(None, every), P(None, every, None))
        frames = P(dp, "seq", None)
        clip = P(dp)
        kinds = (by_column, by_row, by_middle, by_row, by_row, by_row, by_column)
        weights = tuple(kind for kind in kinds for _ in range(3))
        return jax.shard_map(
            inner,
            mesh=used,
            in_specs=(frames, frames, clip, clip, P(dp, None), P(dp, None, None), clip, P())
            + weights,
            out_specs=(P(), P()) + weights,
            check_vma=False,
        )(*args)

    return whole
```

```python
import functools
import math

import jax
import jax.numpy as jnp
from jax import lax
from jax.experimental import pallas as pl
from jax.experimental.pallas import tpu as pltpu
from jax.sharding import Mesh
from jax.sharding import PartitionSpec as P

D = 1536
H = 24
HD = 64
FF = 6144
C = 64
TF = 256
PT = 128
NB = 1000


highest = lax.Precision.HIGHEST
clip_norm = 0.002
learn_rate = 0.1
weight_decay = 0.1
rot_width = 32


def layer_normalize(h, norm_gain):
    centered_input = h - jnp.mean(h, -1, keepdims=True)
    inverse_deviation = lax.rsqrt(
        jnp.mean(centered_input * centered_input, -1, keepdims=True) + 1e-05
    )
    standardized = centered_input * inverse_deviation
    return (standardized * norm_gain, standardized, inverse_deviation)


def norm_backward(incoming_gradient, standardized, inverse_deviation, norm_gain):
    scaled_gradient = incoming_gradient * norm_gain
    gain_gradient = jnp.sum(incoming_gradient * standardized, 0)
    d_in = inverse_deviation * (
        scaled_gradient
        - jnp.mean(scaled_gradient, -1, keepdims=True)
        - standardized * jnp.mean(scaled_gradient * standardized, -1, keepdims=True)
    )
    return (d_in, gain_gradient)


def plan(bucket):
    t = (bucket.astype(jnp.float32) + 0.5) / NB
    keep_rate = jnp.cos(t * (math.pi / 2))
    noise_rate = jnp.sin(t * (math.pi / 2))
    snr_ratio = keep_rate * keep_rate / (noise_rate * noise_rate)
    return (t, keep_rate, noise_rate, jnp.minimum(snr_ratio, 5.0) / (snr_ratio + 1.0))


def time_features(t):
    freqs = jnp.exp(-math.log(10000.0) * jnp.arange(TF // 2, dtype=jnp.float32) / (TF // 2))
    angle = t[:, None] * 1000.0 * freqs[None, :]
    return jnp.concatenate([jnp.cos(angle), jnp.sin(angle)], -1)


def timing_features(timing):
    seconds = timing.astype(jnp.float32) / 64.0
    return jnp.concatenate([time_features(seconds[:, 0]), time_features(seconds[:, 1])], -1)


def rope_tables(positions):
    inverse = 10000.0 ** (-2.0 * jnp.arange(rot_width // 2, dtype=jnp.float32) / rot_width)
    angle = positions[:, None].astype(jnp.float32) * inverse[None, :]
    angle = jnp.concatenate([angle, angle], -1)
    return (jnp.cos(angle), jnp.sin(angle))


def rotate(x):
    half = rot_width // 2
    return jnp.concatenate([-x[..., half:], x[..., :half]], -1)


def apply_rope(x, cosine, sine_part):
    turned = x[..., :rot_width]
    turned = turned * cosine[None, :, None, :] + rotate(turned) * sine_part[None, :, None, :]
    return jnp.concatenate([turned, x[..., rot_width:]], -1)


def rope_back(incoming_gradient, cosine, sine_part):
    turned = incoming_gradient[..., :rot_width]
    turned = turned * cosine[None, :, None, :] - rotate(turned * sine_part[None, :, None, :])
    return jnp.concatenate([turned, incoming_gradient[..., rot_width:]], -1)


def split_blocks(x, count, block):
    return x.reshape((x.shape[0], count, block) + x.shape[2:]).swapaxes(0, 1)


def join_blocks(x):
    x = x.swapaxes(0, 1)
    return x.reshape((x.shape[0], x.shape[1] * x.shape[2]) + x.shape[3:])


def attend(q, keys, values):
    rows_q = q.shape[1]
    block = min(512, rows_q)
    count = rows_q // block
    score_scale = HD ** (-0.5)

    def one_block(q_block):
        s = (
            jnp.einsum("ibd,ikd->ibk", q_block, keys, preferred_element_type=jnp.float32)
            * score_scale
        )
        top = jnp.max(s, -1, keepdims=True)
        lse = top + jnp.log(jnp.sum(jnp.exp(s - top), -1, keepdims=True))
        p = jnp.exp(s - lse)
        o = jnp.einsum(
            "ibk,ikd->ibd", p.astype(jnp.bfloat16), values, preferred_element_type=jnp.float32
        )
        return (o, lse[..., 0])

    outs, lses = lax.map(one_block, split_blocks(q, count, block))
    return (join_blocks(outs), join_blocks(lses))


def attend_back(q, keys, values, lse, grad_o):
    rows_q = q.shape[1]
    block = min(512, rows_q)
    count = rows_q // block
    score_scale = HD ** (-0.5)

    def one_block(carry, parts):
        d_key, d_value = carry
        q_block, g_block, l_block = parts
        s = (
            jnp.einsum("ibd,ikd->ibk", q_block, keys, preferred_element_type=jnp.float32)
            * score_scale
        )
        p = jnp.exp(s - l_block[..., None])
        d_prob = jnp.einsum("ibd,ikd->ibk", g_block, values, preferred_element_type=jnp.float32)
        d_value = d_value + jnp.einsum(
            "ibk,ibd->ikd", p.astype(jnp.bfloat16), g_block, preferred_element_type=jnp.float32
        )
        d_score = (p * (d_prob - jnp.sum(d_prob * p, -1, keepdims=True)) * score_scale).astype(
            jnp.bfloat16
        )
        d_query = jnp.einsum("ibk,ikd->ibd", d_score, keys, preferred_element_type=jnp.float32)
        d_key = d_key + jnp.einsum(
            "ibk,ibd->ikd", d_score, q_block, preferred_element_type=jnp.float32
        )
        return ((d_key, d_value), d_query)

    zeros = jnp.zeros(keys.shape, jnp.float32)
    parts = (
        split_blocks(q, count, block),
        split_blocks(grad_o, count, block),
        split_blocks(lse, count, block),
    )
    (d_key, d_value), d_queries = lax.scan(one_block, (zeros, zeros), parts)
    return (join_blocks(d_queries), d_key, d_value)


def adam(w, m, v, g, first_fix, second_fix):
    first = 0.9 * m + 0.1 * g
    second = 0.999 * v + 0.001 * g * g
    new = w - learn_rate * (
        first / first_fix / (jnp.sqrt(second / second_fix) + 1e-08) + weight_decay * w
    )
    return (new, first, second)


def exact(form, a, b):
    return jnp.einsum(form, a, b, precision=highest, preferred_element_type=jnp.float32)


def general_body(
    latents,
    noise_draw,
    audio_len,
    bucket,
    timing,
    prompt,
    prompt_len,
    step_count,
    edge_weight,
    edge_first,
    edge_second,
    attend_weight,
    attend_first,
    attend_second,
    square_weight,
    square_first,
    square_second,
    cross_weight,
    cross_first,
    cross_second,
    upward_weight,
    upward_first,
    upward_second,
    down_weight,
    down_first,
    down_second,
    gain_weight,
    gain_first,
    gain_second,
):
    low_type = jnp.bfloat16
    wide = jnp.float32
    groups, frames = (latents.shape[0], latents.shape[1])
    total_rows = groups * frames
    items = groups * H
    edge16, attend16, square16, cross16, upward16, down16, gain16 = (
        lax.all_gather(edge_weight.astype(low_type), ("seq", "dp"), axis=1, tiled=True),
        lax.all_gather(attend_weight.astype(low_type), ("seq", "dp"), axis=0, tiled=True),
        lax.all_gather(square_weight.astype(low_type), ("seq", "dp"), axis=1, tiled=True),
        lax.all_gather(cross_weight.astype(low_type), ("seq", "dp"), axis=0, tiled=True),
        lax.all_gather(upward_weight.astype(low_type), ("seq", "dp"), axis=0, tiled=True),
        lax.all_gather(down_weight.astype(low_type), ("seq", "dp"), axis=0, tiled=True),
        lax.all_gather(gain_weight.astype(low_type), ("seq", "dp"), axis=1, tiled=True),
    )
    norm_gains = gain16.astype(wide)
    positions = lax.axis_index("seq") * frames + jnp.arange(frames, dtype=jnp.int32)
    t, keep_rate, noise_rate, clip_weight = plan(bucket)
    frame_mask = (positions[None, :] < audio_len[:, None]).astype(wide)
    row_weight = (clip_weight[:, None] * frame_mask).reshape(total_rows)
    weight_sum = lax.psum(jnp.sum(row_weight), ("seq", "dp"))
    clean = latents.astype(wide)
    noisy_part = noise_draw.astype(wide)
    x_in = (
        (keep_rate[:, None, None] * clean + noise_rate[:, None, None] * noisy_part)
        .astype(low_type)
        .reshape(total_rows, C)
    )
    t_feat = time_features(t).astype(low_type)
    z_feat = timing_features(timing).astype(low_type)
    t_pre = jnp.dot(t_feat, edge16[2 * C : 2 * C + TF], preferred_element_type=wide)
    t_hidden = jax.nn.silu(t_pre).astype(low_type)
    leading_token = jnp.dot(t_hidden, square16[3], preferred_element_type=wide) + jnp.dot(
        z_feat, edge16[2 * C + TF :], preferred_element_type=wide
    )
    prefix_normed, prefix_standardized, prefix_inverse_deviation = layer_normalize(
        leading_token, norm_gains[0]
    )
    n_prefix_low = prefix_normed.astype(low_type)
    kv_prefix = jnp.dot(n_prefix_low, attend16[:, D:], preferred_element_type=wide).astype(low_type)
    k_prefix = kv_prefix[:, :D].reshape(items, 1, HD)
    v_prefix = kv_prefix[:, D:].reshape(items, 1, HD)
    hidden_start = jnp.dot(x_in, edge16[:C], preferred_element_type=wide)
    first_normed, first_standardized, first_inverse_deviation = layer_normalize(
        hidden_start, norm_gains[0]
    )
    n1_low = first_normed.astype(low_type)
    projected = jnp.dot(n1_low, attend16, preferred_element_type=wide).reshape(
        groups, frames, 3, H, HD
    )
    cosine, sine_part = rope_tables(positions + 1)
    rotated = jnp.stack(
        [
            apply_rope(projected[:, :, 0], cosine, sine_part),
            apply_rope(projected[:, :, 1], cosine, sine_part),
            projected[:, :, 2],
        ]
    ).astype(low_type)
    as_items = rotated.transpose(0, 1, 3, 2, 4).reshape(3, items, frames, HD)
    q_use = as_items[0]
    key_value = lax.all_gather(as_items[1:], "seq", axis=2, tiled=True)
    keys = jnp.concatenate([k_prefix, key_value[0]], 1)
    values = jnp.concatenate([v_prefix, key_value[1]], 1)
    o_items, lse = attend(q_use, keys, values)
    o_local = o_items.astype(low_type)
    o_low = o_local.reshape(groups, H, frames, HD).transpose(0, 2, 1, 3).reshape(total_rows, D)
    hidden_after_self = hidden_start + jnp.dot(o_low, square16[0], preferred_element_type=wide)
    second_normed, second_standardized, second_inverse_deviation = layer_normalize(
        hidden_after_self, norm_gains[1]
    )
    n2_low = second_normed.astype(low_type)
    cross_q = (
        jnp.dot(n2_low, square16[1], preferred_element_type=wide)
        .astype(low_type)
        .reshape(groups, frames, H, HD)
    )
    cross_kv = jnp.einsum("gpc,ce->gpe", prompt, cross16, preferred_element_type=wide).astype(
        low_type
    )
    cross_k = cross_kv[..., :D].reshape(groups, PT, H, HD)
    cross_v = cross_kv[..., D:].reshape(groups, PT, H, HD)
    key_mask = jnp.arange(PT)[None, :] < prompt_len[:, None]
    score_scale = HD ** (-0.5)
    scores = (
        jnp.einsum("gfhd,gphd->ghfp", cross_q, cross_k, preferred_element_type=wide) * score_scale
    )
    scores = jnp.where(key_mask[:, None, None, :], scores, -1000000000.0)
    probs = jax.nn.softmax(scores, -1)
    probs_low = probs.astype(low_type)
    co_low = (
        jnp.einsum("ghfp,gphd->gfhd", probs_low, cross_v, preferred_element_type=wide)
        .astype(low_type)
        .reshape(total_rows, D)
    )
    hidden_after_cross = hidden_after_self + jnp.dot(
        co_low, square16[2], preferred_element_type=wide
    )
    third_normed, third_standardized, third_inverse_deviation = layer_normalize(
        hidden_after_cross, norm_gains[2]
    )
    n3_low = third_normed.astype(low_type)
    gate_up = jnp.dot(n3_low, upward16, preferred_element_type=wide)
    gate, upper = (gate_up[:, :FF], gate_up[:, FF:])
    hidden = (jax.nn.silu(gate) * upper).astype(low_type)
    hidden_after_feed = hidden_after_cross + jnp.dot(hidden, down16, preferred_element_type=wide)
    fourth_normed, fourth_standardized, fourth_inverse_deviation = layer_normalize(
        hidden_after_feed, norm_gains[3]
    )
    n4_low = fourth_normed.astype(low_type)
    predicted = jnp.einsum("rd,cd->rc", n4_low, edge16[C : 2 * C], preferred_element_type=wide)
    target = (keep_rate[:, None, None] * noisy_part - noise_rate[:, None, None] * clean).reshape(
        total_rows, C
    )
    error = predicted - target
    loss_local = jnp.sum(row_weight[:, None] * error * error)
    d_pred = (2.0 / (C * weight_sum) * row_weight[:, None] * error).astype(low_type)
    g_out = jnp.einsum("rc,rd->cd", d_pred, n4_low, preferred_element_type=wide)
    fourth_norm_gradient = jnp.dot(d_pred, edge16[C : 2 * C], preferred_element_type=wide)
    hidden_gradient, fourth_gain_gradient = norm_backward(
        fourth_norm_gradient, fourth_standardized, fourth_inverse_deviation, norm_gains[3]
    )
    d_f = hidden_gradient.astype(low_type)
    g_down = jnp.einsum("rf,rd->fd", hidden, d_f, preferred_element_type=wide)
    d_hidden = jnp.einsum("rd,fd->rf", d_f, down16, preferred_element_type=wide)
    sig = jax.nn.sigmoid(gate)
    d_gate_up = jnp.concatenate(
        [d_hidden * upper * sig * (1.0 + gate * (1.0 - sig)), d_hidden * gate * sig], -1
    ).astype(low_type)
    g_up = jnp.einsum("rd,re->de", n3_low, d_gate_up, preferred_element_type=wide)
    third_norm_gradient = jnp.einsum("re,de->rd", d_gate_up, upward16, preferred_element_type=wide)
    partial_gradient, third_gain_gradient = norm_backward(
        third_norm_gradient, third_standardized, third_inverse_deviation, norm_gains[2]
    )
    hidden_gradient = hidden_gradient + partial_gradient
    d_c = hidden_gradient.astype(low_type)
    g_co = jnp.einsum("rd,re->de", co_low, d_c, preferred_element_type=wide)
    d_co = (
        jnp.einsum("re,de->rd", d_c, square16[2], preferred_element_type=wide)
        .astype(low_type)
        .reshape(groups, frames, H, HD)
    )
    d_prob = jnp.einsum("gfhd,gphd->ghfp", d_co, cross_v, preferred_element_type=wide)
    d_cv = jnp.einsum("ghfp,gfhd->gphd", probs_low, d_co, preferred_element_type=wide)
    d_score = (probs * (d_prob - jnp.sum(d_prob * probs, -1, keepdims=True)) * score_scale).astype(
        low_type
    )
    d_cq = (
        jnp.einsum("ghfp,gphd->gfhd", d_score, cross_k, preferred_element_type=wide)
        .astype(low_type)
        .reshape(total_rows, D)
    )
    d_ck = jnp.einsum("ghfp,gfhd->gphd", d_score, cross_q, preferred_element_type=wide)
    d_cross_kv = jnp.concatenate([d_ck.reshape(groups, PT, D), d_cv.reshape(groups, PT, D)], -1)
    g_cross = exact("gpc,gpe->ce", prompt.astype(wide), d_cross_kv)
    g_cq = jnp.einsum("rd,re->de", n2_low, d_cq, preferred_element_type=wide)
    second_norm_gradient = jnp.einsum("re,de->rd", d_cq, square16[1], preferred_element_type=wide)
    partial_gradient, second_gain_gradient = norm_backward(
        second_norm_gradient, second_standardized, second_inverse_deviation, norm_gains[1]
    )
    hidden_gradient = hidden_gradient + partial_gradient
    d_a = hidden_gradient.astype(low_type)
    g_o = jnp.einsum("rd,re->de", o_low, d_a, preferred_element_type=wide)
    d_o = jnp.einsum("re,de->rd", d_a, square16[0], preferred_element_type=wide).astype(low_type)
    d_o_items = d_o.reshape(groups, frames, H, HD).transpose(0, 2, 1, 3).reshape(items, frames, HD)
    d_query, d_key, d_value = attend_back(q_use, keys, values, lse, d_o_items)
    summed_key, summed_value = (
        lax.psum_scatter(
            d_key[:, 1:].astype(jnp.bfloat16), "seq", scatter_dimension=1, tiled=True
        ).astype(jnp.float32),
        lax.psum_scatter(
            d_value[:, 1:].astype(jnp.bfloat16), "seq", scatter_dimension=1, tiled=True
        ).astype(jnp.float32),
    )
    d_items = jnp.stack(
        [d_query.astype(low_type), summed_key.astype(low_type), summed_value.astype(low_type)]
    )
    d_key_prefix = d_key[:, :1]
    d_value_prefix = d_value[:, :1]
    d_rot = d_items.astype(wide).reshape(3, groups, H, frames, HD).transpose(1, 3, 0, 2, 4)
    d_projected = (
        jnp.stack(
            [
                rope_back(d_rot[:, :, 0], cosine, sine_part),
                rope_back(d_rot[:, :, 1], cosine, sine_part),
                d_rot[:, :, 2],
            ],
            2,
        )
        .reshape(total_rows, 3 * D)
        .astype(low_type)
    )
    g_attend = jnp.einsum("rd,re->de", n1_low, d_projected, preferred_element_type=wide)
    first_norm_gradient = jnp.einsum(
        "re,de->rd", d_projected, attend16, preferred_element_type=wide
    )
    partial_gradient, first_gain_gradient = norm_backward(
        first_norm_gradient, first_standardized, first_inverse_deviation, norm_gains[0]
    )
    hidden_gradient = hidden_gradient + partial_gradient
    g_in = jnp.einsum(
        "rc,rd->cd", x_in, hidden_gradient.astype(low_type), preferred_element_type=wide
    )
    d_kv_prefix = jnp.concatenate(
        [d_key_prefix.reshape(groups, D), d_value_prefix.reshape(groups, D)], -1
    )
    attend_kv = attend16[:, D:].astype(wide)
    g_attend = g_attend.at[:, D:].add(exact("gd,ge->de", n_prefix_low.astype(wide), d_kv_prefix))
    prefix_norm_gradient = exact("ge,de->gd", d_kv_prefix, attend_kv)
    leading_token_gradient, prefix_gain_gradient = norm_backward(
        prefix_norm_gradient, prefix_standardized, prefix_inverse_deviation, norm_gains[0]
    )
    g_timing = exact("gz,gd->zd", z_feat.astype(wide), leading_token_gradient)
    g_t2 = exact("ge,gd->ed", t_hidden.astype(wide), leading_token_gradient)
    d_t_hidden = exact("gd,ed->ge", leading_token_gradient, square16[3].astype(wide))
    t_sig = jax.nn.sigmoid(t_pre)
    d_t_pre = d_t_hidden * t_sig * (1.0 + t_pre * (1.0 - t_sig))
    g_t1 = exact("gz,gd->zd", t_feat.astype(wide), d_t_pre)
    g_edge = jnp.concatenate([g_in, g_out, g_t1, g_timing], 0)
    g_square = jnp.stack([g_o, g_cq, g_co, g_t2])
    g_gain = jnp.stack(
        [
            first_gain_gradient + prefix_gain_gradient,
            second_gain_gradient,
            third_gain_gradient,
            fourth_gain_gradient,
        ]
    )
    sharded = (
        lax.psum_scatter(g_edge, ("seq", "dp"), scatter_dimension=1, tiled=True),
        lax.psum_scatter(g_attend, ("seq", "dp"), scatter_dimension=0, tiled=True),
        lax.psum_scatter(g_square, ("seq", "dp"), scatter_dimension=1, tiled=True),
        lax.psum_scatter(g_cross, ("seq", "dp"), scatter_dimension=0, tiled=True),
        lax.psum_scatter(g_up, ("seq", "dp"), scatter_dimension=0, tiled=True),
        lax.psum_scatter(g_down, ("seq", "dp"), scatter_dimension=0, tiled=True),
        lax.psum_scatter(g_gain, ("seq", "dp"), scatter_dimension=1, tiled=True),
    )
    square_local = sum((jnp.sum(g * g) for g in sharded))
    square_total, loss_total = lax.psum((square_local, loss_local), ("seq", "dp"))
    grad_norm = jnp.sqrt(square_total)
    loss_value = loss_total / (C * weight_sum)
    factor = jnp.minimum(1.0, clip_norm / grad_norm)
    count = step_count[0].astype(wide)
    first_fix = 1.0 - 0.9**count
    second_fix = 1.0 - 0.999**count
    weights = (
        edge_weight,
        attend_weight,
        square_weight,
        cross_weight,
        upward_weight,
        down_weight,
        gain_weight,
    )
    firsts = (
        edge_first,
        attend_first,
        square_first,
        cross_first,
        upward_first,
        down_first,
        gain_first,
    )
    seconds = (
        edge_second,
        attend_second,
        square_second,
        cross_second,
        upward_second,
        down_second,
        gain_second,
    )
    out = [
        adam(w, m, v, g * factor, first_fix, second_fix)
        for w, m, v, g in zip(weights, firsts, seconds, sharded)
    ]
    return (
        loss_value,
        grad_norm,
        out[0][0],
        out[0][1],
        out[0][2],
        out[1][0],
        out[1][1],
        out[1][2],
        out[2][0],
        out[2][1],
        out[2][2],
        out[3][0],
        out[3][1],
        out[3][2],
        out[4][0],
        out[4][1],
        out[4][2],
        out[5][0],
        out[5][1],
        out[5][2],
        sharded[6] * factor,
        out[6][1],
        out[6][2],
    )


f32 = jnp.float32
bf16 = jnp.bfloat16
HALF = D // 2
PAIRS = HALF // 128
TRIO = PAIRS // 2
THIRD = HALF // 2
HIDE = FF // 2
CROSS = 768


def dot_nt(a, b):
    return lax.dot_general(a, b, (((1,), (1,)), ((), ())), preferred_element_type=f32)


def dot_nn(a, b):
    return lax.dot_general(a, b, (((1,), (0,)), ((), ())), preferred_element_type=f32)


def dot_tn(a, b):
    return lax.dot_general(a, b, (((0,), (0,)), ((), ())), preferred_element_type=f32)


def call(kernel, grid, in_specs, out_specs, out_shape, scratch, cost, *operands):
    return pl.pallas_call(
        kernel,
        grid=grid,
        in_specs=in_specs,
        out_specs=out_specs,
        out_shape=out_shape,
        scratch_shapes=scratch,
        cost_estimate=pl.CostEstimate(flops=cost[0], bytes_accessed=cost[1], transcendentals=0),
        compiler_params=pltpu.CompilerParams(vmem_limit_bytes=60 << 20),
    )(*operands)


def shape_of(shape, kind):
    return jax.ShapeDtypeStruct(shape, kind)


def turn(y, cosine, sine_up, sine_down):
    return y * cosine + pltpu.roll(y, 16, 1) * sine_up + pltpu.roll(y, 112, 1) * sine_down


def turn_tables(positions):
    lane = jnp.arange(128) % HD
    inverse = 10000.0 ** (-2.0 * jnp.arange(rot_width // 2, dtype=f32) / rot_width)
    angle = positions[:, None].astype(f32) * inverse[None, :]
    wide_angle = jnp.tile(angle, (1, 128 // (rot_width // 2)))
    cosine = jnp.where(lane[None, :] < rot_width, jnp.cos(wide_angle), 1.0)
    sine = jnp.sin(wide_angle)
    second = (lane[None, :] >= rot_width // 2) & (lane[None, :] < rot_width)
    sine_up = jnp.where(second, sine, 0.0)
    sine_down = jnp.where(lane[None, :] < rot_width // 2, -sine, 0.0)
    return (cosine, sine_up, sine_down)


def start_kernel(x_ref, w_ref, gain_ref, h_ref, n_ref, *, own):
    h = dot_nt(x_ref[...], w_ref[...])
    n_ref[...] = layer_normalize(h, gain_ref[...])[0].astype(bf16)

    @pl.when(pl.program_id(0) < own)
    def _():
        h_ref[...] = h


def start_forward(x, w, gain, block=256):
    rows = x.shape[0]
    own = rows // 2 // block
    return call(
        functools.partial(start_kernel, own=own),
        (rows // block,),
        [
            pl.BlockSpec((block, 128), lambda i: (i, 0)),
            pl.BlockSpec((D, 128), lambda i: (0, 3 * PAIRS)),
            pl.BlockSpec((1, D), lambda i: (0, 0)),
        ],
        [
            pl.BlockSpec((block, D), lambda i: (jnp.minimum(i, own - 1), 0)),
            pl.BlockSpec((block, D), lambda i: (i, 0)),
        ],
        [shape_of((rows // 2, D), f32), shape_of((rows, D), bf16)],
        [],
        (2 * rows * D * 128, 4 * rows * D),
        x, w, gain,
    )


def qkv_kernel(n_ref, w_ref, cos_ref, up_ref, down_ref, out_ref):
    part = pl.program_id(0) % 3
    y = dot_nn(n_ref[...], w_ref[...])

    @pl.when(part < 2)
    def _():
        scale = jnp.where(part == 0, HD ** (-0.5), 1.0)
        for j in range(TRIO):
            block = y[:, j * 128 : (j + 1) * 128]
            turned = turn(block, cos_ref[...], up_ref[...], down_ref[...])
            out_ref[:, j * 128 : (j + 1) * 128] = (turned * scale).astype(bf16)

    @pl.when(part == 2)
    def _():
        out_ref[...] = y.astype(bf16)


def qkv_project(n, w, tables, block=1024):
    rows = n.shape[0]
    table = pl.BlockSpec((block, 128), lambda p, i: (i, 0))
    return call(
        qkv_kernel,
        (6, rows // block),
        [
            pl.BlockSpec((block, D), lambda p, i: (i, 0)),
            pl.BlockSpec((D, THIRD), lambda p, i: (0, p)),
            table,
            table,
            table,
        ],
        pl.BlockSpec((block, THIRD), lambda p, i: (i, p)),
        shape_of((rows, 3 * HALF), bf16),
        [],
        (2 * rows * D * 3 * HALF, 4 * rows * D * 2),
        n,
        w,
        *tables,
    )


def attend_kernel(q_ref, k_ref, v_ref, k0_ref, v0_ref, o_ref, lse_ref, *, chunk, count):
    q = q_ref[...]
    rows = q.shape[0]
    lane = lax.broadcasted_iota(jnp.int32, q.shape, 1)
    k0 = k0_ref[0:1].astype(f32)
    v0 = v0_ref[0:1].astype(f32)
    outs = []
    for head in range(2):
        mine = jnp.where((lane // HD) == head, q, jnp.zeros_like(q))
        top = jnp.sum(mine.astype(f32) * k0, 1, keepdims=True)
        total = jnp.ones_like(top)
        acc = jnp.broadcast_to(v0, (rows, 128))
        for c in range(count):
            s = dot_nt(mine, k_ref[c * chunk : (c + 1) * chunk])
            new_top = jnp.maximum(top, jnp.max(s, 1, keepdims=True))
            fade = jnp.exp(top - new_top)
            p = jnp.exp(s - new_top)
            total = total * fade + jnp.sum(p, 1, keepdims=True)
            acc = acc * fade + dot_nn(p.astype(bf16), v_ref[c * chunk : (c + 1) * chunk])
            top = new_top
        outs.append(acc / total)
        lse_ref[0, head : head + 1, :] = (top + jnp.log(total)).T
    o_ref[...] = jnp.where(lane < HD, outs[0], outs[1]).astype(bf16)


def column_of(j, which):
    return (j // TRIO) * (3 * TRIO) + which * TRIO + j % TRIO


def attend_forward(qkv, kv0, block=1024, chunk=1024):
    rows = qkv.shape[0]
    return call(
        functools.partial(attend_kernel, chunk=chunk, count=rows // chunk),
        (PAIRS, rows // block),
        [
            pl.BlockSpec((block, 128), lambda j, i: (i, column_of(j, 0))),
            pl.BlockSpec((rows, 128), lambda j, i: (0, column_of(j, 1))),
            pl.BlockSpec((rows, 128), lambda j, i: (0, column_of(j, 2))),
            pl.BlockSpec((16, 128), lambda j, i: (0, column_of(j, 1))),
            pl.BlockSpec((16, 128), lambda j, i: (0, column_of(j, 2))),
        ],
        [
            pl.BlockSpec((block, 128), lambda j, i: (i, j)),
            pl.BlockSpec((1, 2, block), lambda j, i: (j, 0, i)),
        ],
        [shape_of((rows, HALF), bf16), shape_of((PAIRS, 2, rows), f32)],
        [],
        (16 * rows * rows * HALF, 5 * rows * D * 2),
        qkv,
        qkv,
        qkv,
        kv0,
        kv0,
    )


def attend_back_kernel(*refs, chunk, count, steps, waits):
    (
        q_ref, g_ref, o_ref, lse_ref, cos_ref, up_ref, down_ref,
        k_ref, v_ref, k0_ref, v0_ref, kcos_ref, kup_ref, kdown_ref,
    ) = refs[:14]
    (
        dq_ref, dk_ref, dv_ref, dk0_ref, dv0_ref, kt, dka, dva, dk0a, dv0a,
    ) = refs[14 + waits :]
    i = pl.program_id(1)

    @pl.when(i == 0)
    def _():
        kt[...] = k_ref[...].T
        dka[...] = jnp.zeros_like(dka)
        dva[...] = jnp.zeros_like(dva)
        dk0a[...] = jnp.zeros_like(dk0a)
        dv0a[...] = jnp.zeros_like(dv0a)

    q = q_ref[...]
    g = g_ref[...]
    rows = q.shape[0]
    lane = lax.broadcasted_iota(jnp.int32, q.shape, 1)
    row = lax.broadcasted_iota(jnp.int32, (16, rows), 0)
    go = (g.astype(f32) * o_ref[...].astype(f32)).T
    k0t = k0_ref[...].T
    dqs = []
    for head in range(2):
        sel = (lane // HD) == head
        low_row, high_row = head * HD, (head + 1) * HD
        qm = jnp.where(sel, q, jnp.zeros_like(q))
        gm = jnp.where(sel, g, jnp.zeros_like(g))
        lse = lse_ref[0, head : head + 1, :]
        delta = jnp.sum(go[low_row:high_row], 0, keepdims=True)
        s = dot_nt(k0_ref[...], qm)
        p = jnp.where(row == 0, jnp.exp(s - lse), 0.0)
        ds = (p * (dot_nt(v0_ref[...], gm) - delta)).astype(bf16)
        dk0a[...] += dot_nn(ds, qm)
        dv0a[...] += dot_nn(p.astype(bf16), gm)
        dq = dot_nn(k0t[low_row:high_row], ds)
        for c in range(count):
            part = pl.ds(c * chunk, chunk)
            p = jnp.exp(dot_nt(k_ref[part], qm) - lse)
            ds = (p * (dot_nt(v_ref[part], gm) - delta)).astype(bf16)
            dva[part] += dot_nn(p.astype(bf16), gm)
            dka[part] += dot_nn(ds, qm)
            dq = dq + dot_nn(kt[low_row:high_row, c * chunk : (c + 1) * chunk], ds)
        dqs.append(dq)
    dq = (jnp.concatenate(dqs, 0).T * HD ** (-0.5)).astype(bf16).astype(f32)
    dq_ref[...] = turn(dq, cos_ref[...], -up_ref[...], -down_ref[...]).astype(bf16)

    @pl.when(i == steps - 1)
    def _():
        dk = dka[...].astype(bf16).astype(f32)
        dk_ref[...] = turn(dk, kcos_ref[...], -kup_ref[...], -kdown_ref[...]).astype(bf16)
        dv_ref[...] = dva[...].astype(bf16)
        dk0_ref[...] = dk0a[...]
        dv0_ref[...] = dv0a[...]


def attend_backward(qkv, g, o, lse, kv0, tables, half, after, block=1024, chunk=512):
    rows = qkv.shape[0]
    first = half * TRIO
    out = pl.BlockSpec((block, 128), lambda j, i: (i, j))
    head = pl.BlockSpec((block, 128), lambda j, i: (i, first + j))
    table = pl.BlockSpec((block, 128), lambda j, i: (i, 0))
    whole_table = pl.BlockSpec((rows, 128), lambda j, i: (0, 0))
    whole = pl.BlockSpec((rows, 128), lambda j, i: (0, j))
    lead = pl.BlockSpec((16, 128), lambda j, i: (0, j))

    def part(size, which):
        return pl.BlockSpec((size, 128), lambda j, i: (0, column_of(first + j, which)))

    return call(
        functools.partial(
            attend_back_kernel,
            chunk=chunk, count=rows // chunk, steps=rows // block, waits=len(after),
        ),
        (TRIO, rows // block),
        [
            pl.BlockSpec((block, 128), lambda j, i: (i, column_of(first + j, 0))),
            head, head,
            pl.BlockSpec((1, 2, block), lambda j, i: (first + j, 0, i)),
            table, table, table,
            part(rows, 1), part(rows, 2), part(16, 1), part(16, 2),
            whole_table, whole_table, whole_table,
        ]
        + [pl.BlockSpec(memory_space=pl.ANY)] * len(after),
        [out, whole, whole, lead, lead],
        [shape_of((rows, THIRD), bf16)] * 3 + [shape_of((16, THIRD), f32)] * 2,
        [
            pltpu.VMEM((128, rows), bf16),
            pltpu.VMEM((rows, 128), f32),
            pltpu.VMEM((rows, 128), f32),
            pltpu.VMEM((16, 128), f32),
            pltpu.VMEM((16, 128), f32),
        ],
        (16 * rows * rows * HALF, 5 * rows * D * 2),
        qkv, g, o, lse, *tables, qkv, qkv, kv0, kv0, *tables, *after,
    )


def prompt_probs(k, qm, mask):
    s = dot_nt(k, qm) * HD ** (-0.5) + mask
    e = jnp.exp(s - jnp.max(s, 0, keepdims=True))
    return e / jnp.sum(e, 0, keepdims=True)


def cross_kernel(q_ref, k_ref, v_ref, mask_ref, o_ref):
    q = q_ref[...]
    lane = lax.broadcasted_iota(jnp.int32, q.shape, 1)
    vt = v_ref[...].T
    outs = []
    for head in range(2):
        qm = jnp.where((lane // HD) == head, q, jnp.zeros_like(q))
        p = prompt_probs(k_ref[...], qm, mask_ref[...])
        outs.append(dot_nn(vt[head * HD : (head + 1) * HD], p.astype(bf16)))
    o_ref[...] = jnp.concatenate(outs, 0).T.astype(bf16)


def cross_back_kernel(
    q_ref, g_ref, k_ref, v_ref, mask_ref, dq_ref, dk_ref, dv_ref, dka, dva, *, steps
):
    i = pl.program_id(1)

    @pl.when(i == 0)
    def _():
        dka[...] = jnp.zeros_like(dka)
        dva[...] = jnp.zeros_like(dva)

    q = q_ref[...]
    g = g_ref[...]
    lane = lax.broadcasted_iota(jnp.int32, q.shape, 1)
    kt = k_ref[...].T
    dqs = []
    for head in range(2):
        sel = (lane // HD) == head
        qm = jnp.where(sel, q, jnp.zeros_like(q))
        gm = jnp.where(sel, g, jnp.zeros_like(g))
        p = prompt_probs(k_ref[...], qm, mask_ref[...])
        dp = dot_nt(v_ref[...], gm)
        ds = (p * (dp - jnp.sum(dp * p, 0, keepdims=True)) * HD ** (-0.5)).astype(bf16)
        dva[...] += dot_nn(p.astype(bf16), gm)
        dka[...] += dot_nn(ds, qm)
        dqs.append(dot_nn(kt[head * HD : (head + 1) * HD], ds))
    dq_ref[...] = jnp.concatenate(dqs, 0).T.astype(bf16)

    @pl.when(i == steps - 1)
    def _():
        dk_ref[...] = dka[...]
        dv_ref[...] = dva[...]


def cross_specs(rows, tokens, block):
    q_spec = pl.BlockSpec((block, 128), lambda j, i: (i, j))
    key_spec = pl.BlockSpec((tokens, 128), lambda j, i: (0, j))
    value_spec = pl.BlockSpec((tokens, 128), lambda j, i: (0, PAIRS + j))
    mask_spec = pl.BlockSpec((tokens, 1), lambda j, i: (0, 0))
    return (q_spec, key_spec, value_spec, mask_spec)


def cross_forward(q, kv, mask, block=1024):
    rows, tokens = (q.shape[0], kv.shape[0])
    q_spec, key_spec, value_spec, mask_spec = cross_specs(rows, tokens, block)
    return call(
        cross_kernel,
        (PAIRS, rows // block),
        [q_spec, key_spec, value_spec, mask_spec],
        q_spec,
        shape_of((rows, HALF), bf16),
        [],
        (16 * rows * tokens * HALF, 4 * rows * D),
        q, kv, kv, mask,
    )


def cross_backward(q, g, kv, mask, block=1024):
    rows, tokens = (q.shape[0], kv.shape[0])
    q_spec, key_spec, value_spec, mask_spec = cross_specs(rows, tokens, block)
    return call(
        functools.partial(cross_back_kernel, steps=rows // block),
        (PAIRS, rows // block),
        [q_spec, q_spec, key_spec, value_spec, mask_spec],
        [q_spec, key_spec, key_spec],
        [
            shape_of((rows, HALF), bf16),
            shape_of((tokens, HALF), f32),
            shape_of((tokens, HALF), f32),
        ],
        [pltpu.VMEM((tokens, 128), f32), pltpu.VMEM((tokens, 128), f32)],
        (32 * rows * tokens * HALF, 8 * rows * D),
        q, g, kv, kv, mask,
    )


def gate_up_kernel(n_ref, wg_ref, wu_ref, hidden_ref, gate_ref, up_ref):
    n = n_ref[...]
    gate = dot_nn(n, wg_ref[...])
    up = dot_nn(n, wu_ref[...])
    hidden_ref[...] = (gate / (1.0 + jnp.exp(-gate)) * up).astype(bf16)
    gate_ref[...] = gate.astype(bf16)
    up_ref[...] = up.astype(bf16)


def gate_up(n, w, block=512, columns=512):
    rows = n.shape[0]
    count = HIDE // columns
    out = pl.BlockSpec((block, columns), lambda j, i: (i, j))
    return call(
        gate_up_kernel,
        (count, rows // block),
        [
            pl.BlockSpec((block, D), lambda j, i: (i, 0)),
            pl.BlockSpec((D, columns), lambda j, i: (0, j)),
            pl.BlockSpec((D, columns), lambda j, i: (0, count + j)),
        ],
        [out, out, out],
        [shape_of((rows, HIDE), bf16)] * 3,
        [],
        (4 * rows * D * HIDE, 8 * rows * HIDE + 4 * D * HIDE),
        n, w, w,
    )


def down_back_kernel(d_ref, w_ref, gate_ref, up_ref, after_ref, dgate_ref, dup_ref):
    for part in range(0, w_ref.shape[0], 256):
        cols = slice(part, part + 256)
        d = dot_nt(d_ref[...], w_ref[cols])
        gate = gate_ref[:, cols].astype(f32)
        sig = 1.0 / (1.0 + jnp.exp(-gate))
        d_sig = d * sig
        dgate_ref[:, cols] = (d_sig * up_ref[:, cols] * (1.0 + gate * (1.0 - sig))).astype(bf16)
        dup_ref[:, cols] = (d_sig * gate).astype(bf16)


def down_back(d, w, gate, up, after, block=512, columns=1024):
    rows = d.shape[0]
    out = pl.BlockSpec((block, columns), lambda j, i: (i, j))
    return call(
        down_back_kernel,
        (HIDE // columns, rows // block),
        [
            pl.BlockSpec((block, D), lambda j, i: (i, 0)),
            pl.BlockSpec((columns, D), lambda j, i: (j, 0)),
            out,
            out,
            pl.BlockSpec(memory_space=pl.ANY),
        ],
        [out, out],
        [shape_of((rows, HIDE), bf16)] * 2,
        [],
        (2 * rows * D * HIDE, 10 * rows * HIDE + 2 * D * HIDE),
        d, w, gate, up, after,
    )


def chip_sum_kernel(*refs, inputs, jobs, planes):
    ins, outs = (refs[:inputs], refs[inputs : 2 * inputs])
    scratch = list(refs[2 * inputs : -3])
    send_sem, recv_sem, local_sem = refs[-3:]
    s_at, z_at = (lax.axis_index("seq"), lax.axis_index("z"))
    y_at, x_at = (s_at // 2, s_at % 2)
    y_mate = (1 - y_at) * 2 + x_at
    x_mate = y_at * 2 + (1 - x_at)
    z_mates = [(z_at + offset) % planes for offset in range(1, planes)]
    z_froms = [(z_at + planes - offset) % planes for offset in range(1, planes)]
    barrier = pltpu.get_barrier_semaphore()
    for mate in (y_mate, x_mate):
        pl.semaphore_signal(
            barrier, inc=1, device_id={"seq": mate}, device_id_type=pl.DeviceIdType.MESH
        )
    for mate in z_mates:
        pl.semaphore_signal(
            barrier, inc=1, device_id={"z": mate}, device_id_type=pl.DeviceIdType.MESH
        )
    pl.semaphore_wait(barrier, 1 + planes)

    def remote(job, which, source, target, device):
        copy = pltpu.make_async_remote_copy(
            src_ref=source,
            dst_ref=target,
            send_sem=send_sem.at[job, which],
            recv_sem=recv_sem.at[job, which],
            device_id=device,
            device_id_type=pl.DeviceIdType.MESH,
        )
        copy.start()
        return copy

    def along_z(job, source, received):
        return [
            remote(job, 2 + n, source.at[mate], received.at[n], {"z": mate})
            for n, mate in enumerate(z_mates)
        ]

    state = []
    copies = []
    for n, (full, at, low_col, width, y_first) in enumerate(jobs):
        cols = pl.ds(low_col, width)
        if full:
            own, first, second, third = (scratch.pop(0) for _ in range(4))
            view = ins[at].at[:, :, :, :, cols]
            given = view.at[1 - y_at] if y_first else view.at[:, 1 - x_at]
            kept = view.at[y_at] if y_first else view.at[:, x_at]
            mate = {"seq": y_mate if y_first else x_mate}
            moving = [remote(n, 0, given, first, mate)]
        else:
            own, third = (scratch.pop(0) for _ in range(2))
            first, second = (None, None)
            view = ins[at].at[:, :, cols]
            kept = view.at[z_at]
            moving = along_z(n, view, third)
        local = pltpu.make_async_copy(kept, own, local_sem.at[n])
        local.start()
        copies += moving
        state.append((own, first, second, third, local, moving))

    waiting = []
    for n, (full, at, low_col, width, y_first) in enumerate(jobs):
        own, first, second, third, local, moving = state[n]
        local.wait()
        if not full:
            waiting.append(moving)
            continue
        moving[0].wait_recv()

        def add_first(i, carry):
            half, plane = (i // planes, i % planes)
            own[half, plane] = (
                own[half, plane].astype(f32) + first[half, plane].astype(f32)
            ).astype(bf16)
            return carry

        lax.fori_loop(0, 2 * planes, add_first, 0)
        here = x_at if y_first else y_at
        mate = {"seq": x_mate if y_first else y_mate}
        copy = remote(n, 1, own.at[1 - here], second, mate)
        copies.append(copy)
        waiting.append([copy])
    for n, (full, at, low_col, width, y_first) in enumerate(jobs):
        if not full:
            continue
        own, first, second, third, local, moving = state[n]
        here = x_at if y_first else y_at
        waiting[n][0].wait_recv()

        def add_second(plane, carry):
            second[plane] = (
                own[here, plane].astype(f32) + second[plane].astype(f32)
            ).astype(bf16)
            return carry

        lax.fori_loop(0, planes, add_second, 0)
        waiting[n] = along_z(n, second, third)
        copies += waiting[n]
    for n, (full, at, low_col, width, y_first) in enumerate(jobs):
        own, first, second, third, local, moving = state[n]
        for copy in waiting[n]:
            copy.wait_recv()
        total = (second[z_at] if full else own[...]).astype(f32)
        for m in range(planes - 1):
            total = total + third[m].astype(f32)
        outs[at][:, low_col : low_col + width] = total
    for copy in copies:
        copy.wait_send()


def chip_sums(arrays, jobs, planes):
    scratch = []
    for full, at, _, width, _ in jobs:
        rows = arrays[at].shape[-2]
        if full:
            scratch += [pltpu.VMEM((2, planes, rows, width), bf16)] * 2
            scratch += [pltpu.VMEM((planes, rows, width), bf16)]
        else:
            scratch += [pltpu.VMEM((rows, width), bf16)]
        scratch += [pltpu.VMEM((planes - 1, rows, width), bf16)]
    count = len(jobs)
    scratch += [
        pltpu.SemaphoreType.DMA((count, 1 + planes)),
        pltpu.SemaphoreType.DMA((count, 1 + planes)),
        pltpu.SemaphoreType.DMA((count,)),
    ]
    return pl.pallas_call(
        functools.partial(chip_sum_kernel, inputs=len(arrays), jobs=jobs, planes=planes),
        in_specs=[pl.BlockSpec(memory_space=pl.ANY)] * len(arrays),
        out_specs=[pl.BlockSpec(memory_space=pltpu.VMEM)] * len(arrays),
        out_shape=[shape_of(x.shape[-2:], f32) for x in arrays],
        scratch_shapes=scratch,
        cost_estimate=pl.CostEstimate(flops=10**11, bytes_accessed=10**7, transcendentals=0),
        compiler_params=pltpu.CompilerParams(
            vmem_limit_bytes=56 << 20, collective_id=0, has_side_effects=True
        ),
    )(*arrays)


def chip_body(
    latents, noise_draw, audio_len, bucket, timing, prompt, prompt_len, step_count,
    edge_weight, edge_first, edge_second,
    attend_weight, attend_first, attend_second,
    square_weight, square_first, square_second,
    cross_weight, cross_first, cross_second,
    upward_weight, upward_first, upward_second,
    down_weight, down_first, down_second,
    gain_weight, gain_first, gain_second,
    *, planes, chips,
):
    peers = ("seq", "z")
    many = planes * chips
    groups = latents.shape[0]
    clips = groups * 2 * planes
    frames = latents.shape[1] * chips
    own = frames // 2
    s_at, z_at, k_at = (lax.axis_index("seq"), lax.axis_index("z"), lax.axis_index("core"))
    device = (s_at * planes + z_at) * 2 + k_at
    first_core = k_at == 0

    def swap(x):
        return lax.ppermute(x, "core", [(0, 1), (1, 0)])

    def across(x, axis, size, bit):
        return lax.ppermute(x, axis, [(i, i ^ bit) for i in range(size)])

    def bits(size):
        found = []
        bit = size // 2
        while bit:
            found.append(bit)
            bit //= 2
        return found

    hops = [("z", planes, b) for b in bits(planes)] + [("seq", chips, b) for b in bits(chips)]

    def in_order(mine, other, axis=0):
        return jnp.where(
            first_core,
            jnp.concatenate([mine, other], axis),
            jnp.concatenate([other, mine], axis),
        )

    def pick(x, index, axis):
        return lax.dynamic_index_in_dim(x, index, axis, keepdims=False)

    def halves_of(x, view, axis):
        x = x.reshape(view)
        rows = view[0]
        return (
            pick(x, k_at, axis).reshape(rows, -1),
            pick(x, 1 - k_at, axis).reshape(rows, -1),
        )

    def tie(x):
        return x.reshape(-1, x.shape[-1])[0, 0].astype(f32) * 0.0

    y_at, x_at = (s_at // 2, s_at % 2)

    rows = attend_weight.shape[0]
    attend_view = (rows, 2, 3, 2, THIRD)
    square_view = (rows, 3, 2, HALF)
    cross_view = (cross_weight.shape[0], 2, 2, HALF)
    up_view = (rows, 2, many, 2, FF // (2 * many))
    attend16 = attend_weight.astype(bf16).reshape(rows, 3, 2, 2, THIRD).transpose(0, 3, 1, 2, 4)
    edge16 = jnp.concatenate(
        [edge_weight[: 2 * C].astype(bf16), gain_weight.astype(bf16)], 0
    ).T
    edge16 = jnp.pad(edge16, ((0, 0), (0, 256 - edge16.shape[1])))
    mine, other = halves_of(attend16, attend_view, 3)
    mine, other = (jnp.concatenate([mine, edge16], 1), jnp.concatenate([other, edge16], 1))
    first_mine = in_order(mine, swap(other))
    mine, other = halves_of(
        square_weight[:3].astype(bf16).transpose(1, 0, 2), square_view, 2
    )
    square_mine = in_order(mine, swap(other))
    mine, other = halves_of(cross_weight.astype(bf16), cross_view, 2)
    cross_mine = in_order(mine, swap(other))
    cross_mine = jnp.concatenate([cross_mine[:, :HALF], cross_mine[:, HALF:]], 0)
    first_group = lax.all_gather(
        jnp.concatenate([first_mine, square_mine, cross_mine], 1), peers, axis=0, tiled=True
    )
    square_cols = first_group[:, first_mine.shape[1] :]
    mine, other = halves_of(upward_weight.astype(bf16), up_view, 3)
    up_w = lax.all_gather(in_order(mine, swap(other)), peers, axis=0, tiled=True)
    down_w = lax.all_gather(down_weight.astype(bf16), peers, axis=0, tiled=True)

    attend_w = first_group[:, : 3 * HALF]
    w_in_t = first_group[:, 3 * HALF : 3 * HALF + C]
    w_out_t = first_group[:, 3 * HALF + C : 3 * HALF + 2 * C]
    norm_gains = first_group[:, 3 * HALF + 2 * C : 3 * HALF + 2 * C + 4].astype(f32).T

    def rows_half(columns):
        mine_rows = lax.dynamic_slice_in_dim(columns, k_at * HALF, HALF, 0)
        other_rows = lax.dynamic_slice_in_dim(columns, (1 - k_at) * HALF, HALF, 0)
        return in_order(mine_rows, swap(other_rows), 1)

    local = jnp.stack(
        [audio_len, bucket, timing[:, 0], timing[:, 1], prompt_len], 1
    ).astype(f32)
    clip_index = jnp.arange(clips)
    place = (clip_index // groups) == (z_at * 2 + k_at)
    scalars = jnp.where(place[:, None], jnp.tile(local, (clips // groups, 1)), 0.0)
    scalars = scalars + swap(scalars)
    for b in bits(planes):
        scalars = scalars + across(scalars, "z", planes, b)
    order = (z_at ^ (clip_index // chips)) * chips + (s_at ^ (clip_index % chips))
    chosen = order[:, None] == clip_index[None, :]
    scalars = jnp.sum(jnp.where(chosen[:, :, None], scalars[None], 0.0), 1)
    lengths = scalars[:, 0]
    t, keep_rates, noise_rates, clip_weights = plan(scalars[:, 1])
    weight_sum = jnp.sum(clip_weights * lengths)
    keep_rate, noise_rate, clip_weight = (keep_rates[0], noise_rates[0], clip_weights[0])

    t_feat = time_features(t).astype(bf16)
    z_feat = timing_features(scalars[:, 2:4]).astype(bf16)
    w_t1 = edge_weight[2 * C : 2 * C + TF].astype(bf16)
    w_t2 = square_weight[3].astype(bf16)
    w_timing = edge_weight[2 * C + TF :].astype(bf16)
    t_pre = dot_nn(t_feat, w_t1)
    t_hidden = jax.nn.silu(t_pre).astype(bf16)
    lead = lax.dynamic_update_slice(
        jnp.zeros((clips, D), f32), dot_nn(z_feat, w_timing), (0, device * rows)
    ) + dot_nn(t_hidden, w_t2)
    for axis, size, bit in hops:
        count = lead.shape[0] // 2
        lead = lead[:count] + across(lead[count:], axis, size, bit)
    lead = lead + swap(lead)
    prefix_normed, prefix_std, prefix_dev = layer_normalize(lead, norm_gains[0])
    n_prefix = jnp.pad(prefix_normed.astype(bf16), ((0, 15), (0, 0)))
    kv_prefix = dot_nn(n_prefix, attend_w).astype(bf16)

    part = s_at // groups
    member = s_at % groups
    both = jnp.stack([latents, noise_draw])
    blocks = [pick(both, member, 1)]
    for offset in range(1, chips):
        given = pick(both, (s_at ^ offset) % groups, 1)
        blocks.append(across(given, "seq", chips, offset))
    blocks = jnp.stack(blocks, 1)
    blocks = jnp.where(part == k_at, blocks, swap(blocks))
    seen = s_at ^ jnp.arange(chips)

    def mine_first(x, axis):
        low_half, high_half = jnp.split(x, 2, axis)
        return in_order(low_half, high_half, axis)

    clip = mine_first(blocks, 1).reshape(2, frames, C).astype(f32)
    clean, noisy_part = (clip[0], clip[1])
    positions = (
        mine_first(seen, 0)[:, None] * latents.shape[1] + jnp.arange(latents.shape[1])
    ).reshape(frames)
    row_weight = clip_weight * (positions[:own].astype(f32) < lengths[0]).astype(f32)
    local_prompt = pick(prompt, member, 0)
    other_prompt = swap(local_prompt)
    prompt_low = jnp.where(part == k_at, local_prompt, other_prompt)
    tokens = prompt_low.shape[0]
    mask = jnp.where(
        jnp.arange(tokens)[:, None].astype(f32) < scalars[0, 4], 0.0, -1000000000.0
    ).astype(f32)

    def shared_sum(product):
        given = product(1).astype(bf16)
        return product(0) + swap(given).astype(f32)

    def cut(x, which):
        return x[which * own : (which + 1) * own]

    def both_halves(x):
        return jnp.concatenate([x, swap(x)], 0)

    x_in = (keep_rate * clean + noise_rate * noisy_part).astype(bf16)
    x_wide = jnp.pad(x_in, ((0, 0), (0, C)))
    h0, n1 = start_forward(x_wide, first_group, norm_gains[:1])
    tables = turn_tables(positions + 1)
    qkv = qkv_project(n1, first_group, tables)
    o, lse = attend_forward(qkv, kv_prefix)

    cross_w = square_cols[:, 3 * HALF :].reshape(many, 2, CROSS // many, HALF)
    cross_w = jnp.concatenate(
        [cross_w[:, 0].reshape(CROSS, HALF), cross_w[:, 1].reshape(CROSS, HALF)], 1
    )
    w_o = rows_half(square_cols[:, :HALF])
    w_cq = square_cols[:, HALF : 2 * HALF]
    w_co = rows_half(square_cols[:, 2 * HALF : 3 * HALF])

    h1 = h0 + shared_sum(lambda i: dot_nn(cut(o, i), w_o))
    n2 = both_halves(layer_normalize(h1, norm_gains[1])[0].astype(bf16))
    cross_q = dot_nn(n2, w_cq).astype(bf16)
    cross_kv = dot_nn(prompt_low, cross_w).astype(bf16)
    co = cross_forward(cross_q, cross_kv, mask)
    h2 = h1 + shared_sum(lambda i: dot_nn(cut(co, i), w_co))
    n3 = both_halves(layer_normalize(h2, norm_gains[2])[0].astype(bf16))
    hidden, gate, upper = gate_up(n3, up_w)
    h3 = h2 + shared_sum(lambda i: dot_nn(cut(hidden, i), down_w))
    n4, std4, dev4 = layer_normalize(h3, norm_gains[3])
    n4 = n4.astype(bf16)
    predicted = dot_nn(n4, w_out_t)
    target = keep_rate * noisy_part[:own] - noise_rate * clean[:own]
    error = predicted - target
    loss_local = jnp.sum(row_weight[:, None] * error * error)

    d_pred = (2.0 / (C * weight_sum) * row_weight[:, None] * error).astype(bf16)
    g_out_t = dot_tn(n4, d_pred)
    d_h, gain4 = norm_backward(dot_nt(d_pred, w_out_t), std4, dev4, norm_gains[3])
    d_f = both_halves(d_h.astype(bf16))

    def half_at(x, at, size):
        return lax.dynamic_slice_in_dim(x, at * size, size, 0)

    class Scatter:
        def __init__(self, product, depth, y_first):
            self.product, self.quarter, self.y_first = (product, depth // chips, y_first)
            self.bit, self.later, self.at = (2, 1, x_at) if y_first else (1, 2, y_at)
            given = product(lambda x, axis: self.rows_at(x, axis, True)).astype(bf16)
            self.sent = [given]
            self.taken = across(given, "seq", chips, self.bit)

        def rows_at(self, x, axis, flip):
            quarter = self.quarter

            def block(at):
                return lax.dynamic_slice_in_dim(x, at * quarter, quarter, axis)

            if self.y_first:
                row = (1 - y_at if flip else y_at) * 2
                return lax.dynamic_slice_in_dim(x, row * quarter, 2 * quarter, axis)
            column = 1 - x_at if flip else x_at
            return jnp.concatenate([block(column), block(2 + column)], axis)

        def second(self, behind=0.0):
            own_part = self.product(lambda x, axis: self.rows_at(x, axis, False))
            kept = (own_part + self.taken.astype(f32) + behind).astype(bf16)
            given = half_at(kept, 1 - self.at, self.quarter)
            self.kept = half_at(kept, self.at, self.quarter)
            self.sent = [given]
            self.taken = across(given, "seq", chips, self.later)
            return self

        def folded(self, behind):
            kept = (self.kept.astype(f32) + self.taken.astype(f32) + behind).astype(bf16)
            return kept.reshape(planes, -1, kept.shape[1])

    def gradient(left, right, y_first):
        return Scatter(lambda cut_of: dot_tn(cut_of(left, 1), right), left.shape[1], y_first)

    def gathered_sum(g):
        return lax.psum_scatter(g, peers, scatter_dimension=0, tiled=True)

    g_down = dot_tn(hidden, d_f).astype(bf16)
    s_down = gathered_sum(g_down)
    d_gate, d_up = down_back(d_f, down_w, gate, upper, g_down)
    s_gate = gathered_sum(dot_tn(n3, d_gate).astype(bf16))
    s_upper = gathered_sum(dot_tn(n3, d_up).astype(bf16))
    d_n3 = shared_sum(
        lambda i: dot_nt(cut(d_gate, i), up_w[:, :HIDE]) + dot_nt(cut(d_up, i), up_w[:, HIDE:])
    )

    def norm_again(d_n, h, gain):
        _, std, dev = layer_normalize(h, gain)
        return norm_backward(d_n, std, dev, gain)

    d_part, gain3 = norm_again(d_n3, h2, norm_gains[2])
    d_h = d_h + d_part
    d_c = both_halves(d_h.astype(bf16))
    g_co = dot_tn(co, d_c).astype(bf16)
    d_co = dot_nt(d_c, w_co).astype(bf16)
    d_cq, d_ck, d_cv = cross_backward(cross_q, d_co, cross_kv, mask)
    r_cross = gradient(prompt_low, jnp.concatenate([d_ck, d_cv], 1).astype(bf16), False)
    r_cq = gradient(n2, d_cq, False)
    d_n2 = shared_sum(lambda i: dot_nt(cut(d_cq, i), w_cq))
    d_part, gain2 = norm_again(d_n2, h1, norm_gains[1])
    d_h = d_h + d_part
    d_a = both_halves(d_h.astype(bf16))
    g_o = dot_tn(o, d_a).astype(bf16)

    def columns_half(g):
        kept = lax.dynamic_slice_in_dim(g, k_at * HALF, HALF, 1)
        given = lax.dynamic_slice_in_dim(g, (1 - k_at) * HALF, HALF, 1)
        return in_order(kept, swap(given), 0)

    side = jnp.concatenate([columns_half(g_o), columns_half(g_co)], 1)
    r_side = Scatter(lambda cut_of: cut_of(side, 0).astype(f32), D, True)
    d_o = dot_nt(d_a, w_o).astype(bf16)
    lead_column = n_prefix[:1].astype(f32)

    def attend_half(half, after):
        d_q, d_k, d_v, d_k0, d_v0 = attend_backward(qkv, d_o, o, lse, kv_prefix, tables, half, after)
        lead_row = jnp.concatenate([jnp.zeros_like(d_k0), d_k0, d_v0], 1)
        return (jnp.concatenate([d_q, d_k, d_v], 1), lead_row, tie(d_q))

    def attend_gradient(right, lead_row):
        return (dot_tn(n1, right) + lead_column.T * lead_row[:1]).astype(bf16)

    after = [x for r in (r_cross, r_cq, r_side) for x in r.sent]
    d_first, lead_first, behind_first = attend_half(0, after)
    g_first = attend_gradient(d_first, lead_first)
    for r in (r_cross, r_cq, r_side):
        r.second(behind_first)
    after = [x for r in (r_cross, r_cq, r_side) for x in r.sent] + [g_first]
    d_second, lead_second, behind_second = attend_half(1, after)
    g_second = attend_gradient(d_second, lead_second)
    d_n1 = shared_sum(
        lambda i: dot_nt(cut(d_first, i), attend_w[:, : 3 * THIRD])
        + dot_nt(cut(d_second, i), attend_w[:, 3 * THIRD :])
    )
    d_part, gain1 = norm_again(d_n1, h0, norm_gains[0])
    d_h = d_h + d_part
    g_in_t = dot_tn(d_h.astype(bf16), x_in[:own])
    short = [r.folded(behind_second) for r in (r_cross, r_cq, r_side)]
    d_kv0 = jnp.concatenate([lead_first, lead_second], 1)

    high = d_kv0.astype(bf16)
    rest = (d_kv0 - high.astype(f32)).astype(bf16)
    d_np = dot_nt(jnp.concatenate([high, rest], 0), attend_w)
    d_np = d_np[:1] + d_np[16:17]
    d_np = d_np + swap(d_np)
    d_lead, prefix_gain = norm_backward(d_np, prefix_std, prefix_dev, norm_gains[0])

    def to_owner(x, view, axis):
        count = x.shape[0] // 2
        kept = lax.dynamic_slice_in_dim(x, k_at * count, count, 0)
        given = lax.dynamic_slice_in_dim(x, (1 - k_at) * count, count, 0)
        taken = swap(given.astype(bf16)).astype(f32)
        shape = view[:axis] + view[axis + 1 :]
        joined = jnp.where(
            first_core,
            jnp.stack([kept.reshape(shape), taken.reshape(shape)], axis),
            jnp.stack([taken.reshape(shape), kept.reshape(shape)], axis),
        )
        return joined

    gains = jnp.stack([gain1 + 0.5 * prefix_gain, gain2, gain3, gain4], 1)
    edges = jnp.concatenate([g_in_t, g_out_t], 1)
    gains = jnp.pad(gains, ((0, 0), (0, 128 - gains.shape[1])))
    edges = jnp.where(first_core, edges, gains) + swap(jnp.where(first_core, gains, edges))

    def blocks_of(g):
        return g.astype(bf16).reshape(2, 2, planes, -1, g.shape[1])

    wide, narrow = (5 * 128, 4 * 128)
    jobs = (
        (True, 0, 0, wide, True),
        (True, 0, wide, narrow, False),
        (True, 1, 0, wide, False),
        (True, 1, wide, narrow, True),
        (True, 2, 0, 128, True),
        (False, 3, 0, 2 * HALF, True),
        (False, 4, 0, HALF, True),
        (False, 5, 0, 2 * HALF, True),
    )
    s_first, s_second, s_edge, s_cross, s_cq, s_side = chip_sums(
        [blocks_of(g_first), blocks_of(g_second), blocks_of(edges)] + short, jobs, planes
    )
    s_square = jnp.concatenate([s_side[:, :HALF], s_cq, s_side[:, HALF:]], 1)
    s_attend = jnp.concatenate([s_first, s_second], 1)
    s_edge_part = s_edge
    s_edge = to_owner(s_edge, (rows, 2, 128), 1).reshape(rows, 256)

    d_lead = d_lead + tie(s_first)
    for axis, size in (("seq", chips), ("z", planes)):
        taken = [across(d_lead, axis, size, offset) for offset in range(1, size)]
        d_lead = jnp.concatenate([d_lead] + taken, 0)
    g_t2 = exact("ge,gd->ed", t_hidden.astype(f32), d_lead)
    d_lead_here = lax.dynamic_slice(d_lead, (0, device * rows), (clips, rows))
    g_timing = exact("gz,gd->zd", z_feat.astype(f32), d_lead_here)
    d_t_hidden = exact("gd,ed->ge", d_lead, w_t2.astype(f32))
    t_sig = jax.nn.sigmoid(t_pre)
    d_t_pre = d_t_hidden * t_sig * (1.0 + t_pre * (1.0 - t_sig))
    g_t1 = exact("gz,gd->zd", t_feat.astype(f32), d_t_pre)
    g_attend = to_owner(s_attend, attend_view, 3).transpose(0, 2, 3, 1, 4).reshape(rows, 3 * D)
    g_square = to_owner(s_square, square_view, 2).reshape(rows, 3, D).transpose(1, 0, 2)
    g_square = jnp.concatenate([g_square, g_t2[None]], 0)
    g_cross = to_owner(s_cross, cross_view, 2).reshape(cross_view[0], 2 * D)
    s_upper = s_upper.astype(f32) + tie(s_first)
    s_gate = s_gate.astype(f32)
    half_view = (rows, many, 2, FF // (2 * many))
    g_up = jnp.concatenate(
        [to_owner(x, half_view, 2).reshape(rows, FF) for x in (s_gate, s_upper)], 1
    )
    g_down = s_down.astype(f32)
    g_edge = jnp.concatenate([s_edge[:, : 2 * C].T, g_t1, g_timing], 0)
    g_gain = s_edge[:, 2 * C : 2 * C + 4].T
    sharded = lax.optimization_barrier(
        (g_edge, g_attend, g_square, g_cross, g_up, g_down, g_gain)
    )
    g_gain = sharded[6]
    parts = (s_first, s_second, s_edge_part, s_cross, s_cq, s_side, s_gate, s_upper, g_down)
    parts = parts + (g_t1, g_t2, g_timing)
    totals = jnp.stack([sum(jnp.sum(g * g) for g in parts), loss_local])
    totals = totals + swap(totals)
    for axis, size, bit in hops:
        totals = totals + across(totals, axis, size, bit)
    grad_norm = jnp.sqrt(totals[0])
    loss_value = totals[1] / (C * weight_sum)
    factor = jnp.minimum(1.0, clip_norm / grad_norm)
    count = step_count[0].astype(f32)
    first_fix = 1.0 - 0.9**count
    second_fix = 1.0 - 0.999**count
    states = (
        (edge_weight, edge_first, edge_second),
        (attend_weight, attend_first, attend_second),
        (square_weight, square_first, square_second),
        (cross_weight, cross_first, cross_second),
        (upward_weight, upward_first, upward_second),
        (down_weight, down_first, down_second),
        (gain_weight, gain_first, gain_second),
    )
    out = [
        adam(w, m, v, g * factor, first_fix, second_fix)
        for (w, m, v), g in zip(states, sharded)
    ]
    flat = [x for triple in out[:6] for x in triple]
    return (loss_value, grad_norm, *flat, g_gain * factor, out[6][1], out[6][2])


def solution(mesh):
    chips, spread = (mesh.shape["seq"], mesh.shape["dp"])
    split_mesh = Mesh(mesh.devices.reshape(chips, spread // 2, 2), ("seq", "z", "core"))

    def whole(*args):
        groups = args[0].shape[0] // spread
        one_clip_per_chip = groups * 2 == chips == 4 and spread & (spread - 1) == 0
        if one_clip_per_chip:
            inner = functools.partial(chip_body, planes=spread // 2, chips=chips)
            dp, used = ("z", "core"), split_mesh
        else:
            inner, dp, used = (general_body, "dp", mesh)
        every = ("seq",) + (dp if isinstance(dp, tuple) else (dp,))
        by_row, by_column, by_middle = (P(every, None), P(None, every), P(None, every, None))
        frames = P(dp, "seq", None)
        clip = P(dp)
        kinds = (by_column, by_row, by_middle, by_row, by_row, by_row, by_column)
        weights = tuple(kind for kind in kinds for _ in range(3))
        return jax.shard_map(
            inner,
            mesh=used,
            in_specs=(frames, frames, clip, clip, P(dp, None), P(dp, None, None), clip, P())
            + weights,
            out_specs=(P(), P()) + weights,
            check_vma=False,
        )(*args)

    return whole
```

```python
import functools
import math

import jax
import jax.numpy as jnp
from jax import lax
from jax.experimental import pallas as pl
from jax.experimental.pallas import tpu as pltpu
from jax.sharding import Mesh
from jax.sharding import PartitionSpec as P

D = 1536
H = 24
HD = 64
FF = 6144
C = 64
TF = 256
PT = 128
NB = 1000


highest = lax.Precision.HIGHEST
clip_norm = 0.002
learn_rate = 0.1
weight_decay = 0.1
rot_width = 32


def layer_normalize(h, norm_gain):
    centered_input = h - jnp.mean(h, -1, keepdims=True)
    inverse_deviation = lax.rsqrt(
        jnp.mean(centered_input * centered_input, -1, keepdims=True) + 1e-05
    )
    standardized = centered_input * inverse_deviation
    return (standardized * norm_gain, standardized, inverse_deviation)


def norm_backward(incoming_gradient, standardized, inverse_deviation, norm_gain):
    scaled_gradient = incoming_gradient * norm_gain
    gain_gradient = jnp.sum(incoming_gradient * standardized, 0)
    d_in = inverse_deviation * (
        scaled_gradient
        - jnp.mean(scaled_gradient, -1, keepdims=True)
        - standardized * jnp.mean(scaled_gradient * standardized, -1, keepdims=True)
    )
    return (d_in, gain_gradient)


def plan(bucket):
    t = (bucket.astype(jnp.float32) + 0.5) / NB
    keep_rate = jnp.cos(t * (math.pi / 2))
    noise_rate = jnp.sin(t * (math.pi / 2))
    snr_ratio = keep_rate * keep_rate / (noise_rate * noise_rate)
    return (t, keep_rate, noise_rate, jnp.minimum(snr_ratio, 5.0) / (snr_ratio + 1.0))


def time_features(t):
    freqs = jnp.exp(-math.log(10000.0) * jnp.arange(TF // 2, dtype=jnp.float32) / (TF // 2))
    angle = t[:, None] * 1000.0 * freqs[None, :]
    return jnp.concatenate([jnp.cos(angle), jnp.sin(angle)], -1)


def timing_features(timing):
    seconds = timing.astype(jnp.float32) / 64.0
    return jnp.concatenate([time_features(seconds[:, 0]), time_features(seconds[:, 1])], -1)


def rope_tables(positions):
    inverse = 10000.0 ** (-2.0 * jnp.arange(rot_width // 2, dtype=jnp.float32) / rot_width)
    angle = positions[:, None].astype(jnp.float32) * inverse[None, :]
    angle = jnp.concatenate([angle, angle], -1)
    return (jnp.cos(angle), jnp.sin(angle))


def rotate(x):
    half = rot_width // 2
    return jnp.concatenate([-x[..., half:], x[..., :half]], -1)


def apply_rope(x, cosine, sine_part):
    turned = x[..., :rot_width]
    turned = turned * cosine[None, :, None, :] + rotate(turned) * sine_part[None, :, None, :]
    return jnp.concatenate([turned, x[..., rot_width:]], -1)


def rope_back(incoming_gradient, cosine, sine_part):
    turned = incoming_gradient[..., :rot_width]
    turned = turned * cosine[None, :, None, :] - rotate(turned * sine_part[None, :, None, :])
    return jnp.concatenate([turned, incoming_gradient[..., rot_width:]], -1)


def split_blocks(x, count, block):
    return x.reshape((x.shape[0], count, block) + x.shape[2:]).swapaxes(0, 1)


def join_blocks(x):
    x = x.swapaxes(0, 1)
    return x.reshape((x.shape[0], x.shape[1] * x.shape[2]) + x.shape[3:])


def attend(q, keys, values):
    rows_q = q.shape[1]
    block = min(512, rows_q)
    count = rows_q // block
    score_scale = HD ** (-0.5)

    def one_block(q_block):
        s = (
            jnp.einsum("ibd,ikd->ibk", q_block, keys, preferred_element_type=jnp.float32)
            * score_scale
        )
        top = jnp.max(s, -1, keepdims=True)
        lse = top + jnp.log(jnp.sum(jnp.exp(s - top), -1, keepdims=True))
        p = jnp.exp(s - lse)
        o = jnp.einsum(
            "ibk,ikd->ibd", p.astype(jnp.bfloat16), values, preferred_element_type=jnp.float32
        )
        return (o, lse[..., 0])

    outs, lses = lax.map(one_block, split_blocks(q, count, block))
    return (join_blocks(outs), join_blocks(lses))


def attend_back(q, keys, values, lse, grad_o):
    rows_q = q.shape[1]
    block = min(512, rows_q)
    count = rows_q // block
    score_scale = HD ** (-0.5)

    def one_block(carry, parts):
        d_key, d_value = carry
        q_block, g_block, l_block = parts
        s = (
            jnp.einsum("ibd,ikd->ibk", q_block, keys, preferred_element_type=jnp.float32)
            * score_scale
        )
        p = jnp.exp(s - l_block[..., None])
        d_prob = jnp.einsum("ibd,ikd->ibk", g_block, values, preferred_element_type=jnp.float32)
        d_value = d_value + jnp.einsum(
            "ibk,ibd->ikd", p.astype(jnp.bfloat16), g_block, preferred_element_type=jnp.float32
        )
        d_score = (p * (d_prob - jnp.sum(d_prob * p, -1, keepdims=True)) * score_scale).astype(
            jnp.bfloat16
        )
        d_query = jnp.einsum("ibk,ikd->ibd", d_score, keys, preferred_element_type=jnp.float32)
        d_key = d_key + jnp.einsum(
            "ibk,ibd->ikd", d_score, q_block, preferred_element_type=jnp.float32
        )
        return ((d_key, d_value), d_query)

    zeros = jnp.zeros(keys.shape, jnp.float32)
    parts = (
        split_blocks(q, count, block),
        split_blocks(grad_o, count, block),
        split_blocks(lse, count, block),
    )
    (d_key, d_value), d_queries = lax.scan(one_block, (zeros, zeros), parts)
    return (join_blocks(d_queries), d_key, d_value)


def adam(w, m, v, g, first_fix, second_fix):
    first = 0.9 * m + 0.1 * g
    second = 0.999 * v + 0.001 * g * g
    new = w - learn_rate * (
        first / first_fix / (jnp.sqrt(second / second_fix) + 1e-08) + weight_decay * w
    )
    return (new, first, second)


def exact(form, a, b):
    return jnp.einsum(form, a, b, precision=highest, preferred_element_type=jnp.float32)


def general_body(
    latents,
    noise_draw,
    audio_len,
    bucket,
    timing,
    prompt,
    prompt_len,
    step_count,
    edge_weight,
    edge_first,
    edge_second,
    attend_weight,
    attend_first,
    attend_second,
    square_weight,
    square_first,
    square_second,
    cross_weight,
    cross_first,
    cross_second,
    upward_weight,
    upward_first,
    upward_second,
    down_weight,
    down_first,
    down_second,
    gain_weight,
    gain_first,
    gain_second,
):
    low_type = jnp.bfloat16
    wide = jnp.float32
    groups, frames = (latents.shape[0], latents.shape[1])
    total_rows = groups * frames
    items = groups * H
    edge16, attend16, square16, cross16, upward16, down16, gain16 = (
        lax.all_gather(edge_weight.astype(low_type), ("seq", "dp"), axis=1, tiled=True),
        lax.all_gather(attend_weight.astype(low_type), ("seq", "dp"), axis=0, tiled=True),
        lax.all_gather(square_weight.astype(low_type), ("seq", "dp"), axis=1, tiled=True),
        lax.all_gather(cross_weight.astype(low_type), ("seq", "dp"), axis=0, tiled=True),
        lax.all_gather(upward_weight.astype(low_type), ("seq", "dp"), axis=0, tiled=True),
        lax.all_gather(down_weight.astype(low_type), ("seq", "dp"), axis=0, tiled=True),
        lax.all_gather(gain_weight.astype(low_type), ("seq", "dp"), axis=1, tiled=True),
    )
    norm_gains = gain16.astype(wide)
    positions = lax.axis_index("seq") * frames + jnp.arange(frames, dtype=jnp.int32)
    t, keep_rate, noise_rate, clip_weight = plan(bucket)
    frame_mask = (positions[None, :] < audio_len[:, None]).astype(wide)
    row_weight = (clip_weight[:, None] * frame_mask).reshape(total_rows)
    weight_sum = lax.psum(jnp.sum(row_weight), ("seq", "dp"))
    clean = latents.astype(wide)
    noisy_part = noise_draw.astype(wide)
    x_in = (
        (keep_rate[:, None, None] * clean + noise_rate[:, None, None] * noisy_part)
        .astype(low_type)
        .reshape(total_rows, C)
    )
    t_feat = time_features(t).astype(low_type)
    z_feat = timing_features(timing).astype(low_type)
    t_pre = jnp.dot(t_feat, edge16[2 * C : 2 * C + TF], preferred_element_type=wide)
    t_hidden = jax.nn.silu(t_pre).astype(low_type)
    leading_token = jnp.dot(t_hidden, square16[3], preferred_element_type=wide) + jnp.dot(
        z_feat, edge16[2 * C + TF :], preferred_element_type=wide
    )
    prefix_normed, prefix_standardized, prefix_inverse_deviation = layer_normalize(
        leading_token, norm_gains[0]
    )
    n_prefix_low = prefix_normed.astype(low_type)
    kv_prefix = jnp.dot(n_prefix_low, attend16[:, D:], preferred_element_type=wide).astype(low_type)
    k_prefix = kv_prefix[:, :D].reshape(items, 1, HD)
    v_prefix = kv_prefix[:, D:].reshape(items, 1, HD)
    hidden_start = jnp.dot(x_in, edge16[:C], preferred_element_type=wide)
    first_normed, first_standardized, first_inverse_deviation = layer_normalize(
        hidden_start, norm_gains[0]
    )
    n1_low = first_normed.astype(low_type)
    projected = jnp.dot(n1_low, attend16, preferred_element_type=wide).reshape(
        groups, frames, 3, H, HD
    )
    cosine, sine_part = rope_tables(positions + 1)
    rotated = jnp.stack(
        [
            apply_rope(projected[:, :, 0], cosine, sine_part),
            apply_rope(projected[:, :, 1], cosine, sine_part),
            projected[:, :, 2],
        ]
    ).astype(low_type)
    as_items = rotated.transpose(0, 1, 3, 2, 4).reshape(3, items, frames, HD)
    q_use = as_items[0]
    key_value = lax.all_gather(as_items[1:], "seq", axis=2, tiled=True)
    keys = jnp.concatenate([k_prefix, key_value[0]], 1)
    values = jnp.concatenate([v_prefix, key_value[1]], 1)
    o_items, lse = attend(q_use, keys, values)
    o_local = o_items.astype(low_type)
    o_low = o_local.reshape(groups, H, frames, HD).transpose(0, 2, 1, 3).reshape(total_rows, D)
    hidden_after_self = hidden_start + jnp.dot(o_low, square16[0], preferred_element_type=wide)
    second_normed, second_standardized, second_inverse_deviation = layer_normalize(
        hidden_after_self, norm_gains[1]
    )
    n2_low = second_normed.astype(low_type)
    cross_q = (
        jnp.dot(n2_low, square16[1], preferred_element_type=wide)
        .astype(low_type)
        .reshape(groups, frames, H, HD)
    )
    cross_kv = jnp.einsum("gpc,ce->gpe", prompt, cross16, preferred_element_type=wide).astype(
        low_type
    )
    cross_k = cross_kv[..., :D].reshape(groups, PT, H, HD)
    cross_v = cross_kv[..., D:].reshape(groups, PT, H, HD)
    key_mask = jnp.arange(PT)[None, :] < prompt_len[:, None]
    score_scale = HD ** (-0.5)
    scores = (
        jnp.einsum("gfhd,gphd->ghfp", cross_q, cross_k, preferred_element_type=wide) * score_scale
    )
    scores = jnp.where(key_mask[:, None, None, :], scores, -1000000000.0)
    probs = jax.nn.softmax(scores, -1)
    probs_low = probs.astype(low_type)
    co_low = (
        jnp.einsum("ghfp,gphd->gfhd", probs_low, cross_v, preferred_element_type=wide)
        .astype(low_type)
        .reshape(total_rows, D)
    )
    hidden_after_cross = hidden_after_self + jnp.dot(
        co_low, square16[2], preferred_element_type=wide
    )
    third_normed, third_standardized, third_inverse_deviation = layer_normalize(
        hidden_after_cross, norm_gains[2]
    )
    n3_low = third_normed.astype(low_type)
    gate_up = jnp.dot(n3_low, upward16, preferred_element_type=wide)
    gate, upper = (gate_up[:, :FF], gate_up[:, FF:])
    hidden = (jax.nn.silu(gate) * upper).astype(low_type)
    hidden_after_feed = hidden_after_cross + jnp.dot(hidden, down16, preferred_element_type=wide)
    fourth_normed, fourth_standardized, fourth_inverse_deviation = layer_normalize(
        hidden_after_feed, norm_gains[3]
    )
    n4_low = fourth_normed.astype(low_type)
    predicted = jnp.einsum("rd,cd->rc", n4_low, edge16[C : 2 * C], preferred_element_type=wide)
    target = (keep_rate[:, None, None] * noisy_part - noise_rate[:, None, None] * clean).reshape(
        total_rows, C
    )
    error = predicted - target
    loss_local = jnp.sum(row_weight[:, None] * error * error)
    d_pred = (2.0 / (C * weight_sum) * row_weight[:, None] * error).astype(low_type)
    g_out = jnp.einsum("rc,rd->cd", d_pred, n4_low, preferred_element_type=wide)
    fourth_norm_gradient = jnp.dot(d_pred, edge16[C : 2 * C], preferred_element_type=wide)
    hidden_gradient, fourth_gain_gradient = norm_backward(
        fourth_norm_gradient, fourth_standardized, fourth_inverse_deviation, norm_gains[3]
    )
    d_f = hidden_gradient.astype(low_type)
    g_down = jnp.einsum("rf,rd->fd", hidden, d_f, preferred_element_type=wide)
    d_hidden = jnp.einsum("rd,fd->rf", d_f, down16, preferred_element_type=wide)
    sig = jax.nn.sigmoid(gate)
    d_gate_up = jnp.concatenate(
        [d_hidden * upper * sig * (1.0 + gate * (1.0 - sig)), d_hidden * gate * sig], -1
    ).astype(low_type)
    g_up = jnp.einsum("rd,re->de", n3_low, d_gate_up, preferred_element_type=wide)
    third_norm_gradient = jnp.einsum("re,de->rd", d_gate_up, upward16, preferred_element_type=wide)
    partial_gradient, third_gain_gradient = norm_backward(
        third_norm_gradient, third_standardized, third_inverse_deviation, norm_gains[2]
    )
    hidden_gradient = hidden_gradient + partial_gradient
    d_c = hidden_gradient.astype(low_type)
    g_co = jnp.einsum("rd,re->de", co_low, d_c, preferred_element_type=wide)
    d_co = (
        jnp.einsum("re,de->rd", d_c, square16[2], preferred_element_type=wide)
        .astype(low_type)
        .reshape(groups, frames, H, HD)
    )
    d_prob = jnp.einsum("gfhd,gphd->ghfp", d_co, cross_v, preferred_element_type=wide)
    d_cv = jnp.einsum("ghfp,gfhd->gphd", probs_low, d_co, preferred_element_type=wide)
    d_score = (probs * (d_prob - jnp.sum(d_prob * probs, -1, keepdims=True)) * score_scale).astype(
        low_type
    )
    d_cq = (
        jnp.einsum("ghfp,gphd->gfhd", d_score, cross_k, preferred_element_type=wide)
        .astype(low_type)
        .reshape(total_rows, D)
    )
    d_ck = jnp.einsum("ghfp,gfhd->gphd", d_score, cross_q, preferred_element_type=wide)
    d_cross_kv = jnp.concatenate([d_ck.reshape(groups, PT, D), d_cv.reshape(groups, PT, D)], -1)
    g_cross = exact("gpc,gpe->ce", prompt.astype(wide), d_cross_kv)
    g_cq = jnp.einsum("rd,re->de", n2_low, d_cq, preferred_element_type=wide)
    second_norm_gradient = jnp.einsum("re,de->rd", d_cq, square16[1], preferred_element_type=wide)
    partial_gradient, second_gain_gradient = norm_backward(
        second_norm_gradient, second_standardized, second_inverse_deviation, norm_gains[1]
    )
    hidden_gradient = hidden_gradient + partial_gradient
    d_a = hidden_gradient.astype(low_type)
    g_o = jnp.einsum("rd,re->de", o_low, d_a, preferred_element_type=wide)
    d_o = jnp.einsum("re,de->rd", d_a, square16[0], preferred_element_type=wide).astype(low_type)
    d_o_items = d_o.reshape(groups, frames, H, HD).transpose(0, 2, 1, 3).reshape(items, frames, HD)
    d_query, d_key, d_value = attend_back(q_use, keys, values, lse, d_o_items)
    summed_key, summed_value = (
        lax.psum_scatter(
            d_key[:, 1:].astype(jnp.bfloat16), "seq", scatter_dimension=1, tiled=True
        ).astype(jnp.float32),
        lax.psum_scatter(
            d_value[:, 1:].astype(jnp.bfloat16), "seq", scatter_dimension=1, tiled=True
        ).astype(jnp.float32),
    )
    d_items = jnp.stack(
        [d_query.astype(low_type), summed_key.astype(low_type), summed_value.astype(low_type)]
    )
    d_key_prefix = d_key[:, :1]
    d_value_prefix = d_value[:, :1]
    d_rot = d_items.astype(wide).reshape(3, groups, H, frames, HD).transpose(1, 3, 0, 2, 4)
    d_projected = (
        jnp.stack(
            [
                rope_back(d_rot[:, :, 0], cosine, sine_part),
                rope_back(d_rot[:, :, 1], cosine, sine_part),
                d_rot[:, :, 2],
            ],
            2,
        )
        .reshape(total_rows, 3 * D)
        .astype(low_type)
    )
    g_attend = jnp.einsum("rd,re->de", n1_low, d_projected, preferred_element_type=wide)
    first_norm_gradient = jnp.einsum(
        "re,de->rd", d_projected, attend16, preferred_element_type=wide
    )
    partial_gradient, first_gain_gradient = norm_backward(
        first_norm_gradient, first_standardized, first_inverse_deviation, norm_gains[0]
    )
    hidden_gradient = hidden_gradient + partial_gradient
    g_in = jnp.einsum(
        "rc,rd->cd", x_in, hidden_gradient.astype(low_type), preferred_element_type=wide
    )
    d_kv_prefix = jnp.concatenate(
        [d_key_prefix.reshape(groups, D), d_value_prefix.reshape(groups, D)], -1
    )
    attend_kv = attend16[:, D:].astype(wide)
    g_attend = g_attend.at[:, D:].add(exact("gd,ge->de", n_prefix_low.astype(wide), d_kv_prefix))
    prefix_norm_gradient = exact("ge,de->gd", d_kv_prefix, attend_kv)
    leading_token_gradient, prefix_gain_gradient = norm_backward(
        prefix_norm_gradient, prefix_standardized, prefix_inverse_deviation, norm_gains[0]
    )
    g_timing = exact("gz,gd->zd", z_feat.astype(wide), leading_token_gradient)
    g_t2 = exact("ge,gd->ed", t_hidden.astype(wide), leading_token_gradient)
    d_t_hidden = exact("gd,ed->ge", leading_token_gradient, square16[3].astype(wide))
    t_sig = jax.nn.sigmoid(t_pre)
    d_t_pre = d_t_hidden * t_sig * (1.0 + t_pre * (1.0 - t_sig))
    g_t1 = exact("gz,gd->zd", t_feat.astype(wide), d_t_pre)
    g_edge = jnp.concatenate([g_in, g_out, g_t1, g_timing], 0)
    g_square = jnp.stack([g_o, g_cq, g_co, g_t2])
    g_gain = jnp.stack(
        [
            first_gain_gradient + prefix_gain_gradient,
            second_gain_gradient,
            third_gain_gradient,
            fourth_gain_gradient,
        ]
    )
    sharded = (
        lax.psum_scatter(g_edge, ("seq", "dp"), scatter_dimension=1, tiled=True),
        lax.psum_scatter(g_attend, ("seq", "dp"), scatter_dimension=0, tiled=True),
        lax.psum_scatter(g_square, ("seq", "dp"), scatter_dimension=1, tiled=True),
        lax.psum_scatter(g_cross, ("seq", "dp"), scatter_dimension=0, tiled=True),
        lax.psum_scatter(g_up, ("seq", "dp"), scatter_dimension=0, tiled=True),
        lax.psum_scatter(g_down, ("seq", "dp"), scatter_dimension=0, tiled=True),
        lax.psum_scatter(g_gain, ("seq", "dp"), scatter_dimension=1, tiled=True),
    )
    square_local = sum((jnp.sum(g * g) for g in sharded))
    square_total, loss_total = lax.psum((square_local, loss_local), ("seq", "dp"))
    grad_norm = jnp.sqrt(square_total)
    loss_value = loss_total / (C * weight_sum)
    factor = jnp.minimum(1.0, clip_norm / grad_norm)
    count = step_count[0].astype(wide)
    first_fix = 1.0 - 0.9**count
    second_fix = 1.0 - 0.999**count
    weights = (
        edge_weight,
        attend_weight,
        square_weight,
        cross_weight,
        upward_weight,
        down_weight,
        gain_weight,
    )
    firsts = (
        edge_first,
        attend_first,
        square_first,
        cross_first,
        upward_first,
        down_first,
        gain_first,
    )
    seconds = (
        edge_second,
        attend_second,
        square_second,
        cross_second,
        upward_second,
        down_second,
        gain_second,
    )
    out = [
        adam(w, m, v, g * factor, first_fix, second_fix)
        for w, m, v, g in zip(weights, firsts, seconds, sharded)
    ]
    return (
        loss_value,
        grad_norm,
        out[0][0],
        out[0][1],
        out[0][2],
        out[1][0],
        out[1][1],
        out[1][2],
        out[2][0],
        out[2][1],
        out[2][2],
        out[3][0],
        out[3][1],
        out[3][2],
        out[4][0],
        out[4][1],
        out[4][2],
        out[5][0],
        out[5][1],
        out[5][2],
        sharded[6] * factor,
        out[6][1],
        out[6][2],
    )


f32 = jnp.float32
bf16 = jnp.bfloat16
HALF = D // 2
PAIRS = HALF // 128
TRIO = PAIRS // 2
THIRD = HALF // 2
HIDE = FF // 2
CROSS = 768


def dot_nt(a, b):
    return lax.dot_general(a, b, (((1,), (1,)), ((), ())), preferred_element_type=f32)


def dot_nn(a, b):
    return lax.dot_general(a, b, (((1,), (0,)), ((), ())), preferred_element_type=f32)


def dot_tn(a, b):
    return lax.dot_general(a, b, (((0,), (0,)), ((), ())), preferred_element_type=f32)


def call(kernel, grid, in_specs, out_specs, out_shape, scratch, cost, *operands):
    return pl.pallas_call(
        kernel,
        grid=grid,
        in_specs=in_specs,
        out_specs=out_specs,
        out_shape=out_shape,
        scratch_shapes=scratch,
        cost_estimate=pl.CostEstimate(flops=cost[0], bytes_accessed=cost[1], transcendentals=0),
        compiler_params=pltpu.CompilerParams(vmem_limit_bytes=60 << 20),
    )(*operands)


def shape_of(shape, kind):
    return jax.ShapeDtypeStruct(shape, kind)


def turn(y, cosine, sine_up, sine_down):
    return y * cosine + pltpu.roll(y, 16, 1) * sine_up + pltpu.roll(y, 112, 1) * sine_down


def turn_tables(positions):
    lane = jnp.arange(128) % HD
    inverse = 10000.0 ** (-2.0 * jnp.arange(rot_width // 2, dtype=f32) / rot_width)
    angle = positions[:, None].astype(f32) * inverse[None, :]
    wide_angle = jnp.tile(angle, (1, 128 // (rot_width // 2)))
    cosine = jnp.where(lane[None, :] < rot_width, jnp.cos(wide_angle), 1.0)
    sine = jnp.sin(wide_angle)
    second = (lane[None, :] >= rot_width // 2) & (lane[None, :] < rot_width)
    sine_up = jnp.where(second, sine, 0.0)
    sine_down = jnp.where(lane[None, :] < rot_width // 2, -sine, 0.0)
    return (cosine, sine_up, sine_down)


def start_kernel(x_ref, w_ref, gain_ref, h_ref, n_ref, *, own):
    h = dot_nt(x_ref[...], w_ref[...])
    n_ref[...] = layer_normalize(h, gain_ref[...])[0].astype(bf16)

    @pl.when(pl.program_id(0) < own)
    def _():
        h_ref[...] = h


def start_forward(x, w, gain, block=256):
    rows = x.shape[0]
    own = rows // 2 // block
    return call(
        functools.partial(start_kernel, own=own),
        (rows // block,),
        [
            pl.BlockSpec((block, 128), lambda i: (i, 0)),
            pl.BlockSpec((D, 128), lambda i: (0, 3 * PAIRS)),
            pl.BlockSpec((1, D), lambda i: (0, 0)),
        ],
        [
            pl.BlockSpec((block, D), lambda i: (jnp.minimum(i, own - 1), 0)),
            pl.BlockSpec((block, D), lambda i: (i, 0)),
        ],
        [shape_of((rows // 2, D), f32), shape_of((rows, D), bf16)],
        [],
        (2 * rows * D * 128, 4 * rows * D),
        x, w, gain,
    )


def qkv_kernel(n_ref, w_ref, cos_ref, up_ref, down_ref, out_ref):
    part = pl.program_id(0) % 3
    y = dot_nn(n_ref[...], w_ref[...])

    @pl.when(part < 2)
    def _():
        scale = jnp.where(part == 0, HD ** (-0.5), 1.0)
        for j in range(TRIO):
            block = y[:, j * 128 : (j + 1) * 128]
            turned = turn(block, cos_ref[...], up_ref[...], down_ref[...])
            out_ref[:, j * 128 : (j + 1) * 128] = (turned * scale).astype(bf16)

    @pl.when(part == 2)
    def _():
        out_ref[...] = y.astype(bf16)


def qkv_project(n, w, tables, block=1024):
    rows = n.shape[0]
    table = pl.BlockSpec((block, 128), lambda p, i: (i, 0))
    return call(
        qkv_kernel,
        (6, rows // block),
        [
            pl.BlockSpec((block, D), lambda p, i: (i, 0)),
            pl.BlockSpec((D, THIRD), lambda p, i: (0, p)),
            table,
            table,
            table,
        ],
        pl.BlockSpec((block, THIRD), lambda p, i: (i, p)),
        shape_of((rows, 3 * HALF), bf16),
        [],
        (2 * rows * D * 3 * HALF, 4 * rows * D * 2),
        n,
        w,
        *tables,
    )


def attend_kernel(q_ref, k_ref, v_ref, k0_ref, v0_ref, o_ref, lse_ref, *, chunk, count):
    q = q_ref[...]
    rows = q.shape[0]
    lane = lax.broadcasted_iota(jnp.int32, q.shape, 1)
    k0 = k0_ref[0:1].astype(f32)
    v0 = v0_ref[0:1].astype(f32)
    outs = []
    for head in range(2):
        mine = jnp.where((lane // HD) == head, q, jnp.zeros_like(q))
        top = jnp.sum(mine.astype(f32) * k0, 1, keepdims=True)
        total = jnp.ones_like(top)
        acc = jnp.broadcast_to(v0, (rows, 128))
        for c in range(count):
            s = dot_nt(mine, k_ref[c * chunk : (c + 1) * chunk])
            new_top = jnp.maximum(top, jnp.max(s, 1, keepdims=True))
            fade = jnp.exp(top - new_top)
            p = jnp.exp(s - new_top)
            total = total * fade + jnp.sum(p, 1, keepdims=True)
            acc = acc * fade + dot_nn(p.astype(bf16), v_ref[c * chunk : (c + 1) * chunk])
            top = new_top
        outs.append(acc / total)
        lse_ref[0, head : head + 1, :] = (top + jnp.log(total)).T
    o_ref[...] = jnp.where(lane < HD, outs[0], outs[1]).astype(bf16)


def column_of(j, which):
    return (j // TRIO) * (3 * TRIO) + which * TRIO + j % TRIO


def attend_forward(qkv, kv0, block=1024, chunk=1024):
    rows = qkv.shape[0]
    return call(
        functools.partial(attend_kernel, chunk=chunk, count=rows // chunk),
        (PAIRS, rows // block),
        [
            pl.BlockSpec((block, 128), lambda j, i: (i, column_of(j, 0))),
            pl.BlockSpec((rows, 128), lambda j, i: (0, column_of(j, 1))),
            pl.BlockSpec((rows, 128), lambda j, i: (0, column_of(j, 2))),
            pl.BlockSpec((16, 128), lambda j, i: (0, column_of(j, 1))),
            pl.BlockSpec((16, 128), lambda j, i: (0, column_of(j, 2))),
        ],
        [
            pl.BlockSpec((block, 128), lambda j, i: (i, j)),
            pl.BlockSpec((1, 2, block), lambda j, i: (j, 0, i)),
        ],
        [shape_of((rows, HALF), bf16), shape_of((PAIRS, 2, rows), f32)],
        [],
        (16 * rows * rows * HALF, 5 * rows * D * 2),
        qkv,
        qkv,
        qkv,
        kv0,
        kv0,
    )


def attend_back_kernel(*refs, chunk, count, steps, waits):
    (
        q_ref, g_ref, o_ref, lse_ref, cos_ref, up_ref, down_ref,
        k_ref, v_ref, k0_ref, v0_ref, kcos_ref, kup_ref, kdown_ref,
    ) = refs[:14]
    (
        dq_ref, dk_ref, dv_ref, dk0_ref, dv0_ref, kt, dka, dva, dk0a, dv0a,
    ) = refs[14 + waits :]
    i = pl.program_id(1)

    @pl.when(i == 0)
    def _():
        kt[...] = k_ref[...].T
        dka[...] = jnp.zeros_like(dka)
        dva[...] = jnp.zeros_like(dva)
        dk0a[...] = jnp.zeros_like(dk0a)
        dv0a[...] = jnp.zeros_like(dv0a)

    q = q_ref[...]
    g = g_ref[...]
    rows = q.shape[0]
    lane = lax.broadcasted_iota(jnp.int32, q.shape, 1)
    row = lax.broadcasted_iota(jnp.int32, (16, rows), 0)
    go = (g.astype(f32) * o_ref[...].astype(f32)).T
    k0t = k0_ref[...].T
    dqs = []
    for head in range(2):
        sel = (lane // HD) == head
        low_row, high_row = head * HD, (head + 1) * HD
        qm = jnp.where(sel, q, jnp.zeros_like(q))
        gm = jnp.where(sel, g, jnp.zeros_like(g))
        lse = lse_ref[0, head : head + 1, :]
        delta = jnp.sum(go[low_row:high_row], 0, keepdims=True)
        s = dot_nt(k0_ref[...], qm)
        p = jnp.where(row == 0, jnp.exp(s - lse), 0.0)
        ds = (p * (dot_nt(v0_ref[...], gm) - delta)).astype(bf16)
        dk0a[...] += dot_nn(ds, qm)
        dv0a[...] += dot_nn(p.astype(bf16), gm)
        dq = dot_nn(k0t[low_row:high_row], ds)
        for c in range(count):
            part = pl.ds(c * chunk, chunk)
            p = jnp.exp(dot_nt(k_ref[part], qm) - lse)
            ds = (p * (dot_nt(v_ref[part], gm) - delta)).astype(bf16)
            dva[part] += dot_nn(p.astype(bf16), gm)
            dka[part] += dot_nn(ds, qm)
            dq = dq + dot_nn(kt[low_row:high_row, c * chunk : (c + 1) * chunk], ds)
        dqs.append(dq)
    dq = (jnp.concatenate(dqs, 0).T * HD ** (-0.5)).astype(bf16).astype(f32)
    dq_ref[...] = turn(dq, cos_ref[...], -up_ref[...], -down_ref[...]).astype(bf16)

    @pl.when(i == steps - 1)
    def _():
        dk = dka[...].astype(bf16).astype(f32)
        dk_ref[...] = turn(dk, kcos_ref[...], -kup_ref[...], -kdown_ref[...]).astype(bf16)
        dv_ref[...] = dva[...].astype(bf16)
        dk0_ref[...] = dk0a[...]
        dv0_ref[...] = dv0a[...]


def attend_backward(qkv, g, o, lse, kv0, tables, half, after, block=1024, chunk=512):
    rows = qkv.shape[0]
    first = half * TRIO
    out = pl.BlockSpec((block, 128), lambda j, i: (i, j))
    head = pl.BlockSpec((block, 128), lambda j, i: (i, first + j))
    table = pl.BlockSpec((block, 128), lambda j, i: (i, 0))
    whole_table = pl.BlockSpec((rows, 128), lambda j, i: (0, 0))
    whole = pl.BlockSpec((rows, 128), lambda j, i: (0, j))
    lead = pl.BlockSpec((16, 128), lambda j, i: (0, j))

    def part(size, which):
        return pl.BlockSpec((size, 128), lambda j, i: (0, column_of(first + j, which)))

    return call(
        functools.partial(
            attend_back_kernel,
            chunk=chunk, count=rows // chunk, steps=rows // block, waits=len(after),
        ),
        (TRIO, rows // block),
        [
            pl.BlockSpec((block, 128), lambda j, i: (i, column_of(first + j, 0))),
            head, head,
            pl.BlockSpec((1, 2, block), lambda j, i: (first + j, 0, i)),
            table, table, table,
            part(rows, 1), part(rows, 2), part(16, 1), part(16, 2),
            whole_table, whole_table, whole_table,
        ]
        + [pl.BlockSpec(memory_space=pl.ANY)] * len(after),
        [out, whole, whole, lead, lead],
        [shape_of((rows, THIRD), bf16)] * 3 + [shape_of((16, THIRD), f32)] * 2,
        [
            pltpu.VMEM((128, rows), bf16),
            pltpu.VMEM((rows, 128), f32),
            pltpu.VMEM((rows, 128), f32),
            pltpu.VMEM((16, 128), f32),
            pltpu.VMEM((16, 128), f32),
        ],
        (16 * rows * rows * HALF, 5 * rows * D * 2),
        qkv, g, o, lse, *tables, qkv, qkv, kv0, kv0, *tables, *after,
    )


def prompt_probs(k, qm, mask):
    s = dot_nt(k, qm) * HD ** (-0.5) + mask
    e = jnp.exp(s - jnp.max(s, 0, keepdims=True))
    return e / jnp.sum(e, 0, keepdims=True)


def cross_kernel(q_ref, k_ref, v_ref, mask_ref, o_ref):
    q = q_ref[...]
    lane = lax.broadcasted_iota(jnp.int32, q.shape, 1)
    vt = v_ref[...].T
    outs = []
    for head in range(2):
        qm = jnp.where((lane // HD) == head, q, jnp.zeros_like(q))
        p = prompt_probs(k_ref[...], qm, mask_ref[...])
        outs.append(dot_nn(vt[head * HD : (head + 1) * HD], p.astype(bf16)))
    o_ref[...] = jnp.concatenate(outs, 0).T.astype(bf16)


def cross_back_kernel(
    q_ref, g_ref, k_ref, v_ref, mask_ref, dq_ref, dk_ref, dv_ref, dka, dva, *, steps
):
    i = pl.program_id(1)

    @pl.when(i == 0)
    def _():
        dka[...] = jnp.zeros_like(dka)
        dva[...] = jnp.zeros_like(dva)

    q = q_ref[...]
    g = g_ref[...]
    lane = lax.broadcasted_iota(jnp.int32, q.shape, 1)
    kt = k_ref[...].T
    dqs = []
    for head in range(2):
        sel = (lane // HD) == head
        qm = jnp.where(sel, q, jnp.zeros_like(q))
        gm = jnp.where(sel, g, jnp.zeros_like(g))
        p = prompt_probs(k_ref[...], qm, mask_ref[...])
        dp = dot_nt(v_ref[...], gm)
        ds = (p * (dp - jnp.sum(dp * p, 0, keepdims=True)) * HD ** (-0.5)).astype(bf16)
        dva[...] += dot_nn(p.astype(bf16), gm)
        dka[...] += dot_nn(ds, qm)
        dqs.append(dot_nn(kt[head * HD : (head + 1) * HD], ds))
    dq_ref[...] = jnp.concatenate(dqs, 0).T.astype(bf16)

    @pl.when(i == steps - 1)
    def _():
        dk_ref[...] = dka[...]
        dv_ref[...] = dva[...]


def cross_specs(rows, tokens, block):
    q_spec = pl.BlockSpec((block, 128), lambda j, i: (i, j))
    key_spec = pl.BlockSpec((tokens, 128), lambda j, i: (0, j))
    value_spec = pl.BlockSpec((tokens, 128), lambda j, i: (0, PAIRS + j))
    mask_spec = pl.BlockSpec((tokens, 1), lambda j, i: (0, 0))
    return (q_spec, key_spec, value_spec, mask_spec)


def cross_forward(q, kv, mask, block=1024):
    rows, tokens = (q.shape[0], kv.shape[0])
    q_spec, key_spec, value_spec, mask_spec = cross_specs(rows, tokens, block)
    return call(
        cross_kernel,
        (PAIRS, rows // block),
        [q_spec, key_spec, value_spec, mask_spec],
        q_spec,
        shape_of((rows, HALF), bf16),
        [],
        (16 * rows * tokens * HALF, 4 * rows * D),
        q, kv, kv, mask,
    )


def cross_backward(q, g, kv, mask, block=1024):
    rows, tokens = (q.shape[0], kv.shape[0])
    q_spec, key_spec, value_spec, mask_spec = cross_specs(rows, tokens, block)
    return call(
        functools.partial(cross_back_kernel, steps=rows // block),
        (PAIRS, rows // block),
        [q_spec, q_spec, key_spec, value_spec, mask_spec],
        [q_spec, key_spec, key_spec],
        [
            shape_of((rows, HALF), bf16),
            shape_of((tokens, HALF), f32),
            shape_of((tokens, HALF), f32),
        ],
        [pltpu.VMEM((tokens, 128), f32), pltpu.VMEM((tokens, 128), f32)],
        (32 * rows * tokens * HALF, 8 * rows * D),
        q, g, kv, kv, mask,
    )


def gate_up_kernel(n_ref, wg_ref, wu_ref, hidden_ref, gate_ref, up_ref):
    n = n_ref[...]
    gate = dot_nn(n, wg_ref[...])
    up = dot_nn(n, wu_ref[...])
    hidden_ref[...] = (gate / (1.0 + jnp.exp(-gate)) * up).astype(bf16)
    gate_ref[...] = gate.astype(bf16)
    up_ref[...] = up.astype(bf16)


def gate_up(n, w, block=512, columns=512):
    rows = n.shape[0]
    count = HIDE // columns
    out = pl.BlockSpec((block, columns), lambda j, i: (i, j))
    return call(
        gate_up_kernel,
        (count, rows // block),
        [
            pl.BlockSpec((block, D), lambda j, i: (i, 0)),
            pl.BlockSpec((D, columns), lambda j, i: (0, j)),
            pl.BlockSpec((D, columns), lambda j, i: (0, count + j)),
        ],
        [out, out, out],
        [shape_of((rows, HIDE), bf16)] * 3,
        [],
        (4 * rows * D * HIDE, 8 * rows * HIDE + 4 * D * HIDE),
        n, w, w,
    )


def down_back_kernel(d_ref, w_ref, gate_ref, up_ref, after_ref, dgate_ref, dup_ref):
    for part in range(0, w_ref.shape[0], 256):
        cols = slice(part, part + 256)
        d = dot_nt(d_ref[...], w_ref[cols])
        gate = gate_ref[:, cols].astype(f32)
        sig = 1.0 / (1.0 + jnp.exp(-gate))
        d_sig = d * sig
        dgate_ref[:, cols] = (d_sig * up_ref[:, cols] * (1.0 + gate * (1.0 - sig))).astype(bf16)
        dup_ref[:, cols] = (d_sig * gate).astype(bf16)


def down_back(d, w, gate, up, after, block=512, columns=1024):
    rows = d.shape[0]
    out = pl.BlockSpec((block, columns), lambda j, i: (i, j))
    return call(
        down_back_kernel,
        (HIDE // columns, rows // block),
        [
            pl.BlockSpec((block, D), lambda j, i: (i, 0)),
            pl.BlockSpec((columns, D), lambda j, i: (j, 0)),
            out,
            out,
            pl.BlockSpec(memory_space=pl.ANY),
        ],
        [out, out],
        [shape_of((rows, HIDE), bf16)] * 2,
        [],
        (2 * rows * D * HIDE, 10 * rows * HIDE + 2 * D * HIDE),
        d, w, gate, up, after,
    )


def chip_sum_kernel(*refs, inputs, jobs, planes):
    ins, outs = (refs[:inputs], refs[inputs : 2 * inputs])
    scratch = list(refs[2 * inputs : -3])
    send_sem, recv_sem, local_sem = refs[-3:]
    s_at, z_at = (lax.axis_index("seq"), lax.axis_index("z"))
    y_at, x_at = (s_at // 2, s_at % 2)
    y_mate = (1 - y_at) * 2 + x_at
    x_mate = y_at * 2 + (1 - x_at)
    z_mates = [(z_at + offset) % planes for offset in range(1, planes)]
    z_froms = [(z_at + planes - offset) % planes for offset in range(1, planes)]
    barrier = pltpu.get_barrier_semaphore()
    for mate in (y_mate, x_mate):
        pl.semaphore_signal(
            barrier, inc=1, device_id={"seq": mate}, device_id_type=pl.DeviceIdType.MESH
        )
    for mate in z_mates:
        pl.semaphore_signal(
            barrier, inc=1, device_id={"z": mate}, device_id_type=pl.DeviceIdType.MESH
        )
    pl.semaphore_wait(barrier, 1 + planes)

    def remote(job, which, source, target, device):
        copy = pltpu.make_async_remote_copy(
            src_ref=source,
            dst_ref=target,
            send_sem=send_sem.at[job, which],
            recv_sem=recv_sem.at[job, which],
            device_id=device,
            device_id_type=pl.DeviceIdType.MESH,
        )
        copy.start()
        return copy

    def along_z(job, source, received):
        return [
            remote(job, 2 + n, source.at[mate], received.at[n], {"z": mate})
            for n, mate in enumerate(z_mates)
        ]

    state = []
    copies = []
    for n, (full, at, low_col, width, y_first) in enumerate(jobs):
        cols = pl.ds(low_col, width)
        if full:
            own, first, second, third = (scratch.pop(0) for _ in range(4))
            view = ins[at].at[:, :, :, :, cols]
            given = view.at[1 - y_at] if y_first else view.at[:, 1 - x_at]
            kept = view.at[y_at] if y_first else view.at[:, x_at]
            mate = {"seq": y_mate if y_first else x_mate}
            moving = [remote(n, 0, given, first, mate)]
        else:
            own, third = (scratch.pop(0) for _ in range(2))
            first, second = (None, None)
            view = ins[at].at[:, :, cols]
            kept = view.at[z_at]
            moving = along_z(n, view, third)
        local = pltpu.make_async_copy(kept, own, local_sem.at[n])
        local.start()
        copies += moving
        state.append((own, first, second, third, local, moving))

    waiting = []
    for n, (full, at, low_col, width, y_first) in enumerate(jobs):
        own, first, second, third, local, moving = state[n]
        local.wait()
        if not full:
            waiting.append(moving)
            continue
        moving[0].wait_recv()

        def add_first(i, carry):
            half, plane = (i // planes, i % planes)
            own[half, plane] = (
                own[half, plane].astype(f32) + first[half, plane].astype(f32)
            ).astype(bf16)
            return carry

        lax.fori_loop(0, 2 * planes, add_first, 0)
        here = x_at if y_first else y_at
        mate = {"seq": x_mate if y_first else y_mate}
        copy = remote(n, 1, own.at[1 - here], second, mate)
        copies.append(copy)
        waiting.append([copy])
    for n, (full, at, low_col, width, y_first) in enumerate(jobs):
        if not full:
            continue
        own, first, second, third, local, moving = state[n]
        here = x_at if y_first else y_at
        waiting[n][0].wait_recv()

        def add_second(plane, carry):
            second[plane] = (
                own[here, plane].astype(f32) + second[plane].astype(f32)
            ).astype(bf16)
            return carry

        lax.fori_loop(0, planes, add_second, 0)
        waiting[n] = along_z(n, second, third)
        copies += waiting[n]
    for n, (full, at, low_col, width, y_first) in enumerate(jobs):
        own, first, second, third, local, moving = state[n]
        for copy in waiting[n]:
            copy.wait_recv()
        total = (second[z_at] if full else own[...]).astype(f32)
        for m in range(planes - 1):
            total = total + third[m].astype(f32)
        outs[at][:, low_col : low_col + width] = total
    for copy in copies:
        copy.wait_send()


def chip_sums(arrays, jobs, planes):
    scratch = []
    for full, at, _, width, _ in jobs:
        rows = arrays[at].shape[-2]
        if full:
            scratch += [pltpu.VMEM((2, planes, rows, width), bf16)] * 2
            scratch += [pltpu.VMEM((planes, rows, width), bf16)]
        else:
            scratch += [pltpu.VMEM((rows, width), bf16)]
        scratch += [pltpu.VMEM((planes - 1, rows, width), bf16)]
    count = len(jobs)
    scratch += [
        pltpu.SemaphoreType.DMA((count, 1 + planes)),
        pltpu.SemaphoreType.DMA((count, 1 + planes)),
        pltpu.SemaphoreType.DMA((count,)),
    ]
    return pl.pallas_call(
        functools.partial(chip_sum_kernel, inputs=len(arrays), jobs=jobs, planes=planes),
        in_specs=[pl.BlockSpec(memory_space=pl.ANY)] * len(arrays),
        out_specs=[pl.BlockSpec(memory_space=pltpu.VMEM)] * len(arrays),
        out_shape=[shape_of(x.shape[-2:], f32) for x in arrays],
        scratch_shapes=scratch,
        cost_estimate=pl.CostEstimate(flops=10**11, bytes_accessed=10**7, transcendentals=0),
        compiler_params=pltpu.CompilerParams(
            vmem_limit_bytes=56 << 20, collective_id=0, has_side_effects=True
        ),
    )(*arrays)


def chip_body(
    latents, noise_draw, audio_len, bucket, timing, prompt, prompt_len, step_count,
    edge_weight, edge_first, edge_second,
    attend_weight, attend_first, attend_second,
    square_weight, square_first, square_second,
    cross_weight, cross_first, cross_second,
    upward_weight, upward_first, upward_second,
    down_weight, down_first, down_second,
    gain_weight, gain_first, gain_second,
    *, planes, chips,
):
    peers = ("seq", "z")
    many = planes * chips
    groups = latents.shape[0]
    clips = groups * 2 * planes
    frames = latents.shape[1] * chips
    own = frames // 2
    s_at, z_at, k_at = (lax.axis_index("seq"), lax.axis_index("z"), lax.axis_index("core"))
    device = (s_at * planes + z_at) * 2 + k_at
    first_core = k_at == 0

    def swap(x):
        return lax.ppermute(x, "core", [(0, 1), (1, 0)])

    def across(x, axis, size, bit):
        return lax.ppermute(x, axis, [(i, i ^ bit) for i in range(size)])

    def bits(size):
        found = []
        bit = size // 2
        while bit:
            found.append(bit)
            bit //= 2
        return found

    hops = [("z", planes, b) for b in bits(planes)] + [("seq", chips, b) for b in bits(chips)]

    def in_order(mine, other, axis=0):
        return jnp.where(
            first_core,
            jnp.concatenate([mine, other], axis),
            jnp.concatenate([other, mine], axis),
        )

    def pick(x, index, axis):
        return lax.dynamic_index_in_dim(x, index, axis, keepdims=False)

    def halves_of(x, view, axis):
        x = x.reshape(view)
        rows = view[0]
        return (
            pick(x, k_at, axis).reshape(rows, -1),
            pick(x, 1 - k_at, axis).reshape(rows, -1),
        )

    def tie(x):
        return x.reshape(-1, x.shape[-1])[0, 0].astype(f32) * 0.0

    y_at, x_at = (s_at // 2, s_at % 2)

    rows = attend_weight.shape[0]
    attend_view = (rows, 2, 3, 2, THIRD)
    square_view = (rows, 3, 2, HALF)
    cross_view = (cross_weight.shape[0], 2, 2, HALF)
    up_view = (rows, 2, many, 2, FF // (2 * many))
    attend16 = attend_weight.astype(bf16).reshape(rows, 3, 2, 2, THIRD).transpose(0, 3, 1, 2, 4)
    edge16 = jnp.concatenate(
        [edge_weight[: 2 * C].astype(bf16), gain_weight.astype(bf16)], 0
    ).T
    edge16 = jnp.pad(edge16, ((0, 0), (0, 256 - edge16.shape[1])))
    mine, other = halves_of(attend16, attend_view, 3)
    mine, other = (jnp.concatenate([mine, edge16], 1), jnp.concatenate([other, edge16], 1))
    first_mine = in_order(mine, swap(other))
    mine, other = halves_of(
        square_weight[:3].astype(bf16).transpose(1, 0, 2), square_view, 2
    )
    square_mine = in_order(mine, swap(other))
    mine, other = halves_of(cross_weight.astype(bf16), cross_view, 2)
    cross_mine = in_order(mine, swap(other))
    cross_mine = jnp.concatenate([cross_mine[:, :HALF], cross_mine[:, HALF:]], 0)
    first_group = lax.all_gather(
        jnp.concatenate([first_mine, square_mine, cross_mine], 1), peers, axis=0, tiled=True
    )
    square_cols = first_group[:, first_mine.shape[1] :]
    mine, other = halves_of(upward_weight.astype(bf16), up_view, 3)
    up_w = lax.all_gather(in_order(mine, swap(other)), peers, axis=0, tiled=True)
    down_w = lax.all_gather(down_weight.astype(bf16), peers, axis=0, tiled=True)

    attend_w = first_group[:, : 3 * HALF]
    w_in_t = first_group[:, 3 * HALF : 3 * HALF + C]
    w_out_t = first_group[:, 3 * HALF + C : 3 * HALF + 2 * C]
    norm_gains = first_group[:, 3 * HALF + 2 * C : 3 * HALF + 2 * C + 4].astype(f32).T

    def rows_half(columns):
        mine_rows = lax.dynamic_slice_in_dim(columns, k_at * HALF, HALF, 0)
        other_rows = lax.dynamic_slice_in_dim(columns, (1 - k_at) * HALF, HALF, 0)
        return in_order(mine_rows, swap(other_rows), 1)

    local = jnp.stack(
        [audio_len, bucket, timing[:, 0], timing[:, 1], prompt_len], 1
    ).astype(f32)
    clip_index = jnp.arange(clips)
    place = (clip_index // groups) == (z_at * 2 + k_at)
    scalars = jnp.where(place[:, None], jnp.tile(local, (clips // groups, 1)), 0.0)
    scalars = scalars + swap(scalars)
    for b in bits(planes):
        scalars = scalars + across(scalars, "z", planes, b)
    order = (z_at ^ (clip_index // chips)) * chips + (s_at ^ (clip_index % chips))
    chosen = order[:, None] == clip_index[None, :]
    scalars = jnp.sum(jnp.where(chosen[:, :, None], scalars[None], 0.0), 1)
    lengths = scalars[:, 0]
    t, keep_rates, noise_rates, clip_weights = plan(scalars[:, 1])
    weight_sum = jnp.sum(clip_weights * lengths)
    keep_rate, noise_rate, clip_weight = (keep_rates[0], noise_rates[0], clip_weights[0])

    t_feat = time_features(t).astype(bf16)
    z_feat = timing_features(scalars[:, 2:4]).astype(bf16)
    w_t1 = edge_weight[2 * C : 2 * C + TF].astype(bf16)
    w_t2 = square_weight[3].astype(bf16)
    w_timing = edge_weight[2 * C + TF :].astype(bf16)
    t_pre = dot_nn(t_feat, w_t1)
    t_hidden = jax.nn.silu(t_pre).astype(bf16)
    lead = lax.dynamic_update_slice(
        jnp.zeros((clips, D), f32), dot_nn(z_feat, w_timing), (0, device * rows)
    ) + dot_nn(t_hidden, w_t2)
    for axis, size, bit in hops:
        count = lead.shape[0] // 2
        lead = lead[:count] + across(lead[count:], axis, size, bit)
    lead = lead + swap(lead)
    prefix_normed, prefix_std, prefix_dev = layer_normalize(lead, norm_gains[0])
    n_prefix = jnp.pad(prefix_normed.astype(bf16), ((0, 15), (0, 0)))
    kv_prefix = dot_nn(n_prefix, attend_w).astype(bf16)

    part = s_at // groups
    member = s_at % groups
    both = jnp.stack([latents, noise_draw])
    blocks = [pick(both, member, 1)]
    for offset in range(1, chips):
        given = pick(both, (s_at ^ offset) % groups, 1)
        blocks.append(across(given, "seq", chips, offset))
    blocks = jnp.stack(blocks, 1)
    blocks = jnp.where(part == k_at, blocks, swap(blocks))
    seen = s_at ^ jnp.arange(chips)

    def mine_first(x, axis):
        low_half, high_half = jnp.split(x, 2, axis)
        return in_order(low_half, high_half, axis)

    clip = mine_first(blocks, 1).reshape(2, frames, C).astype(f32)
    clean, noisy_part = (clip[0], clip[1])
    positions = (
        mine_first(seen, 0)[:, None] * latents.shape[1] + jnp.arange(latents.shape[1])
    ).reshape(frames)
    row_weight = clip_weight * (positions[:own].astype(f32) < lengths[0]).astype(f32)
    local_prompt = pick(prompt, member, 0)
    other_prompt = swap(local_prompt)
    prompt_low = jnp.where(part == k_at, local_prompt, other_prompt)
    tokens = prompt_low.shape[0]
    mask = jnp.where(
        jnp.arange(tokens)[:, None].astype(f32) < scalars[0, 4], 0.0, -1000000000.0
    ).astype(f32)

    def shared_sum(product):
        given = product(1).astype(bf16)
        return product(0) + swap(given).astype(f32)

    def cut(x, which):
        return x[which * own : (which + 1) * own]

    def both_halves(x):
        return jnp.concatenate([x, swap(x)], 0)

    x_in = (keep_rate * clean + noise_rate * noisy_part).astype(bf16)
    x_wide = jnp.pad(x_in, ((0, 0), (0, C)))
    h0, n1 = start_forward(x_wide, first_group, norm_gains[:1])
    tables = turn_tables(positions + 1)
    qkv = qkv_project(n1, first_group, tables)
    o, lse = attend_forward(qkv, kv_prefix)

    cross_w = square_cols[:, 3 * HALF :].reshape(many, 2, CROSS // many, HALF)
    cross_w = jnp.concatenate(
        [cross_w[:, 0].reshape(CROSS, HALF), cross_w[:, 1].reshape(CROSS, HALF)], 1
    )
    w_o = rows_half(square_cols[:, :HALF])
    w_cq = square_cols[:, HALF : 2 * HALF]
    w_co = rows_half(square_cols[:, 2 * HALF : 3 * HALF])

    h1 = h0 + shared_sum(lambda i: dot_nn(cut(o, i), w_o))
    n2 = both_halves(layer_normalize(h1, norm_gains[1])[0].astype(bf16))
    cross_q = dot_nn(n2, w_cq).astype(bf16)
    cross_kv = dot_nn(prompt_low, cross_w).astype(bf16)
    co = cross_forward(cross_q, cross_kv, mask)
    h2 = h1 + shared_sum(lambda i: dot_nn(cut(co, i), w_co))
    n3 = both_halves(layer_normalize(h2, norm_gains[2])[0].astype(bf16))
    hidden, gate, upper = gate_up(n3, up_w)
    h3 = h2 + shared_sum(lambda i: dot_nn(cut(hidden, i), down_w))
    n4, std4, dev4 = layer_normalize(h3, norm_gains[3])
    n4 = n4.astype(bf16)
    predicted = dot_nn(n4, w_out_t)
    target = keep_rate * noisy_part[:own] - noise_rate * clean[:own]
    error = predicted - target
    loss_local = jnp.sum(row_weight[:, None] * error * error)

    d_pred = (2.0 / (C * weight_sum) * row_weight[:, None] * error).astype(bf16)
    g_out_t = dot_tn(n4, d_pred)
    d_h, gain4 = norm_backward(dot_nt(d_pred, w_out_t), std4, dev4, norm_gains[3])
    d_f = both_halves(d_h.astype(bf16))

    def half_at(x, at, size):
        return lax.dynamic_slice_in_dim(x, at * size, size, 0)

    class Scatter:
        def __init__(self, product, depth, y_first):
            self.product, self.quarter, self.y_first = (product, depth // chips, y_first)
            self.bit, self.later, self.at = (2, 1, x_at) if y_first else (1, 2, y_at)
            given = product(lambda x, axis: self.rows_at(x, axis, True)).astype(bf16)
            self.sent = [given]
            self.taken = across(given, "seq", chips, self.bit)

        def rows_at(self, x, axis, flip):
            quarter = self.quarter

            def block(at):
                return lax.dynamic_slice_in_dim(x, at * quarter, quarter, axis)

            if self.y_first:
                row = (1 - y_at if flip else y_at) * 2
                return lax.dynamic_slice_in_dim(x, row * quarter, 2 * quarter, axis)
            column = 1 - x_at if flip else x_at
            return jnp.concatenate([block(column), block(2 + column)], axis)

        def second(self, behind=0.0):
            own_part = self.product(lambda x, axis: self.rows_at(x, axis, False))
            kept = (own_part + self.taken.astype(f32) + behind).astype(bf16)
            given = half_at(kept, 1 - self.at, self.quarter)
            self.kept = half_at(kept, self.at, self.quarter)
            self.sent = [given]
            self.taken = across(given, "seq", chips, self.later)
            return self

        def folded(self, behind):
            kept = (self.kept.astype(f32) + self.taken.astype(f32) + behind).astype(bf16)
            return kept.reshape(planes, -1, kept.shape[1])

    def gradient(left, right, y_first):
        return Scatter(lambda cut_of: dot_tn(cut_of(left, 1), right), left.shape[1], y_first)

    def gathered_sum(g):
        return lax.psum_scatter(g, peers, scatter_dimension=0, tiled=True)

    down_parts = [dot_tn(hidden, part).astype(bf16) for part in jnp.split(d_f, 2, 1)]
    s_down = jnp.concatenate([gathered_sum(part) for part in down_parts], 1)
    d_gate, d_up = down_back(d_f, down_w, gate, upper, down_parts[0])
    s_gate = gathered_sum(dot_tn(n3, d_gate).astype(bf16))
    s_upper = gathered_sum(dot_tn(n3, d_up).astype(bf16))
    d_n3 = shared_sum(
        lambda i: dot_nt(cut(d_gate, i), up_w[:, :HIDE]) + dot_nt(cut(d_up, i), up_w[:, HIDE:])
    )

    def norm_again(d_n, h, gain):
        _, std, dev = layer_normalize(h, gain)
        return norm_backward(d_n, std, dev, gain)

    d_part, gain3 = norm_again(d_n3, h2, norm_gains[2])
    d_h = d_h + d_part
    d_c = both_halves(d_h.astype(bf16))
    g_co = dot_tn(co, d_c).astype(bf16)
    d_co = dot_nt(d_c, w_co).astype(bf16)
    d_cq, d_ck, d_cv = cross_backward(cross_q, d_co, cross_kv, mask)
    r_cross = gradient(prompt_low, jnp.concatenate([d_ck, d_cv], 1).astype(bf16), False)
    r_cq = gradient(n2, d_cq, False)
    d_n2 = shared_sum(lambda i: dot_nt(cut(d_cq, i), w_cq))
    d_part, gain2 = norm_again(d_n2, h1, norm_gains[1])
    d_h = d_h + d_part
    d_a = both_halves(d_h.astype(bf16))
    g_o = dot_tn(o, d_a).astype(bf16)

    def columns_half(g):
        kept = lax.dynamic_slice_in_dim(g, k_at * HALF, HALF, 1)
        given = lax.dynamic_slice_in_dim(g, (1 - k_at) * HALF, HALF, 1)
        return in_order(kept, swap(given), 0)

    side = jnp.concatenate([columns_half(g_o), columns_half(g_co)], 1)
    r_side = Scatter(lambda cut_of: cut_of(side, 0).astype(f32), D, True)
    d_o = dot_nt(d_a, w_o).astype(bf16)
    lead_column = n_prefix[:1].astype(f32)

    def attend_half(half, after):
        d_q, d_k, d_v, d_k0, d_v0 = attend_backward(qkv, d_o, o, lse, kv_prefix, tables, half, after)
        lead_row = jnp.concatenate([jnp.zeros_like(d_k0), d_k0, d_v0], 1)
        return (jnp.concatenate([d_q, d_k, d_v], 1), lead_row, tie(d_q))

    def attend_gradient(right, lead_row):
        return (dot_tn(n1, right) + lead_column.T * lead_row[:1]).astype(bf16)

    after = [x for r in (r_cross, r_cq, r_side) for x in r.sent]
    d_first, lead_first, behind_first = attend_half(0, after)
    g_first = attend_gradient(d_first, lead_first)
    for r in (r_cross, r_cq, r_side):
        r.second(behind_first)
    after = [x for r in (r_cross, r_cq, r_side) for x in r.sent] + [g_first]
    d_second, lead_second, behind_second = attend_half(1, after)
    g_second = attend_gradient(d_second, lead_second)
    d_n1 = shared_sum(
        lambda i: dot_nt(cut(d_first, i), attend_w[:, : 3 * THIRD])
        + dot_nt(cut(d_second, i), attend_w[:, 3 * THIRD :])
    )
    d_part, gain1 = norm_again(d_n1, h0, norm_gains[0])
    d_h = d_h + d_part
    g_in_t = dot_tn(d_h.astype(bf16), x_in[:own])
    short = [r.folded(behind_second) for r in (r_cross, r_cq, r_side)]
    d_kv0 = jnp.concatenate([lead_first, lead_second], 1)

    high = d_kv0.astype(bf16)
    rest = (d_kv0 - high.astype(f32)).astype(bf16)
    d_np = dot_nt(jnp.concatenate([high, rest], 0), attend_w)
    d_np = d_np[:1] + d_np[16:17]
    d_np = d_np + swap(d_np)
    d_lead, prefix_gain = norm_backward(d_np, prefix_std, prefix_dev, norm_gains[0])

    def to_owner(x, view, axis):
        count = x.shape[0] // 2
        kept = lax.dynamic_slice_in_dim(x, k_at * count, count, 0)
        given = lax.dynamic_slice_in_dim(x, (1 - k_at) * count, count, 0)
        taken = swap(given.astype(bf16)).astype(f32)
        shape = view[:axis] + view[axis + 1 :]
        joined = jnp.where(
            first_core,
            jnp.stack([kept.reshape(shape), taken.reshape(shape)], axis),
            jnp.stack([taken.reshape(shape), kept.reshape(shape)], axis),
        )
        return joined

    gains = jnp.stack([gain1 + 0.5 * prefix_gain, gain2, gain3, gain4], 1)
    edges = jnp.concatenate([g_in_t, g_out_t], 1)
    gains = jnp.pad(gains, ((0, 0), (0, 128 - gains.shape[1])))
    edges = jnp.where(first_core, edges, gains) + swap(jnp.where(first_core, gains, edges))

    def blocks_of(g):
        return g.astype(bf16).reshape(2, 2, planes, -1, g.shape[1])

    wide, narrow = (5 * 128, 4 * 128)
    jobs = (
        (True, 0, 0, wide, True),
        (True, 0, wide, narrow, False),
        (True, 1, 0, wide, False),
        (True, 1, wide, narrow, True),
        (True, 2, 0, 128, True),
        (False, 3, 0, 2 * HALF, True),
        (False, 4, 0, HALF, True),
        (False, 5, 0, 2 * HALF, True),
    )
    s_first, s_second, s_edge, s_cross, s_cq, s_side = chip_sums(
        [blocks_of(g_first), blocks_of(g_second), blocks_of(edges)] + short, jobs, planes
    )
    s_square = jnp.concatenate([s_side[:, :HALF], s_cq, s_side[:, HALF:]], 1)
    s_attend = jnp.concatenate([s_first, s_second], 1)
    s_edge_part = s_edge
    s_edge = to_owner(s_edge, (rows, 2, 128), 1).reshape(rows, 256)

    d_lead = d_lead + tie(s_first)
    for axis, size in (("seq", chips), ("z", planes)):
        taken = [across(d_lead, axis, size, offset) for offset in range(1, size)]
        d_lead = jnp.concatenate([d_lead] + taken, 0)
    g_t2 = exact("ge,gd->ed", t_hidden.astype(f32), d_lead)
    d_lead_here = lax.dynamic_slice(d_lead, (0, device * rows), (clips, rows))
    g_timing = exact("gz,gd->zd", z_feat.astype(f32), d_lead_here)
    d_t_hidden = exact("gd,ed->ge", d_lead, w_t2.astype(f32))
    t_sig = jax.nn.sigmoid(t_pre)
    d_t_pre = d_t_hidden * t_sig * (1.0 + t_pre * (1.0 - t_sig))
    g_t1 = exact("gz,gd->zd", t_feat.astype(f32), d_t_pre)
    g_attend = to_owner(s_attend, attend_view, 3).transpose(0, 2, 3, 1, 4).reshape(rows, 3 * D)
    g_square = to_owner(s_square, square_view, 2).reshape(rows, 3, D).transpose(1, 0, 2)
    g_square = jnp.concatenate([g_square, g_t2[None]], 0)
    g_cross = to_owner(s_cross, cross_view, 2).reshape(cross_view[0], 2 * D)
    s_upper = s_upper.astype(f32) + tie(s_first)
    s_gate = s_gate.astype(f32)
    half_view = (rows, many, 2, FF // (2 * many))
    g_up = jnp.concatenate(
        [to_owner(x, half_view, 2).reshape(rows, FF) for x in (s_gate, s_upper)], 1
    )
    g_down = s_down.astype(f32)
    g_edge = jnp.concatenate([s_edge[:, : 2 * C].T, g_t1, g_timing], 0)
    g_gain = s_edge[:, 2 * C : 2 * C + 4].T
    sharded = lax.optimization_barrier(
        (g_edge, g_attend, g_square, g_cross, g_up, g_down, g_gain)
    )
    g_gain = sharded[6]
    parts = (s_first, s_second, s_edge_part, s_cross, s_cq, s_side, s_gate, s_upper, g_down)
    parts = parts + (g_t1, g_t2, g_timing)
    totals = jnp.stack([sum(jnp.sum(g * g) for g in parts), loss_local])
    totals = totals + swap(totals)
    for axis, size, bit in hops:
        totals = totals + across(totals, axis, size, bit)
    grad_norm = jnp.sqrt(totals[0])
    loss_value = totals[1] / (C * weight_sum)
    factor = jnp.minimum(1.0, clip_norm / grad_norm)
    count = step_count[0].astype(f32)
    first_fix = 1.0 - 0.9**count
    second_fix = 1.0 - 0.999**count
    states = (
        (edge_weight, edge_first, edge_second),
        (attend_weight, attend_first, attend_second),
        (square_weight, square_first, square_second),
        (cross_weight, cross_first, cross_second),
        (upward_weight, upward_first, upward_second),
        (down_weight, down_first, down_second),
        (gain_weight, gain_first, gain_second),
    )
    out = [
        adam(w, m, v, g * factor, first_fix, second_fix)
        for (w, m, v), g in zip(states, sharded)
    ]
    flat = [x for triple in out[:6] for x in triple]
    return (loss_value, grad_norm, *flat, g_gain * factor, out[6][1], out[6][2])


def solution(mesh):
    chips, spread = (mesh.shape["seq"], mesh.shape["dp"])
    split_mesh = Mesh(mesh.devices.reshape(chips, spread // 2, 2), ("seq", "z", "core"))

    def whole(*args):
        groups = args[0].shape[0] // spread
        one_clip_per_chip = groups * 2 == chips == 4 and spread & (spread - 1) == 0
        if one_clip_per_chip:
            inner = functools.partial(chip_body, planes=spread // 2, chips=chips)
            dp, used = ("z", "core"), split_mesh
        else:
            inner, dp, used = (general_body, "dp", mesh)
        every = ("seq",) + (dp if isinstance(dp, tuple) else (dp,))
        by_row, by_column, by_middle = (P(every, None), P(None, every), P(None, every, None))
        frames = P(dp, "seq", None)
        clip = P(dp)
        kinds = (by_column, by_row, by_middle, by_row, by_row, by_row, by_column)
        weights = tuple(kind for kind in kinds for _ in range(3))
        return jax.shard_map(
            inner,
            mesh=used,
            in_specs=(frames, frames, clip, clip, P(dp, None), P(dp, None, None), clip, P())
            + weights,
            out_specs=(P(), P()) + weights,
            check_vma=False,
        )(*args)

    return whole
```
